32 devices in a mesh: gx: 8 (over z, x), gy: 4 (over y, core).
Axes of the slice: x: 2, y: 2, z: 4, core: 2. Of those that a mesh axis runs over, the one named last changes fastest.
Arguments:
- misfit: float32 [2, 16, 256, 1024], P(None, None, 'gx', 'gy'), may hold values from -6 to 6
- viscosity: float32 [16, 256, 1024], P(None, 'gx', 'gy'), may hold values from 0.1 to 10
- friction: float32 [256, 1024], P('gx', 'gy'), may hold values from 0.5 to 50
- ice_mask: int32 [256, 1024], P('gx', 'gy'), may hold values 0 or 1
- grounded: int32 [256, 1024], P('gx', 'gy'), may hold values 0 or 1
Outputs:
- adjoint_velocity: float32 [2, 16, 256, 1024], P(None, None, 'gx', 'gy')
The draws below stay inside these ranges and needn't reach their ends.
All inputs are finite; a program needn't handle non-finite values. No bound on the sum of `ice_mask` or of `grounded` on one device may be relied on, other than what follows from the above.
Results may differ from the reference program's by a relative error of at most 0.00002.
Values sent between devices are 32-bit elements; how exact they have to be, the bound alone decides.
No kernel may reach another device: no remote copies, remote signals or barrier semaphores. Data moves between devices by JAX's collectives and lax.ppermute only.
A program may use at most 128 MiB of HBM per device.

```python
import math
import jax
import jax.numpy as jnp
from jax import lax

NZ = 16
LEVELS = 4
SWEEPS = 2
COARSE_ITERS = 20
NX = 256
NY = 1024


def touch_ends(values, key, smallest, high):
    spot = [jax.random.randint(jax.random.fold_in(key, axis), (), 0, length) for axis, length in enumerate(values.shape)]
    widest = values.shape.index(max(values.shape))
    neighbour = spot[:widest] + [(spot[widest] + 1) % values.shape[widest]] + spot[widest + 1:]
    return values.at[tuple(spot)].set(smallest).at[tuple(neighbour)].set(high)


def shard_levels(key, shape, shards, smallest, top_value):
    def one(position, parts):
        steps = jax.random.uniform(jax.random.fold_in(jax.random.fold_in(key, 6), position), (parts,), jnp.float32, smallest / len(shards), top_value / len(shards))
        return jnp.repeat(jnp.exp(steps), shape[position] // parts).reshape((-1,) + (1,) * (len(shape) - position - 1))

    gain = one(*shards[0])
    for cut in shards[1:]:
        gain = gain * one(*cut)
    return gain


def bell_draw(key, shape, spread, most, cuts=(), dtype=jnp.bfloat16):
    entries = jax.random.normal(key, shape, jnp.float32) * spread
    if len(cuts) > 0:
        entries = shard_levels(key, shape, cuts, -0.22, 0.18) * entries
    return jnp.clip(entries, min=-most, max=most).astype(dtype)


def setup_inputs(seed: int = 0) -> dict:
    key_of = jax.random.split(jax.random.key(seed), 6)
    return {
        "misfit": bell_draw(key_of[0], (2, NZ, NX, NY), 1.0, 6.0, ((2, 8), (3, 4)), jnp.float32),
        "viscosity": jnp.clip(jnp.exp(math.log(10.0) - 4.6051702 * jax.random.uniform(key_of[1], (NZ, NX, NY), jnp.float32) ** shard_levels(key_of[1], (NZ, NX, NY), ((1, 8), (2, 4)), -0.2, 0.2)), 0.1, 10.0),
        "friction": jnp.clip(jnp.exp(math.log(50.0) - 4.6051702 * jax.random.uniform(key_of[2], (NX, NY), jnp.float32) ** shard_levels(key_of[2], (NX, NY), ((0, 8), (1, 4)), -0.2, 0.2)), 0.5, 50.0),
        "ice_mask": touch_ends((jax.random.randint(key_of[3], (NX, NY), 0, 10) < 9).astype(jnp.int32), jax.random.fold_in(key_of[3], 1), 0, 1),
        "grounded": touch_ends((jax.random.randint(key_of[4], (NX, NY), 0, 4) < 3).astype(jnp.int32), jax.random.fold_in(key_of[4], 1), 0, 1),
    }


OMEGA = 0.6
ZWEIGHT = 4.0
CROSS = 0.75


def apply_operator(padded, coef_pad, horizontal):
    layers = padded.shape[1]
    viscous = coef_pad[:layers]
    ice_share = coef_pad[layers, 1:-1, 1:-1]
    drag_term = coef_pad[layers + 1, 1:-1, 1:-1]
    centre = viscous[:, 1:-1, 1:-1]
    east_face = 0.5 * (centre + viscous[:, 2:, 1:-1])
    west_face = 0.5 * (centre + viscous[:, :-2, 1:-1])
    north_face = 0.5 * (centre + viscous[:, 1:-1, 2:])
    south_face = 0.5 * (centre + viscous[:, 1:-1, :-2])
    vertical = ZWEIGHT * 0.5 * (centre[1:] + centre[:-1])
    layer_index = lax.broadcasted_iota(jnp.int32, centre.shape, 0)
    bottom = jnp.where(layer_index == 0, drag_term, jnp.zeros_like(centre))
    vert_diag = jnp.pad(vertical, ((1, 0), (0, 0), (0, 0))) + jnp.pad(vertical, ((0, 1), (0, 0), (0, 0)))
    images = []
    diagonals = []
    for component, (x_weight, y_weight) in enumerate(((4.0, 1.0), (1.0, 4.0))):
        field = padded[component]
        middle = field[:, 1:-1, 1:-1]
        lateral = x_weight * (east_face * (middle - field[:, 2:, 1:-1]) + west_face * (middle - field[:, :-2, 1:-1]))
        lateral = lateral + y_weight * (north_face * (middle - field[:, 1:-1, 2:]) + south_face * (middle - field[:, 1:-1, :-2]))
        fluxes = vertical * (middle[1:] - middle[:-1])
        column = jnp.pad(fluxes, ((1, 0), (0, 0), (0, 0))) - jnp.pad(fluxes, ((0, 1), (0, 0), (0, 0)))
        other = padded[1 - component]
        mixed = other[:, 2:, 2:] - other[:, 2:, :-2] - other[:, :-2, 2:] + other[:, :-2, :-2]
        flow = horizontal * (lateral - CROSS * centre * mixed) + column + bottom * middle
        images.append(ice_share * flow + (1.0 - ice_share) * middle)
        lateral_diag = x_weight * (east_face + west_face) + y_weight * (north_face + south_face)
        diagonals.append(ice_share * (horizontal * lateral_diag + vert_diag + bottom) + (1.0 - ice_share))
    return jnp.stack(images), jnp.stack(diagonals)


def jacobi_update(inside, target, padded, coef_pad, horizontal):
    image, diagonal = apply_operator(padded, coef_pad, horizontal)
    return inside + OMEGA * (target - image) / diagonal


def pad_rim(array, width):
    widths = ((0, 0),) * (array.ndim - 2) + ((width, width), (width, width))
    return jnp.pad(array, widths)


def restrict(array):
    shape = array.shape
    blocks = array.reshape(shape[:-2] + (shape[-2] // 2, 2, shape[-1] // 2, 2))
    return jnp.mean(blocks, axis=(-3, -1))


def prolong(array):
    return jnp.repeat(jnp.repeat(array, 2, axis=-2), 2, axis=-1)


def cycle(level, target, coefs):
    horizontal = 0.25 ** level
    coef_pad = pad_rim(coefs, 1)
    solution = jnp.zeros_like(target)
    if level == LEVELS - 1:
        def coarse_step(iteration, current):
            return jacobi_update(current, target, pad_rim(current, 1), coef_pad, horizontal)
        return lax.fori_loop(0, COARSE_ITERS, coarse_step, solution)
    for sweep in range(SWEEPS):
        solution = jacobi_update(solution, target, pad_rim(solution, 1), coef_pad, horizontal)
    image, diagonal = apply_operator(pad_rim(solution, 1), coef_pad, horizontal)
    remainder = target - image
    correction = cycle(level + 1, restrict(remainder), restrict(coefs))
    solution = solution + prolong(correction)
    for sweep in range(SWEEPS):
        solution = jacobi_update(solution, target, pad_rim(solution, 1), coef_pad, horizontal)
    return solution


def reference(misfit, viscosity, friction, ice_mask, grounded):
    ice_share = ice_mask.astype(jnp.float32)
    drag_term = friction * grounded.astype(jnp.float32)
    coefs = jnp.concatenate([viscosity, ice_share[None], drag_term[None]], 0)
    return cycle(0, misfit * ice_share, coefs)
```

```python
import functools

import jax
import jax.numpy as jnp
from jax import lax
from jax.experimental import pallas as pl
from jax.experimental.pallas import tpu as pltpu
from jax.sharding import PartitionSpec as P

LEVELS = 4
COARSE_ITERS = 20
OMEGA = 0.6
CROSS = 0.75
NP = 56
LANES = 128
RIM0 = 4
RIM1 = 13
RIM2 = 6
RIM3 = 2
STRIP1 = 16
NC = 15
VMEM_LIMIT = 60 * 1024 * 1024
F32 = jnp.float32


def rows_loop(first, last, body, unroll):
    count = (last - first) // unroll

    def step(i, carry):
        for j in range(unroll):
            body(first + i * unroll + j)
        return carry

    if count:
        lax.fori_loop(0, count, step, 0)
    for r in range(first + count * unroll, last):
        body(r)


def lane_ids(rows=8):
    return lax.broadcasted_iota(jnp.int32, (rows, LANES), 1)


def shifted(tiles, closed):
    lane = lax.broadcasted_iota(jnp.int32, tiles[0].shape, 1)
    up = [pltpu.roll(v, LANES - 1, 1) for v in tiles]
    down = [pltpu.roll(v, 1, 1) for v in tiles]
    n = len(tiles)
    if closed:
        zero = jnp.zeros_like(tiles[0])
        return (
            [jnp.where(lane == LANES - 1, zero, v) for v in up],
            [jnp.where(lane == 0, zero, v) for v in down],
        )
    if n == 1:
        return up, down
    return (
        [jnp.where(lane == LANES - 1, up[(t + 1) % n], up[t]) for t in range(n)],
        [jnp.where(lane == 0, down[(t - 1) % n], down[t]) for t in range(n)],
    )


def twice(v):
    return jnp.concatenate([v, v], 0)


def make_coefs(data, coef, scaled, diag, first, last, horizontal, closed, unroll):
    nt = data.shape[1]
    sub = lax.broadcasted_iota(jnp.int32, (8, LANES), 0)

    def row(r):
        mids = [data[r, t, 32:48, :] for t in range(nt)]
        norths, souths = shifted(mids, closed)
        for t in range(nt):
            mid = mids[t]
            west = (0.5 * horizontal) * (mid + data[r - 1, t, 32:48, :])
            east = (0.5 * horizontal) * (mid + data[r + 1, t, 32:48, :])
            north = (0.5 * horizontal) * (mid + norths[t])
            south = (0.5 * horizontal) * (mid + souths[t])
            low, high = mid[:8], mid[8:]
            inner = 2.0 * (low + high)
            outer = jnp.where(sub == 7, 0.0, 2.0 * (high + pltpu.roll(low, 7, 0)))
            outer_down = pltpu.roll(outer, 1, 0)
            coef[r, t, 0:16, :] = west
            coef[r, t, 16:32, :] = north
            coef[r, t, 32:48, :] = south
            coef[r, t, 48:64, :] = (CROSS * horizontal) * mid
            coef[r, t, 64:72, :] = inner
            coef[r, t, 72:80, :] = outer
            coef[r, t, 80:88, :] = outer_down
            ice = data[r, t, 48:49, :]
            drag = data[r, t, 49:50, :]
            bottom = jnp.where(sub == 0, drag, 0.0)
            upright = jnp.concatenate([inner + outer_down + bottom, inner + outer], 0)
            along_x = east + west
            along_y = north + south
            rest = 1.0 - ice
            for c, lateral in enumerate((4.0 * along_x + along_y, along_x + 4.0 * along_y)):
                diagonal = ice * (lateral + upright) + rest
                inverse = OMEGA / diagonal
                coef[r, t, 88 + 16 * c : 104 + 16 * c, :] = ice * inverse
                scaled[r, t, 16 * c : 16 * c + 16, :] = inverse * data[r, t, 16 * c : 16 * c + 16, :]
                if diag is not None:
                    diag[r, t, 16 * c : 16 * c + 16, :] = diagonal

    rows_loop(first, last, row, unroll)


def prepare(w, coef, slope, across, first, last, closed, unroll):
    nt = w.shape[1]

    def row(r):
        norths, souths = shifted([w[r, t] for t in range(nt)], closed)
        for t in range(nt):
            slope[r, t] = norths[t] - souths[t]
            across[r, t] = twice(coef[r, t, 16:32, :]) * norths[t] + twice(coef[r, t, 32:48, :]) * souths[t]

    rows_loop(first, last, row, unroll)


def off_diagonal(w, coef, slope, across, r, t):
    here = w[r, t]
    along = twice(coef[r + 1, t, 0:16, :]) * w[r + 1, t] + twice(coef[r, t, 0:16, :]) * w[r - 1, t]
    side = across[r, t]
    mixed = slope[r + 1, t] - slope[r - 1, t]
    cross = coef[r, t, 48:64, :]
    inner = coef[r, t, 64:72, :]
    outer = coef[r, t, 72:80, :]
    outer_down = coef[r, t, 80:88, :]
    parts = []
    for c in range(2):
        mine = slice(16 * c, 16 * c + 16)
        other = slice(16 - 16 * c, 32 - 16 * c)
        low, high = here[16 * c : 16 * c + 8], here[16 * c + 8 : 16 * c + 16]
        column = jnp.concatenate(
            [inner * high + outer_down * pltpu.roll(high, 1, 0), inner * low + outer * pltpu.roll(low, 7, 0)], 0
        )
        if c == 0:
            lateral = 4.0 * along[mine] + side[mine]
        else:
            lateral = along[mine] + 4.0 * side[mine]
        parts.append(lateral + cross * mixed[other] + column)
    return here, jnp.concatenate(parts, 0)


def sweep(w, new, coef, scaled, slope, across, first, last, closed, unroll, tiles=None, emit=None):
    nt = w.shape[1]
    prepare(w, coef, slope, across, first - 1, last + 1, closed, unroll)

    def row(r):
        for t in range(nt if tiles is None else tiles):
            here, total = off_diagonal(w, coef, slope, across, r, t)
            value = (1.0 - OMEGA) * here + scaled[r, t] + coef[r, t, 88:120, :] * total
            if emit is None:
                new[r, t] = value
            else:
                emit(r, t, value)

    rows_loop(first, last, row, unroll)


def remainders(w, out, data, diag, coef, slope, across, first, last, unroll, tiles):
    prepare(w, coef, slope, across, first - 1, last + 1, False, unroll)

    def row(r):
        for t in range(tiles):
            here, total = off_diagonal(w, coef, slope, across, r, t)
            out[r, t] = data[r, t, 0:32, :] + data[r, t, 48:49, :] * total - diag[r, t] * here

    rows_loop(first, last, row, unroll)


def gather_lanes(v, index):
    return jnp.take_along_axis(v, index, axis=1, mode="promise_in_bounds")


def halve(first, second):
    lane = lax.broadcasted_iota(jnp.int32, first.shape, 1)
    even = (2 * lane) % LANES
    low = gather_lanes(first + pltpu.roll(first, LANES - 1, 1), even)
    if second is None:
        return low
    high = gather_lanes(second + pltpu.roll(second, LANES - 1, 1), even)
    return jnp.where(lane < LANES // 2, low, high)


def restrict_row(source, planes, r):
    both = [source[r, t, planes, :] + source[r + 1, t, planes, :] for t in range(min(2, source.shape[1]))]
    return 0.25 * halve(both[0], both[1] if len(both) > 1 else None)


def prolong_row(tiles, fine_tiles):
    lane = lax.broadcasted_iota(jnp.int32, tiles[0].shape, 1)
    low = lane // 2
    high = LANES // 2 + lane // 2
    first = tiles[0]
    last = tiles[-1]
    out = [gather_lanes(first, low)]
    if fine_tiles == 2:
        out.append(gather_lanes(first, high))
    else:
        out.append(gather_lanes(first, high))
        out.append(gather_lanes(last, jnp.where(lane < LANES // 2, low, high)))
    return out


def put(strip, v, shift, width, at):
    lane = lax.broadcasted_iota(jnp.int32, v.shape, 1)
    rolled = pltpu.roll(v, shift % LANES, 1) if shift % LANES else v
    return jnp.where((lane >= at) & (lane < at + width), rolled, strip)


def unpack_rim(left, right, at, width):
    lane = lax.broadcasted_iota(jnp.int32, left.shape, 1)
    to_low = pltpu.roll(right, (LANES - at) % LANES, 1) if at else right
    shift = (2 * LANES - width - at) % LANES
    to_high = pltpu.roll(left, shift, 1) if shift else left
    return jnp.where(lane < LANES // 2, to_low, to_high)


def arrange_kernel(misfit, viscosity, friction, ice_mask, grounded, data, strips, misfit_half, viscosity_half, sems):
    rows = friction.shape[0]
    copies = []
    for t in range(2):
        lanes = pl.ds(t * LANES, LANES)
        copies.append(pltpu.make_async_copy(misfit.at[:, lanes], misfit_half.at[t], sems.at[t]))
        copies.append(pltpu.make_async_copy(viscosity.at[:, lanes], viscosity_half.at[t], sems.at[2 + t]))
    for copy in copies:
        copy.start()
    for copy in copies:
        copy.wait()
    sub = lax.broadcasted_iota(jnp.int32, (8, LANES), 0)
    stride = 2 * rows

    def eight(i, carry):
        block = pl.ds(pl.multiple_of(8 * i, 8), 8)
        for t in range(2):
            lanes = pl.ds(t * LANES, LANES)
            ices = ice_mask[block, lanes].astype(F32)
            drags = friction[block, lanes] * grounded[block, lanes].astype(F32)
            for j in range(8):
                r = 8 * i + j
                ice, drag = ices[j : j + 1], drags[j : j + 1]
                for c in range(2):
                    for p in range(2):
                        v = misfit_half[t, pl.ds(c * 16 * rows + p * rows + r, 8, stride=stride), :]
                        data[r, t, 16 * c + 8 * p : 16 * c + 8 * p + 8, :] = v * ice
                for p in range(2):
                    data[r, t, 32 + 8 * p : 40 + 8 * p, :] = viscosity_half[t, pl.ds(p * rows + r, 8, stride=stride), :]
                data[r, t, 48:56, :] = jnp.where(sub == 0, ice, jnp.where(sub == 1, drag, 0.0))
        return carry

    lax.fori_loop(0, rows // 8, eight, 0)
    for side in range(2):
        for first in range(0, NP, 8):
            planes = slice(first, first + 8)
            strip = jnp.zeros((8, LANES), F32)
            for r in range(rows):
                at = r * RIM0
                strip = put(strip, data[r, side, planes, :], at if side == 0 else at + RIM0, RIM0, at)
            strips[side, planes, :] = strip


def down0_kernel(own, sent, from_low, from_high, coarse, strips1, w_out, coef_out, scaled_out,
                 data, coef, scaled, diag, wa, slope, across, sems):
    rows = own.shape[0]
    total = rows + 2 * RIM0

    def copy_row(r):
        for t in range(2):
            data[RIM0 + r, t] = own[r, t]

    rows_loop(0, rows, copy_row, 4)
    for r in range(rows):
        data[RIM0 + r, 2] = unpack_rim(sent[2 * RIM0], sent[2 * RIM0 + 1], r * RIM0, RIM0)
    for r in range(RIM0):
        for t in range(2):
            data[r, t] = from_low[2 * r + t]
            data[RIM0 + rows + r, t] = from_high[2 * r + t]
        low_at = (rows - RIM0 + r) * RIM0
        data[r, 2] = unpack_rim(from_low[2 * RIM0], from_low[2 * RIM0 + 1], low_at, RIM0)
        data[RIM0 + rows + r, 2] = unpack_rim(from_high[2 * RIM0], from_high[2 * RIM0 + 1], r * RIM0, RIM0)

    make_coefs(data, coef, scaled, diag, 1, total - 1, 1.0, False, 1)
    copies = [pltpu.make_async_copy(coef, coef_out, sems.at[0]), pltpu.make_async_copy(scaled, scaled_out, sems.at[1])]
    for copy in copies:
        copy.start()
    sweep(scaled, wa, coef, scaled, slope, across, 2, total - 2, False, 1)
    copies.append(pltpu.make_async_copy(wa, w_out, sems.at[2]))
    copies[-1].start()

    def coefs_row(i):
        coarse[i, 32:56, :] = restrict_row(data, slice(32, 56), RIM0 + 2 * i)

    rows_loop(0, rows // 2, coefs_row, 2)
    remainders(wa, diag, data, diag, coef, slope, across, RIM0, RIM0 + rows, 1, 2)

    def target_row(i):
        coarse[i, 0:32, :] = restrict_row(diag, slice(0, 32), RIM0 + 2 * i)

    rows_loop(0, rows // 2, target_row, 2)
    group = LANES // STRIP1
    for side in range(2):
        for part in range(rows // 2 // group):
            for first in range(0, NP, 8):
                planes = slice(first, first + 8)
                strip = jnp.zeros((8, LANES), F32)
                for j in range(group):
                    at = j * STRIP1
                    shift = at if side == 0 else at + STRIP1
                    strip = put(strip, coarse[part * group + j, planes, :], shift, STRIP1, at)
                strips1[side, part, planes, :] = strip
    for copy in copies:
        copy.wait()


def down12_kernel(own, sent, from_low, from_high, piece, w1_out, coef1_out, scaled1_out, w2_out, coef2_out, scaled2_out,
                  data1, coef1, scaled1, diag1, wa1, slope1, across1,
                  data2, coef2, scaled2, diag2, wa2, slope2, across2, sems):
    rows = own.shape[0]
    total = rows + 2 * RIM1
    group = LANES // STRIP1
    parts = rows // group

    def rim(source, base, r):
        part, j = r // group, r % group
        return unpack_rim(source[base + part], source[base + parts + part], j * STRIP1, STRIP1)

    def copy_row(r):
        data1[RIM1 + r, 0] = own[r]

    rows_loop(0, rows, copy_row, 4)

    def copy_rim(r):
        data1[r, 0] = from_low[r]
        data1[RIM1 + rows + r, 0] = from_high[r]

    rows_loop(0, RIM1, copy_rim, 1)
    for r in range(rows):
        data1[RIM1 + r, 1] = rim(sent, RIM1, r)
    for r in range(RIM1):
        data1[r, 1] = rim(from_low, RIM1, rows - RIM1 + r)
        data1[RIM1 + rows + r, 1] = rim(from_high, RIM1, r)

    make_coefs(data1, coef1, scaled1, diag1, 1, total - 1, 0.25, False, 2)
    copies = [pltpu.make_async_copy(coef1, coef1_out, sems.at[0]), pltpu.make_async_copy(scaled1, scaled1_out, sems.at[1])]
    for copy in copies:
        copy.start()
    sweep(scaled1, wa1, coef1, scaled1, slope1, across1, 2, total - 2, False, 2)
    copies.append(pltpu.make_async_copy(wa1, w1_out, sems.at[2]))
    copies[-1].start()
    remainders(wa1, diag1, data1, diag1, coef1, slope1, across1, 3, total - 3, 2, 2)

    rows2 = rows // 2
    total2 = rows2 + 2 * RIM2

    def coefs_row(i):
        data2[i, 0, 32:56, :] = restrict_row(data1, slice(32, 56), 1 + 2 * i)

    rows_loop(0, total2, coefs_row, 2)

    def target_row(i):
        data2[i, 0, 0:32, :] = restrict_row(diag1, slice(0, 32), 1 + 2 * i)

    rows_loop(1, total2 - 1, target_row, 2)

    make_coefs(data2, coef2, scaled2, diag2, 1, total2 - 1, 0.0625, False, 2)
    sweep(scaled2, wa2, coef2, scaled2, slope2, across2, 2, total2 - 2, False, 2)
    late = [
        pltpu.make_async_copy(coef2, coef2_out, sems.at[3]),
        pltpu.make_async_copy(scaled2, scaled2_out, sems.at[4]),
        pltpu.make_async_copy(wa2, w2_out, sems.at[5]),
    ]
    for copy in late:
        copy.start()
    remainders(wa2, diag2, data2, diag2, coef2, slope2, across2, RIM2, RIM2 + rows2, 2, 1)

    rows3 = rows2 // 2
    width = LANES // rows3
    for first in range(0, NP, 8):
        planes = slice(first, first + 8)
        source = diag2 if first < 32 else data2
        strip = jnp.zeros((8, LANES), F32)
        for i in range(rows3):
            strip = put(strip, restrict_row(source, planes, RIM2 + 2 * i), i * width, width, i * width)
        piece[planes, :] = strip
    for copy in copies + late:
        copy.wait()


def up_kernel(place, pieces, w0_in, coef0_in, scaled0_in, w1_in, coef1_in, scaled1_in, w2_in, coef2_in, scaled2_in, result,
              data3, coef3, scaled3, wa3, wb3, slope3, across3,
              wa2, wb2, coef2, scaled2, slope2, across2,
              wa1, wb1, coef1, scaled1, slope1, across1,
              wa0, wb0, coef0, scaled0, slope0, across0, result_half, sems):
    copies = [
        pltpu.make_async_copy(source, target, sems.at[n])
        for n, (source, target) in enumerate(
            (
                (w2_in, wa2), (coef2_in, coef2), (scaled2_in, scaled2),
                (w1_in, wa1), (coef1_in, coef1), (scaled1_in, scaled1),
                (w0_in, wa0), (coef0_in, coef0), (scaled0_in, scaled0),
            )
        )
    ]
    for copy in copies:
        copy.start()

    devices_x, devices_y = pieces.shape[0], pieces.shape[1]
    rows3 = devices_y
    width = LANES // devices_y
    whole = devices_x * rows3
    zero = jnp.zeros((NP, LANES), F32)
    for r in range(RIM3):
        for end in (r, RIM3 + whole + r):
            data3[end, 0] = zero
            wa3[end, 0] = zero[:32]
            wb3[end, 0] = zero[:32]
            scaled3[end, 0] = zero[:32]
            slope3[end, 0] = zero[:32]
            coef3[end, 0, 0:16, :] = zero[:16]

    def assemble(d, carry):
        for i in range(rows3):
            line = jnp.zeros((NP, LANES), F32)
            for j in range(devices_y):
                line = put(line, pieces[d, j], (j - i) * width, width, j * width)
            data3[RIM3 + d * rows3 + i, 0] = line
        return carry

    lax.fori_loop(0, devices_x, assemble, 0)
    first, last = RIM3, RIM3 + whole
    make_coefs(data3, coef3, scaled3, None, first, last, 0.25 ** (LEVELS - 1), True, 2)

    def coarse_sweep(source, target):
        def look(r):
            norths, souths = shifted([source[r, 0]], True)
            slope3[r, 0] = norths[0] - souths[0]
            across3[r, 0] = twice(coef3[r, 0, 16:32, :]) * norths[0] + twice(coef3[r, 0, 32:48, :]) * souths[0]

        rows_loop(first, last, look, 4)

        def row(r):
            here, total = off_diagonal(source, coef3, slope3, across3, r, 0)
            target[r, 0] = (1.0 - OMEGA) * here + scaled3[r, 0] + coef3[r, 0, 88:120, :] * total

        rows_loop(first, last, row, 4)

    coarse_sweep(scaled3, wa3)

    def two_sweeps(i, carry):
        coarse_sweep(wa3, wb3)
        coarse_sweep(wb3, wa3)
        return carry

    lax.fori_loop(0, (COARSE_ITERS - 2) // 2, two_sweeps, 0)

    gx, gy, = place[0], place[1]
    lane = lane_ids(32)
    y = jnp.where(lane < 96, lane, lane - LANES)
    column = gy * width + (y + LANES) // 2 - LANES // 2
    inside = (column >= 0) & (column < LANES)
    pick = jnp.where(inside, column, 0)

    for copy in copies[:3]:
        copy.wait()
    rows2 = 2 * rows3
    for i in range(rows2 // 2 + 2 * RIM3):
        line = wa3[gx * rows3 + i, 0]
        add = jnp.where(inside, gather_lanes(line, pick), 0.0)
        for r in (2 * i + 2, 2 * i + 3):
            wa2[r, 0] = wa2[r, 0] + add
    total2 = rows2 + 2 * RIM2
    sweep(wa2, wb2, coef2, scaled2, slope2, across2, 3, total2 - 3, False, 2)
    sweep(wb2, wa2, coef2, scaled2, slope2, across2, 4, total2 - 4, False, 2)

    for copy in copies[3:6]:
        copy.wait()

    def add1(r):
        adds = prolong_row([wa2[r, 0]], 2)
        for t in range(2):
            for fine in (2 * r + 1, 2 * r + 2):
                wa1[fine, t] = wa1[fine, t] + adds[t]

    rows_loop(4, total2 - 4, add1, 2)
    total1 = 2 * rows2 + 2 * RIM1
    sweep(wa1, wb1, coef1, scaled1, slope1, across1, 11, total1 - 11, False, 2)
    sweep(wb1, wa1, coef1, scaled1, slope1, across1, 12, total1 - 12, False, 2)

    for copy in copies[6:]:
        copy.wait()

    def add0(r):
        adds = prolong_row([wa1[r, t] for t in range(2)], 3)
        for t in range(3):
            for fine in (2 * r - 22, 2 * r - 21):
                wa0[fine, t] = wa0[fine, t] + adds[t]

    rows_loop(12, total1 - 12, add0, 2)
    rows0 = 4 * rows2
    total0 = rows0 + 2 * RIM0
    sweep(wa0, wb0, coef0, scaled0, slope0, across0, 3, total0 - 3, False, 1)

    def emit(r, t, value):
        for c in range(2):
            for p in range(2):
                start = c * 16 * rows0 + p * rows0 + r - RIM0
                result_half[t, pl.ds(start, 8, stride=2 * rows0), :] = value[16 * c + 8 * p : 16 * c + 8 * p + 8]

    sweep(wb0, None, coef0, scaled0, slope0, across0, RIM0, RIM0 + rows0, False, 1, tiles=2, emit=emit)
    copies = [
        pltpu.make_async_copy(result_half.at[t], result.at[:, pl.ds(t * LANES, LANES)], sems.at[t]) for t in range(2)
    ]
    for copy in copies:
        copy.start()
    for copy in copies:
        copy.wait()


def shape(*dims):
    return jax.ShapeDtypeStruct(dims, F32)


VM = pl.BlockSpec(memory_space=pltpu.VMEM)
SM = pl.BlockSpec(memory_space=pltpu.SMEM)
HB = pl.BlockSpec(memory_space=pl.ANY)
PARAMS = pltpu.CompilerParams(vmem_limit_bytes=VMEM_LIMIT)


def buffers(rows, tiles, names):
    planes = {"data": NP, "coef": 8 * NC}
    return [pltpu.VMEM((rows, tiles, planes.get(name, 32), LANES), F32) for name in names]


def per_device(misfit, viscosity, friction, ice_mask, grounded):
    rows, columns = friction.shape
    gx, gy = lax.axis_index("gx"), lax.axis_index("gy")
    nx, ny = lax.axis_size("gx"), lax.axis_size("gy")
    upward = [(i, i + 1) for i in range(nx - 1)]
    downward = [(i + 1, i) for i in range(nx - 1)]

    def beside(strips):
        every = lax.all_gather(strips, "gy", axis=0)
        left = lax.dynamic_index_in_dim(every, jnp.maximum(gy - 1, 0), 0, keepdims=False)[1]
        right = lax.dynamic_index_in_dim(every, jnp.minimum(gy + 1, ny - 1), 0, keepdims=False)[0]
        return jnp.where(gy > 0, left, 0.0), jnp.where(gy < ny - 1, right, 0.0)

    data0, strips0 = pl.pallas_call(
        arrange_kernel,
        out_shape=(shape(rows, 2, NP, LANES), shape(2, NP, LANES)),
        in_specs=[HB, HB, VM, VM, VM],
        out_specs=(VM, VM),
        scratch_shapes=[
            pltpu.VMEM((2, 2 * 16 * rows, LANES), F32),
            pltpu.VMEM((2, 16 * rows, LANES), F32),
            pltpu.SemaphoreType.DMA((4,)),
        ],
        compiler_params=PARAMS,
        name="arrange",
    )(misfit.reshape(-1, columns), viscosity.reshape(-1, columns), friction, ice_mask, grounded)
    left, right = beside(strips0)
    rims = [left[None], right[None]]
    low_face = jnp.concatenate([data0[:RIM0].reshape(-1, NP, LANES)] + rims, 0)
    high_face = jnp.concatenate([data0[rows - RIM0 :].reshape(-1, NP, LANES)] + rims, 0)
    from_low = lax.ppermute(high_face, "gx", upward)
    from_high = lax.ppermute(low_face, "gx", downward)

    total0 = rows + 2 * RIM0
    rows1 = rows // 2
    group = LANES // STRIP1
    field0 = shape(total0, 3, 32, LANES)
    data1, strips1, w0, coef0, scaled0 = pl.pallas_call(
        down0_kernel,
        out_shape=(
            shape(rows1, NP, LANES),
            shape(2, rows1 // group, NP, LANES),
            field0,
            shape(total0, 3, 8 * NC, LANES),
            field0,
        ),
        in_specs=[VM] * 4,
        out_specs=(VM, VM, HB, HB, HB),
        scratch_shapes=buffers(total0, 3, ("data", "coef", "scaled", "diag", "w", "slope", "across"))
        + [pltpu.SemaphoreType.DMA((3,))],
        compiler_params=PARAMS,
        name="down0",
    )(data0, low_face, from_low, from_high)

    left, right = beside(strips1)
    low_face = jnp.concatenate([data1[:RIM1], left, right], 0)
    high_face = jnp.concatenate([data1[rows1 - RIM1 :], left, right], 0)
    from_low = lax.ppermute(high_face, "gx", upward)
    from_high = lax.ppermute(low_face, "gx", downward)

    total1 = rows1 + 2 * RIM1
    rows2 = rows1 // 2
    total2 = rows2 + 2 * RIM2
    field1 = shape(total1, 2, 32, LANES)
    field2 = shape(total2, 1, 32, LANES)
    names = ("data", "coef", "scaled", "diag", "w", "slope", "across")
    piece, w1, coef1, scaled1, w2, coef2, scaled2 = pl.pallas_call(
        down12_kernel,
        out_shape=(
            shape(NP, LANES),
            field1,
            shape(total1, 2, 8 * NC, LANES),
            field1,
            field2,
            shape(total2, 1, 8 * NC, LANES),
            field2,
        ),
        in_specs=[VM] * 4,
        out_specs=(VM,) + (HB,) * 6,
        scratch_shapes=buffers(total1, 2, names) + buffers(total2, 1, names) + [pltpu.SemaphoreType.DMA((6,))],
        compiler_params=PARAMS,
        name="down12",
    )(data1, low_face, from_low, from_high)

    pieces = lax.all_to_all(jnp.broadcast_to(piece, (nx * ny,) + piece.shape), ("gx", "gy"), 0, 0)
    pieces = pieces.reshape((nx, ny) + piece.shape)

    rows3 = rows2 // 2
    total3 = nx * rows3 + 2 * RIM3
    ups = ("w", "w", "coef", "scaled", "slope", "across")
    result = pl.pallas_call(
        up_kernel,
        out_shape=shape(2 * 16 * rows, columns),
        in_specs=[SM, VM] + [HB] * 9,
        out_specs=HB,
        scratch_shapes=buffers(total3, 1, ("data", "coef", "scaled", "w", "w", "slope", "across"))
        + buffers(total2, 1, ups)
        + buffers(total1, 2, ups)
        + buffers(total0, 3, ups)
        + [pltpu.VMEM((2, 2 * 16 * rows, LANES), F32), pltpu.SemaphoreType.DMA((9,))],
        compiler_params=PARAMS,
        name="up",
    )(jnp.stack([gx, gy]).astype(jnp.int32), pieces, w0, coef0, scaled0, w1, coef1, scaled1, w2, coef2, scaled2)
    return result.reshape(misfit.shape)


def solution(mesh):
    placed = (
        P(None, None, "gx", "gy"),
        P(None, "gx", "gy"),
        P("gx", "gy"),
        P("gx", "gy"),
        P("gx", "gy"),
    )
    return jax.shard_map(
        per_device, mesh=mesh, in_specs=placed, out_specs=P(None, None, "gx", "gy"), check_vma=False
    )
```

```python
import functools

import jax
import jax.numpy as jnp
from jax import lax
from jax.experimental import pallas as pl
from jax.experimental.pallas import tpu as pltpu
from jax.sharding import PartitionSpec as P

LEVELS = 4
COARSE_ITERS = 20
OMEGA = 0.6
CROSS = 0.75
NP = 56
LANES = 128
RIM0 = 4
RIM1 = 13
RIM2 = 6
RIM3 = 2
STRIP1 = 16
NC = 15
VMEM_DOWN = 20 * 1024 * 1024
VMEM_UP = 39 * 1024 * 1024
F32 = jnp.float32
UNROLL0 = (18, 6, 4)
UNROLL1 = (18, 6, 4)
UNROLL2 = (18, 6, 4)
UNROLL3 = (32, 32, 2)
UNROLL_MOVE = 8


def rows_loop(first, last, body, unroll):
    count = (last - first) // unroll

    def step(i, carry):
        for j in range(unroll):
            body(first + i * unroll + j)
        return carry

    if count:
        lax.fori_loop(0, count, step, 0)
    for r in range(first + count * unroll, last):
        body(r)


def lane_ids(rows=8):
    return lax.broadcasted_iota(jnp.int32, (rows, LANES), 1)


def shifted(tiles, closed):
    lane = lax.broadcasted_iota(jnp.int32, tiles[0].shape, 1)
    up = [pltpu.roll(v, LANES - 1, 1) for v in tiles]
    down = [pltpu.roll(v, 1, 1) for v in tiles]
    n = len(tiles)
    if closed:
        zero = jnp.zeros_like(tiles[0])
        return (
            [jnp.where(lane == LANES - 1, zero, v) for v in up],
            [jnp.where(lane == 0, zero, v) for v in down],
        )
    if n == 1:
        return up, down
    return (
        [jnp.where(lane == LANES - 1, up[(t + 1) % n], up[t]) for t in range(n)],
        [jnp.where(lane == 0, down[(t - 1) % n], down[t]) for t in range(n)],
    )


def twice(v):
    return jnp.concatenate([v, v], 0)


def make_coefs(data, coef, scaled, diag, first, last, horizontal, closed, unroll):
    nt = data.shape[1]
    sub = lax.broadcasted_iota(jnp.int32, (8, LANES), 0)

    def row(r):
        mids = [data[r, t, 32:48, :] for t in range(nt)]
        norths, souths = shifted(mids, closed)
        for t in range(nt):
            mid = mids[t]
            west = (0.5 * horizontal) * (mid + data[r - 1, t, 32:48, :])
            east = (0.5 * horizontal) * (mid + data[r + 1, t, 32:48, :])
            north = (0.5 * horizontal) * (mid + norths[t])
            south = (0.5 * horizontal) * (mid + souths[t])
            low, high = mid[:8], mid[8:]
            inner = 2.0 * (low + high)
            outer = jnp.where(sub == 7, 0.0, 2.0 * (high + pltpu.roll(low, 7, 0)))
            outer_down = pltpu.roll(outer, 1, 0)
            coef[r, t, 0:16, :] = west
            coef[r, t, 16:32, :] = north
            coef[r, t, 32:48, :] = south
            coef[r, t, 48:64, :] = (CROSS * horizontal) * mid
            coef[r, t, 64:72, :] = inner
            coef[r, t, 72:80, :] = outer
            coef[r, t, 80:88, :] = outer_down
            ice = data[r, t, 48:49, :]
            drag = data[r, t, 49:50, :]
            bottom = jnp.where(sub == 0, drag, 0.0)
            upright = jnp.concatenate([inner + outer_down + bottom, inner + outer], 0)
            along_x = east + west
            along_y = north + south
            rest = 1.0 - ice
            for c, lateral in enumerate((4.0 * along_x + along_y, along_x + 4.0 * along_y)):
                diagonal = ice * (lateral + upright) + rest
                inverse = OMEGA / diagonal
                coef[r, t, 88 + 16 * c : 104 + 16 * c, :] = ice * inverse
                scaled[r, t, 16 * c : 16 * c + 16, :] = inverse * data[r, t, 16 * c : 16 * c + 16, :]
                if diag is not None:
                    diag[r, t, 16 * c : 16 * c + 16, :] = diagonal

    rows_loop(first, last, row, unroll)


def prepare(w, coef, slope, across, first, last, closed, unroll):
    nt = w.shape[1]

    def row(r):
        norths, souths = shifted([w[r, t] for t in range(nt)], closed)
        for t in range(nt):
            slope[r, t] = norths[t] - souths[t]
            across[r, t] = twice(coef[r, t, 16:32, :]) * norths[t] + twice(coef[r, t, 32:48, :]) * souths[t]

    rows_loop(first, last, row, unroll)


def off_diagonal(w, coef, slope, across, r, t):
    here = w[r, t]
    along = twice(coef[r + 1, t, 0:16, :]) * w[r + 1, t] + twice(coef[r, t, 0:16, :]) * w[r - 1, t]
    side = across[r, t]
    mixed = slope[r + 1, t] - slope[r - 1, t]
    cross = coef[r, t, 48:64, :]
    inner = coef[r, t, 64:72, :]
    outer = coef[r, t, 72:80, :]
    outer_down = coef[r, t, 80:88, :]
    parts = []
    for c in range(2):
        mine = slice(16 * c, 16 * c + 16)
        other = slice(16 - 16 * c, 32 - 16 * c)
        low, high = here[16 * c : 16 * c + 8], here[16 * c + 8 : 16 * c + 16]
        column = jnp.concatenate(
            [inner * high + outer_down * pltpu.roll(high, 1, 0), inner * low + outer * pltpu.roll(low, 7, 0)], 0
        )
        if c == 0:
            lateral = 4.0 * along[mine] + side[mine]
        else:
            lateral = along[mine] + 4.0 * side[mine]
        parts.append(lateral + cross * mixed[other] + column)
    return here, jnp.concatenate(parts, 0)


def sweep(w, new, coef, scaled, slope, across, first, last, closed, unroll, tiles=None, emit=None):
    look, unroll, _ = unroll
    nt = w.shape[1]
    prepare(w, coef, slope, across, first - 1, last + 1, closed, look)

    def row(r):
        for t in range(nt if tiles is None else tiles):
            here, total = off_diagonal(w, coef, slope, across, r, t)
            value = (1.0 - OMEGA) * here + scaled[r, t] + coef[r, t, 88:120, :] * total
            if emit is None:
                new[r, t] = value
            else:
                emit(r, t, value)

    rows_loop(first, last, row, unroll)


def remainders(w, out, data, diag, coef, slope, across, first, last, unroll, tiles):
    look, unroll, _ = unroll
    prepare(w, coef, slope, across, first - 1, last + 1, False, look)

    def row(r):
        for t in range(tiles):
            here, total = off_diagonal(w, coef, slope, across, r, t)
            out[r, t] = data[r, t, 0:32, :] + data[r, t, 48:49, :] * total - diag[r, t] * here

    rows_loop(first, last, row, unroll)


def gather_lanes(v, index):
    return jnp.take_along_axis(v, index, axis=1, mode="promise_in_bounds")


def halve(first, second):
    lane = lax.broadcasted_iota(jnp.int32, first.shape, 1)
    even = (2 * lane) % LANES
    low = gather_lanes(first + pltpu.roll(first, LANES - 1, 1), even)
    if second is None:
        return low
    high = gather_lanes(second + pltpu.roll(second, LANES - 1, 1), even)
    return jnp.where(lane < LANES // 2, low, high)


def restrict_row(source, planes, r):
    both = [source[r, t, planes, :] + source[r + 1, t, planes, :] for t in range(min(2, source.shape[1]))]
    return 0.25 * halve(both[0], both[1] if len(both) > 1 else None)


def prolong_row(tiles, fine_tiles):
    lane = lax.broadcasted_iota(jnp.int32, tiles[0].shape, 1)
    low = lane // 2
    high = LANES // 2 + lane // 2
    first = tiles[0]
    last = tiles[-1]
    out = [gather_lanes(first, low)]
    if fine_tiles == 2:
        out.append(gather_lanes(first, high))
    else:
        out.append(gather_lanes(first, high))
        out.append(gather_lanes(last, jnp.where(lane < LANES // 2, low, high)))
    return out


def put(strip, v, shift, width, at):
    lane = lax.broadcasted_iota(jnp.int32, v.shape, 1)
    rolled = pltpu.roll(v, shift % LANES, 1) if shift % LANES else v
    return jnp.where((lane >= at) & (lane < at + width), rolled, strip)


def unpack_rim(left, right, at, width):
    lane = lax.broadcasted_iota(jnp.int32, left.shape, 1)
    to_low = pltpu.roll(right, (LANES - at) % LANES, 1) if at else right
    shift = (2 * LANES - width - at) % LANES
    to_high = pltpu.roll(left, shift, 1) if shift else left
    return jnp.where(lane < LANES // 2, to_low, to_high)


def arrange_kernel(misfit, viscosity, friction, ice_mask, grounded, data, strips, misfit_half, viscosity_half, sems):
    rows = friction.shape[0]
    copies = []
    for t in range(2):
        lanes = pl.ds(t * LANES, LANES)
        copies.append(pltpu.make_async_copy(misfit.at[:, lanes], misfit_half.at[t], sems.at[t]))
        copies.append(pltpu.make_async_copy(viscosity.at[:, lanes], viscosity_half.at[t], sems.at[2 + t]))
    for copy in copies:
        copy.start()
    for copy in copies:
        copy.wait()
    sub = lax.broadcasted_iota(jnp.int32, (8, LANES), 0)
    stride = 2 * rows

    def eight(i, carry):
        block = pl.ds(pl.multiple_of(8 * i, 8), 8)
        for t in range(2):
            lanes = pl.ds(t * LANES, LANES)
            ices = ice_mask[block, lanes].astype(F32)
            drags = friction[block, lanes] * grounded[block, lanes].astype(F32)
            for j in range(8):
                r = 8 * i + j
                ice, drag = ices[j : j + 1], drags[j : j + 1]
                for c in range(2):
                    for p in range(2):
                        v = misfit_half[t, pl.ds(c * 16 * rows + p * rows + r, 8, stride=stride), :]
                        data[r, t, 16 * c + 8 * p : 16 * c + 8 * p + 8, :] = v * ice
                for p in range(2):
                    data[r, t, 32 + 8 * p : 40 + 8 * p, :] = viscosity_half[t, pl.ds(p * rows + r, 8, stride=stride), :]
                data[r, t, 48:56, :] = jnp.where(sub == 0, ice, jnp.where(sub == 1, drag, 0.0))
        return carry

    lax.fori_loop(0, rows // 8, eight, 0)
    for side in range(2):
        for first in range(0, NP, 8):
            planes = slice(first, first + 8)
            strip = jnp.zeros((8, LANES), F32)
            for r in range(rows):
                at = r * RIM0
                strip = put(strip, data[r, side, planes, :], at if side == 0 else at + RIM0, RIM0, at)
            strips[side, planes, :] = strip


def down0_kernel(own, sent, from_low, from_high, coarse, strips1, wa, coef, scaled,
                 data, diag, slope, across):
    rows = own.shape[0]
    total = rows + 2 * RIM0

    def copy_row(r):
        for t in range(2):
            data[RIM0 + r, t] = own[r, t]

    rows_loop(0, rows, copy_row, 4)
    for r in range(rows):
        data[RIM0 + r, 2] = unpack_rim(sent[2 * RIM0], sent[2 * RIM0 + 1], r * RIM0, RIM0)
    for r in range(RIM0):
        for t in range(2):
            data[r, t] = from_low[2 * r + t]
            data[RIM0 + rows + r, t] = from_high[2 * r + t]
        low_at = (rows - RIM0 + r) * RIM0
        data[r, 2] = unpack_rim(from_low[2 * RIM0], from_low[2 * RIM0 + 1], low_at, RIM0)
        data[RIM0 + rows + r, 2] = unpack_rim(from_high[2 * RIM0], from_high[2 * RIM0 + 1], r * RIM0, RIM0)

    make_coefs(data, coef, scaled, diag, 1, total - 1, 1.0, False, UNROLL0[2])
    sweep(scaled, wa, coef, scaled, slope, across, 2, total - 2, False, UNROLL0)

    def coefs_row(i):
        coarse[i, 32:56, :] = restrict_row(data, slice(32, 56), RIM0 + 2 * i)

    rows_loop(0, rows // 2, coefs_row, UNROLL_MOVE)
    remainders(wa, diag, data, diag, coef, slope, across, RIM0, RIM0 + rows, UNROLL0, 2)

    def target_row(i):
        coarse[i, 0:32, :] = restrict_row(diag, slice(0, 32), RIM0 + 2 * i)

    rows_loop(0, rows // 2, target_row, UNROLL_MOVE)
    group = LANES // STRIP1
    for side in range(2):
        for part in range(rows // 2 // group):
            for first in range(0, NP, 8):
                planes = slice(first, first + 8)
                strip = jnp.zeros((8, LANES), F32)
                for j in range(group):
                    at = j * STRIP1
                    shift = at if side == 0 else at + STRIP1
                    strip = put(strip, coarse[part * group + j, planes, :], shift, STRIP1, at)
                strips1[side, part, planes, :] = strip


def down12_kernel(own, sent, from_low, from_high, piece, wa1, coef1, scaled1, wa2, coef2, scaled2,
                  data1, diag1, slope1, across1, data2, diag2, slope2, across2):
    rows = own.shape[0]
    total = rows + 2 * RIM1
    group = LANES // STRIP1
    parts = rows // group

    def rim(source, base, r):
        part, j = r // group, r % group
        return unpack_rim(source[base + part], source[base + parts + part], j * STRIP1, STRIP1)

    def copy_row(r):
        data1[RIM1 + r, 0] = own[r]

    rows_loop(0, rows, copy_row, 4)

    def copy_rim(r):
        data1[r, 0] = from_low[r]
        data1[RIM1 + rows + r, 0] = from_high[r]

    rows_loop(0, RIM1, copy_rim, 1)
    for r in range(rows):
        data1[RIM1 + r, 1] = rim(sent, RIM1, r)
    for r in range(RIM1):
        data1[r, 1] = rim(from_low, RIM1, rows - RIM1 + r)
        data1[RIM1 + rows + r, 1] = rim(from_high, RIM1, r)

    make_coefs(data1, coef1, scaled1, diag1, 1, total - 1, 0.25, False, UNROLL1[2])
    sweep(scaled1, wa1, coef1, scaled1, slope1, across1, 2, total - 2, False, UNROLL1)
    remainders(wa1, diag1, data1, diag1, coef1, slope1, across1, 3, total - 3, UNROLL1, 2)

    rows2 = rows // 2
    total2 = rows2 + 2 * RIM2

    def coefs_row(i):
        data2[i, 0, 32:56, :] = restrict_row(data1, slice(32, 56), 1 + 2 * i)

    rows_loop(0, total2, coefs_row, UNROLL_MOVE)

    def target_row(i):
        data2[i, 0, 0:32, :] = restrict_row(diag1, slice(0, 32), 1 + 2 * i)

    rows_loop(1, total2 - 1, target_row, UNROLL_MOVE)

    make_coefs(data2, coef2, scaled2, diag2, 1, total2 - 1, 0.0625, False, UNROLL2[2])
    sweep(scaled2, wa2, coef2, scaled2, slope2, across2, 2, total2 - 2, False, UNROLL2)
    remainders(wa2, diag2, data2, diag2, coef2, slope2, across2, RIM2, RIM2 + rows2, UNROLL2, 1)

    rows3 = rows2 // 2
    width = LANES // rows3
    for first in range(0, NP, 8):
        planes = slice(first, first + 8)
        source = diag2 if first < 32 else data2
        strip = jnp.zeros((8, LANES), F32)
        for i in range(rows3):
            strip = put(strip, restrict_row(source, planes, RIM2 + 2 * i), i * width, width, i * width)
        piece[planes, :] = strip


def up_kernel(place, pieces, w0, coef0, scaled0, w1, coef1, scaled1, w2, coef2, scaled2, result,
              data3, coef3, scaled3, wa3, wb3, slope3, across3,
              wa2, wb2, wa1, wb1, wa0, wb0, slope0, across0, result_half, sems):
    slope1, across1 = (v.at[pl.ds(0, wa1.shape[0]), pl.ds(0, 2)] for v in (slope0, across0))
    slope2, across2 = (v.at[pl.ds(0, wa2.shape[0]), pl.ds(0, 1)] for v in (slope0, across0))
    devices_x, devices_y = pieces.shape[0], pieces.shape[1]
    rows3 = devices_y
    width = LANES // devices_y
    whole = devices_x * rows3
    zero = jnp.zeros((NP, LANES), F32)
    for r in range(RIM3):
        for end in (r, RIM3 + whole + r):
            data3[end, 0] = zero
            wa3[end, 0] = zero[:32]
            wb3[end, 0] = zero[:32]
            scaled3[end, 0] = zero[:32]
            slope3[end, 0] = zero[:32]
            coef3[end, 0, 0:16, :] = zero[:16]

    def assemble(d, carry):
        for i in range(rows3):
            line = jnp.zeros((NP, LANES), F32)
            for j in range(devices_y):
                line = put(line, pieces[d, j], (j - i) * width, width, j * width)
            data3[RIM3 + d * rows3 + i, 0] = line
        return carry

    lax.fori_loop(0, devices_x, assemble, 0)
    first, last = RIM3, RIM3 + whole
    make_coefs(data3, coef3, scaled3, None, first, last, 0.25 ** (LEVELS - 1), True, UNROLL3[2])

    def coarse_sweep(source, target):
        def look(r):
            norths, souths = shifted([source[r, 0]], True)
            slope3[r, 0] = norths[0] - souths[0]
            across3[r, 0] = twice(coef3[r, 0, 16:32, :]) * norths[0] + twice(coef3[r, 0, 32:48, :]) * souths[0]

        rows_loop(first, last, look, UNROLL3[0])

        def row(r):
            here, total = off_diagonal(source, coef3, slope3, across3, r, 0)
            target[r, 0] = (1.0 - OMEGA) * here + scaled3[r, 0] + coef3[r, 0, 88:120, :] * total

        rows_loop(first, last, row, UNROLL3[1])

    coarse_sweep(scaled3, wa3)

    def two_sweeps(i, carry):
        coarse_sweep(wa3, wb3)
        coarse_sweep(wb3, wa3)
        return carry

    lax.fori_loop(0, (COARSE_ITERS - 2) // 2, two_sweeps, 0)

    gx, gy, = place[0], place[1]
    lane = lane_ids(32)
    y = jnp.where(lane < 96, lane, lane - LANES)
    column = gy * width + (y + LANES) // 2 - LANES // 2
    inside = (column >= 0) & (column < LANES)
    pick = jnp.where(inside, column, 0)

    rows2 = 2 * rows3
    for i in range(rows2 // 2 + 2 * RIM3):
        line = wa3[gx * rows3 + i, 0]
        add = jnp.where(inside, gather_lanes(line, pick), 0.0)
        for r in (2 * i + 2, 2 * i + 3):
            wa2[r, 0] = w2[r, 0] + add
    total2 = rows2 + 2 * RIM2
    sweep(wa2, wb2, coef2, scaled2, slope2, across2, 3, total2 - 3, False, UNROLL2)
    sweep(wb2, wa2, coef2, scaled2, slope2, across2, 4, total2 - 4, False, UNROLL2)


    def add1(r):
        adds = prolong_row([wa2[r, 0]], 2)
        for t in range(2):
            for fine in (2 * r + 1, 2 * r + 2):
                wa1[fine, t] = w1[fine, t] + adds[t]

    rows_loop(4, total2 - 4, add1, UNROLL_MOVE)
    total1 = 2 * rows2 + 2 * RIM1
    sweep(wa1, wb1, coef1, scaled1, slope1, across1, 11, total1 - 11, False, UNROLL1)
    sweep(wb1, wa1, coef1, scaled1, slope1, across1, 12, total1 - 12, False, UNROLL1)


    def add0(r):
        adds = prolong_row([wa1[r, t] for t in range(2)], 3)
        for t in range(3):
            for fine in (2 * r - 22, 2 * r - 21):
                wa0[fine, t] = w0[fine, t] + adds[t]

    rows_loop(12, total1 - 12, add0, UNROLL_MOVE)
    rows0 = 4 * rows2
    total0 = rows0 + 2 * RIM0
    sweep(wa0, wb0, coef0, scaled0, slope0, across0, 3, total0 - 3, False, UNROLL0)

    def emit(r, t, value):
        for c in range(2):
            for p in range(2):
                start = c * 16 * rows0 + p * rows0 + r - RIM0
                result_half[t, pl.ds(start, 8, stride=2 * rows0), :] = value[16 * c + 8 * p : 16 * c + 8 * p + 8]

    sweep(wb0, None, coef0, scaled0, slope0, across0, RIM0, RIM0 + rows0, False, UNROLL0, tiles=2, emit=emit)
    copies = [
        pltpu.make_async_copy(result_half.at[t], result.at[:, pl.ds(t * LANES, LANES)], sems.at[t]) for t in range(2)
    ]
    for copy in copies:
        copy.start()
    for copy in copies:
        copy.wait()


def shape(*dims):
    return jax.ShapeDtypeStruct(dims, F32)


def kept(*dims):
    return pltpu.VMEM(dims, F32)


def keep(arrays):
    return [pltpu.with_memory_space_constraint(v, pltpu.VMEM) for v in arrays]


VM = pl.BlockSpec(memory_space=pltpu.VMEM)
SM = pl.BlockSpec(memory_space=pltpu.SMEM)
HB = pl.BlockSpec(memory_space=pl.ANY)
PARAMS = pltpu.CompilerParams(vmem_limit_bytes=VMEM_DOWN)
UP_PARAMS = pltpu.CompilerParams(vmem_limit_bytes=VMEM_UP)


def buffers(rows, tiles, names):
    planes = {"data": NP, "coef": 8 * NC}
    return [pltpu.VMEM((rows, tiles, planes.get(name, 32), LANES), F32) for name in names]


def per_device(misfit, viscosity, friction, ice_mask, grounded):
    rows, columns = friction.shape
    gx, gy = lax.axis_index("gx"), lax.axis_index("gy")
    nx, ny = lax.axis_size("gx"), lax.axis_size("gy")
    upward = [(i, i + 1) for i in range(nx - 1)]
    downward = [(i + 1, i) for i in range(nx - 1)]

    def beside(strips):
        every = lax.all_gather(strips, "gy", axis=0)
        left = lax.dynamic_index_in_dim(every, jnp.maximum(gy - 1, 0), 0, keepdims=False)[1]
        right = lax.dynamic_index_in_dim(every, jnp.minimum(gy + 1, ny - 1), 0, keepdims=False)[0]
        return jnp.where(gy > 0, left, 0.0), jnp.where(gy < ny - 1, right, 0.0)

    data0, strips0 = pl.pallas_call(
        arrange_kernel,
        out_shape=(shape(rows, 2, NP, LANES), shape(2, NP, LANES)),
        in_specs=[HB, HB, VM, VM, VM],
        out_specs=(VM, VM),
        scratch_shapes=[
            pltpu.VMEM((2, 2 * 16 * rows, LANES), F32),
            pltpu.VMEM((2, 16 * rows, LANES), F32),
            pltpu.SemaphoreType.DMA((4,)),
        ],
        compiler_params=PARAMS,
        name="arrange",
    )(
        *(pltpu.with_memory_space_constraint(v.reshape(-1, columns), pltpu.HBM) for v in (misfit, viscosity)),
        friction,
        ice_mask,
        grounded,
    )
    left, right = beside(strips0)
    rims = [left[None], right[None]]
    low_face = jnp.concatenate([data0[:RIM0].reshape(-1, NP, LANES)] + rims, 0)
    high_face = jnp.concatenate([data0[rows - RIM0 :].reshape(-1, NP, LANES)] + rims, 0)
    from_low = lax.ppermute(high_face, "gx", upward)
    from_high = lax.ppermute(low_face, "gx", downward)

    total0 = rows + 2 * RIM0
    names = ("data", "diag", "slope", "across")
    rows1 = rows // 2
    group = LANES // STRIP1
    field0 = kept(total0, 3, 32, LANES)
    data1, strips1, w0, coef0, scaled0 = pl.pallas_call(
        down0_kernel,
        out_shape=(
            shape(rows1, NP, LANES),
            shape(2, rows1 // group, NP, LANES),
            field0,
            kept(total0, 3, 8 * NC, LANES),
            field0,
        ),
        in_specs=[VM] * 4,
        out_specs=(VM,) * 5,
        scratch_shapes=buffers(total0, 3, names),
        compiler_params=PARAMS,
        name="down0",
    )(data0, low_face, from_low, from_high)

    left, right = beside(strips1)
    low_face = jnp.concatenate([data1[:RIM1], left, right], 0)
    high_face = jnp.concatenate([data1[rows1 - RIM1 :], left, right], 0)
    from_low = lax.ppermute(high_face, "gx", upward)
    from_high = lax.ppermute(low_face, "gx", downward)

    total1 = rows1 + 2 * RIM1
    rows2 = rows1 // 2
    total2 = rows2 + 2 * RIM2
    field1 = kept(total1, 2, 32, LANES)
    field2 = kept(total2, 1, 32, LANES)
    piece, w1, coef1, scaled1, w2, coef2, scaled2 = pl.pallas_call(
        down12_kernel,
        out_shape=(
            shape(NP, LANES),
            field1,
            kept(total1, 2, 8 * NC, LANES),
            field1,
            field2,
            kept(total2, 1, 8 * NC, LANES),
            field2,
        ),
        in_specs=[VM] * 4,
        out_specs=(VM,) * 7,
        scratch_shapes=buffers(total1, 2, names) + buffers(total2, 1, names),
        compiler_params=PARAMS,
        name="down12",
    )(data1, low_face, from_low, from_high)

    pieces = lax.all_to_all(jnp.broadcast_to(piece, (nx * ny,) + piece.shape), ("gx", "gy"), 0, 0)
    pieces = pieces.reshape((nx, ny) + piece.shape)

    rows3 = rows2 // 2
    total3 = nx * rows3 + 2 * RIM3
    ups = ("w", "w")
    result = pl.pallas_call(
        up_kernel,
        out_shape=shape(2 * 16 * rows, columns),
        in_specs=[SM] + [VM] * 10,
        out_specs=HB,
        scratch_shapes=buffers(total3, 1, ("data", "coef", "scaled", "w", "w", "slope", "across"))
        + buffers(total2, 1, ups)
        + buffers(total1, 2, ups)
        + buffers(total0, 3, ups)
        + buffers(max(total0, total1), 3, ("slope", "across"))
        + [pltpu.VMEM((2, 2 * 16 * rows, LANES), F32), pltpu.SemaphoreType.DMA((2,))],
        compiler_params=UP_PARAMS,
        name="up",
    )(
        jnp.stack([gx, gy]).astype(jnp.int32),
        pieces,
        *keep([w0, coef0, scaled0, w1, coef1, scaled1, w2, coef2, scaled2]),
    )
    return result.reshape(misfit.shape)


def solution(mesh):
    placed = (
        P(None, None, "gx", "gy"),
        P(None, "gx", "gy"),
        P("gx", "gy"),
        P("gx", "gy"),
        P("gx", "gy"),
    )
    return jax.shard_map(
        per_device, mesh=mesh, in_specs=placed, out_specs=P(None, None, "gx", "gy"), check_vma=False
    )
```

```python
import functools

import jax
import jax.numpy as jnp
from jax import lax
from jax.experimental import pallas as pl
from jax.experimental.pallas import tpu as pltpu
from jax.sharding import PartitionSpec as P

LEVELS = 4
COARSE_ITERS = 20
OMEGA = 0.6
CROSS = 0.75
NP = 56
LANES = 128
RIM0 = 4
RIM1 = 13
RIM2 = 6
RIM3 = 2
STRIP1 = 16
NC = 15
VMEM_DOWN = 14 * 1024 * 1024
VMEM_UP = 17 * 1024 * 1024
VMEM_COARSE = 3 * 1024 * 1024
VMEM_COARSE_ROW = 200 * 1024
F32 = jnp.float32
UNROLL0 = (18, 6, 4)
UNROLL1 = (18, 6, 4)
UNROLL2 = (18, 6, 4)
UNROLL3 = (32, 32, 2)
UNROLL_MOVE = 8


def rows_loop(first, last, body, unroll):
    count = (last - first) // unroll

    def step(i, carry):
        for j in range(unroll):
            body(first + i * unroll + j)
        return carry

    if count:
        lax.fori_loop(0, count, step, 0)
    for r in range(first + count * unroll, last):
        body(r)


def lane_ids(rows=8):
    return lax.broadcasted_iota(jnp.int32, (rows, LANES), 1)


def shifted(tiles, closed):
    lane = lax.broadcasted_iota(jnp.int32, tiles[0].shape, 1)
    up = [pltpu.roll(v, LANES - 1, 1) for v in tiles]
    down = [pltpu.roll(v, 1, 1) for v in tiles]
    n = len(tiles)
    if closed:
        zero = jnp.zeros_like(tiles[0])
        return (
            [jnp.where(lane == LANES - 1, zero, v) for v in up],
            [jnp.where(lane == 0, zero, v) for v in down],
        )
    if n == 1:
        return up, down
    return (
        [jnp.where(lane == LANES - 1, up[(t + 1) % n], up[t]) for t in range(n)],
        [jnp.where(lane == 0, down[(t - 1) % n], down[t]) for t in range(n)],
    )


def twice(v):
    return jnp.concatenate([v, v], 0)


def make_coefs(data, coef, scaled, diag, first, last, horizontal, closed, unroll):
    nt = data.shape[1]
    sub = lax.broadcasted_iota(jnp.int32, (8, LANES), 0)

    def row(r):
        mids = [data[r, t, 32:48, :] for t in range(nt)]
        norths, souths = shifted(mids, closed)
        for t in range(nt):
            mid = mids[t]
            west = (0.5 * horizontal) * (mid + data[r - 1, t, 32:48, :])
            east = (0.5 * horizontal) * (mid + data[r + 1, t, 32:48, :])
            north = (0.5 * horizontal) * (mid + norths[t])
            south = (0.5 * horizontal) * (mid + souths[t])
            low, high = mid[:8], mid[8:]
            inner = 2.0 * (low + high)
            outer = jnp.where(sub == 7, 0.0, 2.0 * (high + pltpu.roll(low, 7, 0)))
            outer_down = pltpu.roll(outer, 1, 0)
            coef[r, t, 0:16, :] = west
            coef[r, t, 16:32, :] = north
            coef[r, t, 32:48, :] = south
            coef[r, t, 48:64, :] = (CROSS * horizontal) * mid
            coef[r, t, 64:72, :] = inner
            coef[r, t, 72:80, :] = outer
            coef[r, t, 80:88, :] = outer_down
            ice = data[r, t, 48:49, :]
            drag = data[r, t, 49:50, :]
            bottom = jnp.where(sub == 0, drag, 0.0)
            upright = jnp.concatenate([inner + outer_down + bottom, inner + outer], 0)
            along_x = east + west
            along_y = north + south
            rest = 1.0 - ice
            for c, lateral in enumerate((4.0 * along_x + along_y, along_x + 4.0 * along_y)):
                diagonal = ice * (lateral + upright) + rest
                inverse = OMEGA / diagonal
                coef[r, t, 88 + 16 * c : 104 + 16 * c, :] = ice * inverse
                scaled[r, t, 16 * c : 16 * c + 16, :] = inverse * data[r, t, 16 * c : 16 * c + 16, :]
                if diag is not None:
                    diag[r, t, 16 * c : 16 * c + 16, :] = diagonal

    rows_loop(first, last, row, unroll)


def prepare(w, coef, slope, across, first, last, closed, unroll):
    nt = w.shape[1]

    def row(r):
        norths, souths = shifted([w[r, t] for t in range(nt)], closed)
        for t in range(nt):
            slope[r, t] = norths[t] - souths[t]
            across[r, t] = twice(coef[r, t, 16:32, :]) * norths[t] + twice(coef[r, t, 32:48, :]) * souths[t]

    rows_loop(first, last, row, unroll)


def off_diagonal(w, coef, slope, across, r, t):
    here = w[r, t]
    along = twice(coef[r + 1, t, 0:16, :]) * w[r + 1, t] + twice(coef[r, t, 0:16, :]) * w[r - 1, t]
    side = across[r, t]
    mixed = slope[r + 1, t] - slope[r - 1, t]
    cross = coef[r, t, 48:64, :]
    inner = coef[r, t, 64:72, :]
    outer = coef[r, t, 72:80, :]
    outer_down = coef[r, t, 80:88, :]
    parts = []
    for c in range(2):
        mine = slice(16 * c, 16 * c + 16)
        other = slice(16 - 16 * c, 32 - 16 * c)
        low, high = here[16 * c : 16 * c + 8], here[16 * c + 8 : 16 * c + 16]
        column = jnp.concatenate(
            [inner * high + outer_down * pltpu.roll(high, 1, 0), inner * low + outer * pltpu.roll(low, 7, 0)], 0
        )
        if c == 0:
            lateral = 4.0 * along[mine] + side[mine]
        else:
            lateral = along[mine] + 4.0 * side[mine]
        parts.append(lateral + cross * mixed[other] + column)
    return here, jnp.concatenate(parts, 0)


def sweep(w, new, coef, scaled, slope, across, first, last, closed, unroll, tiles=None, emit=None):
    look, unroll, _ = unroll
    nt = w.shape[1]
    prepare(w, coef, slope, across, first - 1, last + 1, closed, look)

    def row(r):
        for t in range(nt if tiles is None else tiles):
            here, total = off_diagonal(w, coef, slope, across, r, t)
            value = (1.0 - OMEGA) * here + scaled[r, t] + coef[r, t, 88:120, :] * total
            if emit is None:
                new[r, t] = value
            else:
                emit(r, t, value)

    rows_loop(first, last, row, unroll)


def remainders(w, out, data, diag, coef, slope, across, first, last, unroll, tiles):
    look, unroll, _ = unroll
    prepare(w, coef, slope, across, first - 1, last + 1, False, look)

    def row(r):
        for t in range(tiles):
            here, total = off_diagonal(w, coef, slope, across, r, t)
            out[r, t] = data[r, t, 0:32, :] + data[r, t, 48:49, :] * total - diag[r, t] * here

    rows_loop(first, last, row, unroll)


def gather_lanes(v, index):
    return jnp.take_along_axis(v, index, axis=1, mode="promise_in_bounds")


def halve(first, second):
    lane = lax.broadcasted_iota(jnp.int32, first.shape, 1)
    even = (2 * lane) % LANES
    low = gather_lanes(first + pltpu.roll(first, LANES - 1, 1), even)
    if second is None:
        return low
    high = gather_lanes(second + pltpu.roll(second, LANES - 1, 1), even)
    return jnp.where(lane < LANES // 2, low, high)


def restrict_row(source, planes, r):
    both = [source[r, t, planes, :] + source[r + 1, t, planes, :] for t in range(min(2, source.shape[1]))]
    return 0.25 * halve(both[0], both[1] if len(both) > 1 else None)


def prolong_row(tiles, fine_tiles):
    lane = lax.broadcasted_iota(jnp.int32, tiles[0].shape, 1)
    low = lane // 2
    high = LANES // 2 + lane // 2
    first = tiles[0]
    last = tiles[-1]
    out = [gather_lanes(first, low)]
    if fine_tiles == 2:
        out.append(gather_lanes(first, high))
    else:
        out.append(gather_lanes(first, high))
        out.append(gather_lanes(last, jnp.where(lane < LANES // 2, low, high)))
    return out


def put(strip, v, shift, width, at):
    lane = lax.broadcasted_iota(jnp.int32, v.shape, 1)
    rolled = pltpu.roll(v, shift % LANES, 1) if shift % LANES else v
    return jnp.where((lane >= at) & (lane < at + width), rolled, strip)


def unpack_rim(left, right, at, width):
    lane = lax.broadcasted_iota(jnp.int32, left.shape, 1)
    to_low = pltpu.roll(right, (LANES - at) % LANES, 1) if at else right
    shift = (2 * LANES - width - at) % LANES
    to_high = pltpu.roll(left, shift, 1) if shift else left
    return jnp.where(lane < LANES // 2, to_low, to_high)


def arrange_kernel(misfit, viscosity, friction_in, ice_mask_in, grounded_in, data, strips,
                   misfit_half, viscosity_half, friction, ice_mask, grounded, sems):
    rows = friction.shape[0]
    copies = [
        pltpu.make_async_copy(source, target, sems.at[4 + n])
        for n, (source, target) in enumerate(((friction_in, friction), (ice_mask_in, ice_mask), (grounded_in, grounded)))
    ]
    for t in range(2):
        lanes = pl.ds(t * LANES, LANES)
        copies.append(pltpu.make_async_copy(misfit.at[:, lanes], misfit_half.at[t], sems.at[t]))
        copies.append(pltpu.make_async_copy(viscosity.at[:, lanes], viscosity_half.at[t], sems.at[2 + t]))
    for copy in copies:
        copy.start()
    for copy in copies:
        copy.wait()
    sub = lax.broadcasted_iota(jnp.int32, (8, LANES), 0)
    stride = 2 * rows

    def eight(i, carry):
        block = pl.ds(pl.multiple_of(8 * i, 8), 8)
        for t in range(2):
            lanes = pl.ds(t * LANES, LANES)
            ices = ice_mask[block, lanes].astype(F32)
            drags = friction[block, lanes] * grounded[block, lanes].astype(F32)
            for j in range(8):
                r = 8 * i + j
                ice, drag = ices[j : j + 1], drags[j : j + 1]
                for c in range(2):
                    for p in range(2):
                        v = misfit_half[t, pl.ds(c * 16 * rows + p * rows + r, 8, stride=stride), :]
                        data[r, t, 16 * c + 8 * p : 16 * c + 8 * p + 8, :] = v * ice
                for p in range(2):
                    data[r, t, 32 + 8 * p : 40 + 8 * p, :] = viscosity_half[t, pl.ds(p * rows + r, 8, stride=stride), :]
                data[r, t, 48:56, :] = jnp.where(sub == 0, ice, jnp.where(sub == 1, drag, 0.0))
        return carry

    lax.fori_loop(0, rows // 8, eight, 0)
    for side in range(2):
        for first in range(0, NP, 8):
            planes = slice(first, first + 8)
            strip = jnp.zeros((8, LANES), F32)
            for r in range(rows):
                at = r * RIM0
                strip = put(strip, data[r, side, planes, :], at if side == 0 else at + RIM0, RIM0, at)
            strips[side, planes, :] = strip


def down0_kernel(own, sent, from_low, from_high, coarse, strips1, wa, coef, scaled,
                 data, diag, slope, across):
    rows = own.shape[0]
    total = rows + 2 * RIM0

    def copy_row(r):
        for t in range(2):
            data[RIM0 + r, t] = own[r, t]

    rows_loop(0, rows, copy_row, 4)
    for r in range(rows):
        data[RIM0 + r, 2] = unpack_rim(sent[2 * RIM0], sent[2 * RIM0 + 1], r * RIM0, RIM0)
    for r in range(RIM0):
        for t in range(2):
            data[r, t] = from_low[2 * r + t]
            data[RIM0 + rows + r, t] = from_high[2 * r + t]
        low_at = (rows - RIM0 + r) * RIM0
        data[r, 2] = unpack_rim(from_low[2 * RIM0], from_low[2 * RIM0 + 1], low_at, RIM0)
        data[RIM0 + rows + r, 2] = unpack_rim(from_high[2 * RIM0], from_high[2 * RIM0 + 1], r * RIM0, RIM0)

    make_coefs(data, coef, scaled, diag, 1, total - 1, 1.0, False, UNROLL0[2])
    sweep(scaled, wa, coef, scaled, slope, across, 2, total - 2, False, UNROLL0)

    def coefs_row(i):
        coarse[i, 32:56, :] = restrict_row(data, slice(32, 56), RIM0 + 2 * i)

    rows_loop(0, rows // 2, coefs_row, UNROLL_MOVE)
    remainders(wa, diag, data, diag, coef, slope, across, RIM0, RIM0 + rows, UNROLL0, 2)

    def target_row(i):
        coarse[i, 0:32, :] = restrict_row(diag, slice(0, 32), RIM0 + 2 * i)

    rows_loop(0, rows // 2, target_row, UNROLL_MOVE)
    group = LANES // STRIP1
    for side in range(2):
        for part in range(rows // 2 // group):
            for first in range(0, NP, 8):
                planes = slice(first, first + 8)
                strip = jnp.zeros((8, LANES), F32)
                for j in range(group):
                    at = j * STRIP1
                    shift = at if side == 0 else at + STRIP1
                    strip = put(strip, coarse[part * group + j, planes, :], shift, STRIP1, at)
                strips1[side, part, planes, :] = strip


def down12_kernel(own, sent, from_low, from_high, piece, wa1, coef1, scaled1, wa2, coef2, scaled2,
                  data1, diag1, slope1, across1, data2, diag2, slope2, across2):
    rows = own.shape[0]
    total = rows + 2 * RIM1
    group = LANES // STRIP1
    parts = rows // group

    def rim(source, base, r):
        part, j = r // group, r % group
        return unpack_rim(source[base + part], source[base + parts + part], j * STRIP1, STRIP1)

    def copy_row(r):
        data1[RIM1 + r, 0] = own[r]

    rows_loop(0, rows, copy_row, 4)

    def copy_rim(r):
        data1[r, 0] = from_low[r]
        data1[RIM1 + rows + r, 0] = from_high[r]

    rows_loop(0, RIM1, copy_rim, 1)
    for r in range(rows):
        data1[RIM1 + r, 1] = rim(sent, RIM1, r)
    for r in range(RIM1):
        data1[r, 1] = rim(from_low, RIM1, rows - RIM1 + r)
        data1[RIM1 + rows + r, 1] = rim(from_high, RIM1, r)

    make_coefs(data1, coef1, scaled1, diag1, 1, total - 1, 0.25, False, UNROLL1[2])
    sweep(scaled1, wa1, coef1, scaled1, slope1, across1, 2, total - 2, False, UNROLL1)
    remainders(wa1, diag1, data1, diag1, coef1, slope1, across1, 3, total - 3, UNROLL1, 2)

    rows2 = rows // 2
    total2 = rows2 + 2 * RIM2

    def coefs_row(i):
        data2[i, 0, 32:56, :] = restrict_row(data1, slice(32, 56), 1 + 2 * i)

    rows_loop(0, total2, coefs_row, UNROLL_MOVE)

    def target_row(i):
        data2[i, 0, 0:32, :] = restrict_row(diag1, slice(0, 32), 1 + 2 * i)

    rows_loop(1, total2 - 1, target_row, UNROLL_MOVE)

    make_coefs(data2, coef2, scaled2, diag2, 1, total2 - 1, 0.0625, False, UNROLL2[2])
    sweep(scaled2, wa2, coef2, scaled2, slope2, across2, 2, total2 - 2, False, UNROLL2)
    remainders(wa2, diag2, data2, diag2, coef2, slope2, across2, RIM2, RIM2 + rows2, UNROLL2, 1)

    rows3 = rows2 // 2
    width = LANES // rows3
    for first in range(0, NP, 8):
        planes = slice(first, first + 8)
        source = diag2 if first < 32 else data2
        strip = jnp.zeros((8, LANES), F32)
        for i in range(rows3):
            strip = put(strip, restrict_row(source, planes, RIM2 + 2 * i), i * width, width, i * width)
        for d in range(piece.shape[0]):
            piece[d, planes, :] = strip


def coarse_kernel(place, pieces, correction, data3, coef3, scaled3, wa3, wb3, slope3, across3):
    devices_y, devices_x = pieces.shape[0], pieces.shape[1]
    rows3 = devices_y
    width = LANES // devices_y
    whole = devices_x * rows3
    zero = jnp.zeros((NP, LANES), F32)
    for r in range(RIM3):
        for end in (r, RIM3 + whole + r):
            data3[end, 0] = zero
            wa3[end, 0] = zero[:32]
            wb3[end, 0] = zero[:32]
            scaled3[end, 0] = zero[:32]
            slope3[end, 0] = zero[:32]
            coef3[end, 0, 0:16, :] = zero[:16]

    def assemble(d, carry):
        for i in range(rows3):
            line = jnp.zeros((NP, LANES), F32)
            for j in range(devices_y):
                line = put(line, pieces[j, d], (j - i) * width, width, j * width)
            data3[RIM3 + d * rows3 + i, 0] = line
        return carry

    lax.fori_loop(0, devices_x, assemble, 0)
    first, last = RIM3, RIM3 + whole
    make_coefs(data3, coef3, scaled3, None, first, last, 0.25 ** (LEVELS - 1), True, UNROLL3[2])

    def coarse_sweep(source, target):
        def look(r):
            norths, souths = shifted([source[r, 0]], True)
            slope3[r, 0] = norths[0] - souths[0]
            across3[r, 0] = twice(coef3[r, 0, 16:32, :]) * norths[0] + twice(coef3[r, 0, 32:48, :]) * souths[0]

        rows_loop(first, last, look, UNROLL3[0])

        def row(r):
            here, total = off_diagonal(source, coef3, slope3, across3, r, 0)
            target[r, 0] = (1.0 - OMEGA) * here + scaled3[r, 0] + coef3[r, 0, 88:120, :] * total

        rows_loop(first, last, row, UNROLL3[1])

    coarse_sweep(scaled3, wa3)

    def two_sweeps(i, carry):
        coarse_sweep(wa3, wb3)
        coarse_sweep(wb3, wa3)
        return carry

    lax.fori_loop(0, (COARSE_ITERS - 2) // 2, two_sweeps, 0)

    gx, gy, = place[0], place[1]
    lane = lane_ids(32)
    y = jnp.where(lane < 96, lane, lane - LANES)
    column = gy * width + (y + LANES) // 2 - LANES // 2
    inside = (column >= 0) & (column < LANES)
    pick = jnp.where(inside, column, 0)

    for i in range(rows3 + 2 * RIM3):
        line = wa3[gx * rows3 + i, 0]
        correction[i] = jnp.where(inside, gather_lanes(line, pick), 0.0)


def up_kernel(correction, w0, coef0, scaled0, w1, coef1, scaled1, w2, coef2, scaled2, result,
              wa2, wb2, wa1, wb1, wa0, wb0, slope0, across0, result_half, sems):
    slope1, across1 = (v.at[pl.ds(0, wa1.shape[0]), pl.ds(0, 2)] for v in (slope0, across0))
    slope2, across2 = (v.at[pl.ds(0, wa2.shape[0]), pl.ds(0, 1)] for v in (slope0, across0))
    rows2 = w2.shape[0] - 2 * RIM2
    for i in range(correction.shape[0]):
        for r in (2 * i + 2, 2 * i + 3):
            wa2[r, 0] = w2[r, 0] + correction[i]
    total2 = rows2 + 2 * RIM2
    sweep(wa2, wb2, coef2, scaled2, slope2, across2, 3, total2 - 3, False, UNROLL2)
    sweep(wb2, wa2, coef2, scaled2, slope2, across2, 4, total2 - 4, False, UNROLL2)


    def add1(r):
        adds = prolong_row([wa2[r, 0]], 2)
        for t in range(2):
            for fine in (2 * r + 1, 2 * r + 2):
                wa1[fine, t] = w1[fine, t] + adds[t]

    rows_loop(4, total2 - 4, add1, UNROLL_MOVE)
    total1 = 2 * rows2 + 2 * RIM1
    sweep(wa1, wb1, coef1, scaled1, slope1, across1, 11, total1 - 11, False, UNROLL1)
    sweep(wb1, wa1, coef1, scaled1, slope1, across1, 12, total1 - 12, False, UNROLL1)


    def add0(r):
        adds = prolong_row([wa1[r, t] for t in range(2)], 3)
        for t in range(3):
            for fine in (2 * r - 22, 2 * r - 21):
                wa0[fine, t] = w0[fine, t] + adds[t]

    rows_loop(12, total1 - 12, add0, UNROLL_MOVE)
    rows0 = 4 * rows2
    total0 = rows0 + 2 * RIM0
    sweep(wa0, wb0, coef0, scaled0, slope0, across0, 3, total0 - 3, False, UNROLL0)

    def emit(r, t, value):
        for c in range(2):
            for p in range(2):
                start = c * 16 * rows0 + p * rows0 + r - RIM0
                result_half[t, pl.ds(start, 8, stride=2 * rows0), :] = value[16 * c + 8 * p : 16 * c + 8 * p + 8]

    sweep(wb0, None, coef0, scaled0, slope0, across0, RIM0, RIM0 + rows0, False, UNROLL0, tiles=2, emit=emit)
    copies = [
        pltpu.make_async_copy(result_half.at[t], result.at[:, pl.ds(t * LANES, LANES)], sems.at[t]) for t in range(2)
    ]
    for copy in copies:
        copy.start()
    for copy in copies:
        copy.wait()


def shape(*dims):
    return jax.ShapeDtypeStruct(dims, F32)


def kept(*dims):
    return pltpu.VMEM(dims, F32)


def keep(arrays):
    return [pltpu.with_memory_space_constraint(v, pltpu.VMEM) for v in arrays]


VM = pl.BlockSpec(memory_space=pltpu.VMEM)
SM = pl.BlockSpec(memory_space=pltpu.SMEM)
HB = pl.BlockSpec(memory_space=pl.ANY)
PARAMS = pltpu.CompilerParams(vmem_limit_bytes=VMEM_DOWN)
UP_PARAMS = pltpu.CompilerParams(vmem_limit_bytes=VMEM_UP)


def buffers(rows, tiles, names):
    planes = {"data": NP, "coef": 8 * NC}
    return [pltpu.VMEM((rows, tiles, planes.get(name, 32), LANES), F32) for name in names]


def per_device(misfit, viscosity, friction, ice_mask, grounded):
    rows, columns = friction.shape
    gx, gy = lax.axis_index("gx"), lax.axis_index("gy")
    nx, ny = lax.axis_size("gx"), lax.axis_size("gy")
    upward = [(i, i + 1) for i in range(nx - 1)]
    downward = [(i + 1, i) for i in range(nx - 1)]

    def beside(strips):
        every = lax.all_gather(strips, "gy", axis=0)
        left = lax.dynamic_index_in_dim(every, jnp.maximum(gy - 1, 0), 0, keepdims=False)[1]
        right = lax.dynamic_index_in_dim(every, jnp.minimum(gy + 1, ny - 1), 0, keepdims=False)[0]
        return jnp.where(gy > 0, left, 0.0), jnp.where(gy < ny - 1, right, 0.0)

    data0, strips0 = pl.pallas_call(
        arrange_kernel,
        out_shape=(shape(rows, 2, NP, LANES), shape(2, NP, LANES)),
        in_specs=[HB] * 5,
        out_specs=(VM, VM),
        scratch_shapes=[
            pltpu.VMEM((2, 2 * 16 * rows, LANES), F32),
            pltpu.VMEM((2, 16 * rows, LANES), F32),
            pltpu.VMEM((rows, columns), F32),
            pltpu.VMEM((rows, columns), jnp.int32),
            pltpu.VMEM((rows, columns), jnp.int32),
            pltpu.SemaphoreType.DMA((7,)),
        ],
        compiler_params=PARAMS,
        name="arrange",
    )(
        *(
            pltpu.with_memory_space_constraint(v.reshape(-1, columns), pltpu.HBM)
            for v in (misfit, viscosity, friction, ice_mask, grounded)
        )
    )
    left, right = beside(strips0)
    rims = [left[None], right[None]]
    low_face = jnp.concatenate([data0[:RIM0].reshape(-1, NP, LANES)] + rims, 0)
    high_face = jnp.concatenate([data0[rows - RIM0 :].reshape(-1, NP, LANES)] + rims, 0)
    from_low = lax.ppermute(high_face, "gx", upward)
    from_high = lax.ppermute(low_face, "gx", downward)

    total0 = rows + 2 * RIM0
    names = ("data", "diag", "slope", "across")
    rows1 = rows // 2
    group = LANES // STRIP1
    field0 = kept(total0, 3, 32, LANES)
    data1, strips1, w0, coef0, scaled0 = pl.pallas_call(
        down0_kernel,
        out_shape=(
            shape(rows1, NP, LANES),
            shape(2, rows1 // group, NP, LANES),
            field0,
            kept(total0, 3, 8 * NC, LANES),
            field0,
        ),
        in_specs=[VM] * 4,
        out_specs=(VM,) * 5,
        scratch_shapes=buffers(total0, 3, names),
        compiler_params=PARAMS,
        name="down0",
    )(data0, low_face, from_low, from_high)

    left, right = beside(strips1)
    low_face = jnp.concatenate([data1[:RIM1], left, right], 0)
    high_face = jnp.concatenate([data1[rows1 - RIM1 :], left, right], 0)
    from_low = lax.ppermute(high_face, "gx", upward)
    from_high = lax.ppermute(low_face, "gx", downward)

    total1 = rows1 + 2 * RIM1
    rows2 = rows1 // 2
    total2 = rows2 + 2 * RIM2
    field1 = kept(total1, 2, 32, LANES)
    field2 = kept(total2, 1, 32, LANES)
    piece, w1, coef1, scaled1, w2, coef2, scaled2 = pl.pallas_call(
        down12_kernel,
        out_shape=(
            shape(nx, NP, LANES),
            field1,
            kept(total1, 2, 8 * NC, LANES),
            field1,
            field2,
            kept(total2, 1, 8 * NC, LANES),
            field2,
        ),
        in_specs=[VM] * 4,
        out_specs=(VM,) * 7,
        scratch_shapes=buffers(total1, 2, names) + buffers(total2, 1, names),
        compiler_params=PARAMS,
        name="down12",
    )(data1, low_face, from_low, from_high)

    pieces = lax.all_gather(lax.all_to_all(piece, "gx", 0, 0), "gy", axis=0)

    rows3 = rows2 // 2
    total3 = nx * rows3 + 2 * RIM3
    ups = ("w", "w")
    correction = pl.pallas_call(
        coarse_kernel,
        out_shape=shape(rows3 + 2 * RIM3, 32, LANES),
        in_specs=[SM, VM],
        out_specs=VM,
        scratch_shapes=buffers(total3, 1, ("data", "coef", "scaled", "w", "w", "slope", "across")),
        compiler_params=pltpu.CompilerParams(vmem_limit_bytes=VMEM_COARSE + VMEM_COARSE_ROW * total3),
        name="coarse",
    )(jnp.stack([gx, gy]).astype(jnp.int32), pieces)
    result = pl.pallas_call(
        up_kernel,
        out_shape=shape(2 * 16 * rows, columns),
        in_specs=[VM] * 10,
        out_specs=HB,
        scratch_shapes=buffers(total2, 1, ups)
        + buffers(total1, 2, ups)
        + buffers(total0, 3, ups)
        + buffers(max(total0, total1), 3, ("slope", "across"))
        + [pltpu.VMEM((2, 2 * 16 * rows, LANES), F32), pltpu.SemaphoreType.DMA((2,))],
        compiler_params=UP_PARAMS,
        name="up",
    )(
        correction,
        *keep([w0, coef0, scaled0, w1, coef1, scaled1, w2, coef2, scaled2]),
    )
    return result.reshape(misfit.shape)


def solution(mesh):
    placed = (
        P(None, None, "gx", "gy"),
        P(None, "gx", "gy"),
        P("gx", "gy"),
        P("gx", "gy"),
        P("gx", "gy"),
    )
    return jax.shard_map(
        per_device, mesh=mesh, in_specs=placed, out_specs=P(None, None, "gx", "gy"), check_vma=False
    )
```

```python
import functools

import jax
import jax.numpy as jnp
from jax import lax
from jax.experimental import pallas as pl
from jax.experimental.pallas import tpu as pltpu
from jax.sharding import PartitionSpec as P

LEVELS = 4
COARSE_ITERS = 20
OMEGA = 0.6
CROSS = 0.75
NP = 56
LANES = 128
RIM0 = 4
RIM1 = 13
RIM2 = 6
RIM3 = 2
STRIP1 = 16
NC = 15
VMEM_DOWN = 28 * 1024 * 1024
VMEM_UP = 60 * 1024 * 1024
F32 = jnp.float32
UNROLL0 = (18, 6, 4)
UNROLL1 = (18, 6, 4)
UNROLL2 = (18, 6, 4)
UNROLL3 = (32, 32, 2)
UNROLL_MOVE = 8


def rows_loop(first, last, body, unroll):
    count = (last - first) // unroll

    def step(i, carry):
        for j in range(unroll):
            body(first + i * unroll + j)
        return carry

    if count:
        lax.fori_loop(0, count, step, 0)
    for r in range(first + count * unroll, last):
        body(r)


def lane_ids(rows=8):
    return lax.broadcasted_iota(jnp.int32, (rows, LANES), 1)


def shifted(tiles, closed):
    lane = lax.broadcasted_iota(jnp.int32, tiles[0].shape, 1)
    up = [pltpu.roll(v, LANES - 1, 1) for v in tiles]
    down = [pltpu.roll(v, 1, 1) for v in tiles]
    n = len(tiles)
    if closed:
        zero = jnp.zeros_like(tiles[0])
        return (
            [jnp.where(lane == LANES - 1, zero, v) for v in up],
            [jnp.where(lane == 0, zero, v) for v in down],
        )
    if n == 1:
        return up, down
    return (
        [jnp.where(lane == LANES - 1, up[(t + 1) % n], up[t]) for t in range(n)],
        [jnp.where(lane == 0, down[(t - 1) % n], down[t]) for t in range(n)],
    )


def twice(v):
    return jnp.concatenate([v, v], 0)


def make_coefs(data, coef, scaled, diag, first, last, horizontal, closed, unroll):
    nt = data.shape[1]
    sub = lax.broadcasted_iota(jnp.int32, (8, LANES), 0)

    def row(r):
        mids = [data[r, t, 32:48, :] for t in range(nt)]
        norths, souths = shifted(mids, closed)
        for t in range(nt):
            mid = mids[t]
            west = (0.5 * horizontal) * (mid + data[r - 1, t, 32:48, :])
            east = (0.5 * horizontal) * (mid + data[r + 1, t, 32:48, :])
            north = (0.5 * horizontal) * (mid + norths[t])
            south = (0.5 * horizontal) * (mid + souths[t])
            low, high = mid[:8], mid[8:]
            inner = 2.0 * (low + high)
            outer = jnp.where(sub == 7, 0.0, 2.0 * (high + pltpu.roll(low, 7, 0)))
            outer_down = pltpu.roll(outer, 1, 0)
            coef[r, t, 0:16, :] = west
            coef[r, t, 16:32, :] = north
            coef[r, t, 32:48, :] = south
            coef[r, t, 48:64, :] = (CROSS * horizontal) * mid
            coef[r, t, 64:72, :] = inner
            coef[r, t, 72:80, :] = outer
            coef[r, t, 80:88, :] = outer_down
            ice = data[r, t, 48:49, :]
            drag = data[r, t, 49:50, :]
            bottom = jnp.where(sub == 0, drag, 0.0)
            upright = jnp.concatenate([inner + outer_down + bottom, inner + outer], 0)
            along_x = east + west
            along_y = north + south
            rest = 1.0 - ice
            for c, lateral in enumerate((4.0 * along_x + along_y, along_x + 4.0 * along_y)):
                diagonal = ice * (lateral + upright) + rest
                inverse = OMEGA / diagonal
                coef[r, t, 88 + 16 * c : 104 + 16 * c, :] = ice * inverse
                scaled[r, t, 16 * c : 16 * c + 16, :] = inverse * data[r, t, 16 * c : 16 * c + 16, :]
                if diag is not None:
                    diag[r, t, 16 * c : 16 * c + 16, :] = diagonal

    rows_loop(first, last, row, unroll)


def prepare(w, coef, slope, across, first, last, closed, unroll):
    nt = w.shape[1]

    def row(r):
        norths, souths = shifted([w[r, t] for t in range(nt)], closed)
        for t in range(nt):
            slope[r, t] = norths[t] - souths[t]
            across[r, t] = twice(coef[r, t, 16:32, :]) * norths[t] + twice(coef[r, t, 32:48, :]) * souths[t]

    rows_loop(first, last, row, unroll)


def off_diagonal(w, coef, slope, across, r, t):
    here = w[r, t]
    along = twice(coef[r + 1, t, 0:16, :]) * w[r + 1, t] + twice(coef[r, t, 0:16, :]) * w[r - 1, t]
    side = across[r, t]
    mixed = slope[r + 1, t] - slope[r - 1, t]
    cross = coef[r, t, 48:64, :]
    inner = coef[r, t, 64:72, :]
    outer = coef[r, t, 72:80, :]
    outer_down = coef[r, t, 80:88, :]
    parts = []
    for c in range(2):
        mine = slice(16 * c, 16 * c + 16)
        other = slice(16 - 16 * c, 32 - 16 * c)
        low, high = here[16 * c : 16 * c + 8], here[16 * c + 8 : 16 * c + 16]
        column = jnp.concatenate(
            [inner * high + outer_down * pltpu.roll(high, 1, 0), inner * low + outer * pltpu.roll(low, 7, 0)], 0
        )
        if c == 0:
            lateral = 4.0 * along[mine] + side[mine]
        else:
            lateral = along[mine] + 4.0 * side[mine]
        parts.append(lateral + cross * mixed[other] + column)
    return here, jnp.concatenate(parts, 0)


def sweep(w, new, coef, scaled, slope, across, first, last, closed, unroll, tiles=None, emit=None):
    look, unroll, _ = unroll
    nt = w.shape[1]
    prepare(w, coef, slope, across, first - 1, last + 1, closed, look)

    def row(r):
        for t in range(nt if tiles is None else tiles):
            here, total = off_diagonal(w, coef, slope, across, r, t)
            value = (1.0 - OMEGA) * here + scaled[r, t] + coef[r, t, 88:120, :] * total
            if emit is None:
                new[r, t] = value
            else:
                emit(r, t, value)

    rows_loop(first, last, row, unroll)


def remainders(w, out, data, diag, coef, slope, across, first, last, unroll, tiles):
    look, unroll, _ = unroll
    prepare(w, coef, slope, across, first - 1, last + 1, False, look)

    def row(r):
        for t in range(tiles):
            here, total = off_diagonal(w, coef, slope, across, r, t)
            out[r, t] = data[r, t, 0:32, :] + data[r, t, 48:49, :] * total - diag[r, t] * here

    rows_loop(first, last, row, unroll)


def gather_lanes(v, index):
    return jnp.take_along_axis(v, index, axis=1, mode="promise_in_bounds")


def halve(first, second):
    lane = lax.broadcasted_iota(jnp.int32, first.shape, 1)
    even = (2 * lane) % LANES
    low = gather_lanes(first + pltpu.roll(first, LANES - 1, 1), even)
    if second is None:
        return low
    high = gather_lanes(second + pltpu.roll(second, LANES - 1, 1), even)
    return jnp.where(lane < LANES // 2, low, high)


def restrict_row(source, planes, r):
    both = [source[r, t, planes, :] + source[r + 1, t, planes, :] for t in range(min(2, source.shape[1]))]
    return 0.25 * halve(both[0], both[1] if len(both) > 1 else None)


def prolong_row(tiles, fine_tiles):
    lane = lax.broadcasted_iota(jnp.int32, tiles[0].shape, 1)
    low = lane // 2
    high = LANES // 2 + lane // 2
    first = tiles[0]
    last = tiles[-1]
    out = [gather_lanes(first, low)]
    if fine_tiles == 2:
        out.append(gather_lanes(first, high))
    else:
        out.append(gather_lanes(first, high))
        out.append(gather_lanes(last, jnp.where(lane < LANES // 2, low, high)))
    return out


def put(strip, v, shift, width, at):
    lane = lax.broadcasted_iota(jnp.int32, v.shape, 1)
    rolled = pltpu.roll(v, shift % LANES, 1) if shift % LANES else v
    return jnp.where((lane >= at) & (lane < at + width), rolled, strip)


def unpack_rim(left, right, at, width):
    lane = lax.broadcasted_iota(jnp.int32, left.shape, 1)
    to_low = pltpu.roll(right, (LANES - at) % LANES, 1) if at else right
    shift = (2 * LANES - width - at) % LANES
    to_high = pltpu.roll(left, shift, 1) if shift else left
    return jnp.where(lane < LANES // 2, to_low, to_high)


def copy_rows(source, target, sem, first, last):
    rows = pl.ds(first, last - first)
    copy = pltpu.make_async_copy(source.at[rows], target.at[rows], sem)
    copy.start()
    return copy


def arrange_kernel(misfit, viscosity, friction_in, ice_mask_in, grounded_in, data, strips,
                   misfit_half, viscosity_half, friction, ice_mask, grounded, sems):
    rows = friction.shape[0]
    copies = [
        pltpu.make_async_copy(source, target, sems.at[4 + n])
        for n, (source, target) in enumerate(((friction_in, friction), (ice_mask_in, ice_mask), (grounded_in, grounded)))
    ]
    for t in range(2):
        lanes = pl.ds(t * LANES, LANES)
        copies.append(pltpu.make_async_copy(misfit.at[:, lanes], misfit_half.at[t], sems.at[t]))
        copies.append(pltpu.make_async_copy(viscosity.at[:, lanes], viscosity_half.at[t], sems.at[2 + t]))
    for copy in copies:
        copy.start()
    for copy in copies:
        copy.wait()
    sub = lax.broadcasted_iota(jnp.int32, (8, LANES), 0)
    stride = 2 * rows

    def eight(i, carry):
        block = pl.ds(pl.multiple_of(8 * i, 8), 8)
        for t in range(2):
            lanes = pl.ds(t * LANES, LANES)
            ices = ice_mask[block, lanes].astype(F32)
            drags = friction[block, lanes] * grounded[block, lanes].astype(F32)
            for j in range(8):
                r = 8 * i + j
                ice, drag = ices[j : j + 1], drags[j : j + 1]
                for c in range(2):
                    for p in range(2):
                        v = misfit_half[t, pl.ds(c * 16 * rows + p * rows + r, 8, stride=stride), :]
                        data[r, t, 16 * c + 8 * p : 16 * c + 8 * p + 8, :] = v * ice
                for p in range(2):
                    data[r, t, 32 + 8 * p : 40 + 8 * p, :] = viscosity_half[t, pl.ds(p * rows + r, 8, stride=stride), :]
                data[r, t, 48:56, :] = jnp.where(sub == 0, ice, jnp.where(sub == 1, drag, 0.0))
        return carry

    lax.fori_loop(0, rows // 8, eight, 0)
    for side in range(2):
        for first in range(0, NP, 8):
            planes = slice(first, first + 8)
            strip = jnp.zeros((8, LANES), F32)
            for r in range(rows):
                at = r * RIM0
                strip = put(strip, data[r, side, planes, :], at if side == 0 else at + RIM0, RIM0, at)
            strips[side, planes, :] = strip


def down0_kernel(own, sent, from_low, from_high, coarse, strips1, w_out, coef_out, scaled_out,
                 data, diag, slope, across, wa, coef, scaled, sems):
    rows = own.shape[0]
    total = rows + 2 * RIM0

    def copy_row(r):
        for t in range(2):
            data[RIM0 + r, t] = own[r, t]

    rows_loop(0, rows, copy_row, 4)
    for r in range(rows):
        data[RIM0 + r, 2] = unpack_rim(sent[2 * RIM0], sent[2 * RIM0 + 1], r * RIM0, RIM0)
    for r in range(RIM0):
        for t in range(2):
            data[r, t] = from_low[2 * r + t]
            data[RIM0 + rows + r, t] = from_high[2 * r + t]
        low_at = (rows - RIM0 + r) * RIM0
        data[r, 2] = unpack_rim(from_low[2 * RIM0], from_low[2 * RIM0 + 1], low_at, RIM0)
        data[RIM0 + rows + r, 2] = unpack_rim(from_high[2 * RIM0], from_high[2 * RIM0 + 1], r * RIM0, RIM0)

    half = total // 2 + 1
    make_coefs(data, coef, scaled, diag, 1, half, 1.0, False, UNROLL0[2])
    copies = [copy_rows(coef, coef_out, sems.at[0], 2, half)]
    make_coefs(data, coef, scaled, diag, half, total - 1, 1.0, False, UNROLL0[2])
    copies.append(copy_rows(coef, coef_out, sems.at[1], half, total - 2))
    copies.append(copy_rows(scaled, scaled_out, sems.at[2], 3, total - 3))
    sweep(scaled, wa, coef, scaled, slope, across, 2, total - 2, False, UNROLL0)
    copies.append(copy_rows(wa, w_out, sems.at[3], 2, total - 2))

    def coefs_row(i):
        coarse[i, 32:56, :] = restrict_row(data, slice(32, 56), RIM0 + 2 * i)

    rows_loop(0, rows // 2, coefs_row, UNROLL_MOVE)
    remainders(wa, diag, data, diag, coef, slope, across, RIM0, RIM0 + rows, UNROLL0, 2)

    def target_row(i):
        coarse[i, 0:32, :] = restrict_row(diag, slice(0, 32), RIM0 + 2 * i)

    rows_loop(0, rows // 2, target_row, UNROLL_MOVE)
    group = LANES // STRIP1
    for side in range(2):
        for part in range(rows // 2 // group):
            for first in range(0, NP, 8):
                planes = slice(first, first + 8)
                strip = jnp.zeros((8, LANES), F32)
                for j in range(group):
                    at = j * STRIP1
                    shift = at if side == 0 else at + STRIP1
                    strip = put(strip, coarse[part * group + j, planes, :], shift, STRIP1, at)
                strips1[side, part, planes, :] = strip
    for copy in copies:
        copy.wait()


def down12_kernel(own, sent, from_low, from_high, piece, w1_out, coef1_out, scaled1_out, w2_out, coef2_out, scaled2_out,
                  data1, diag1, slope1, across1, wa1, coef1, scaled1, data2, diag2, slope2, across2, wa2, coef2, scaled2, sems):
    rows = own.shape[0]
    total = rows + 2 * RIM1
    group = LANES // STRIP1
    parts = rows // group

    def rim(source, base, r):
        part, j = r // group, r % group
        return unpack_rim(source[base + part], source[base + parts + part], j * STRIP1, STRIP1)

    def copy_row(r):
        data1[RIM1 + r, 0] = own[r]

    rows_loop(0, rows, copy_row, 4)

    def copy_rim(r):
        data1[r, 0] = from_low[r]
        data1[RIM1 + rows + r, 0] = from_high[r]

    rows_loop(0, RIM1, copy_rim, 1)
    for r in range(rows):
        data1[RIM1 + r, 1] = rim(sent, RIM1, r)
    for r in range(RIM1):
        data1[r, 1] = rim(from_low, RIM1, rows - RIM1 + r)
        data1[RIM1 + rows + r, 1] = rim(from_high, RIM1, r)

    make_coefs(data1, coef1, scaled1, diag1, 1, total - 1, 0.25, False, UNROLL1[2])
    copies = [copy_rows(coef1, coef1_out, sems.at[0], 10, total - 10)]
    copies.append(copy_rows(scaled1, scaled1_out, sems.at[1], 11, total - 11))
    sweep(scaled1, wa1, coef1, scaled1, slope1, across1, 2, total - 2, False, UNROLL1)
    copies.append(copy_rows(wa1, w1_out, sems.at[2], 9, total - 9))
    remainders(wa1, diag1, data1, diag1, coef1, slope1, across1, 3, total - 3, UNROLL1, 2)

    rows2 = rows // 2
    total2 = rows2 + 2 * RIM2

    def coefs_row(i):
        data2[i, 0, 32:56, :] = restrict_row(data1, slice(32, 56), 1 + 2 * i)

    rows_loop(0, total2, coefs_row, UNROLL_MOVE)

    def target_row(i):
        data2[i, 0, 0:32, :] = restrict_row(diag1, slice(0, 32), 1 + 2 * i)

    rows_loop(1, total2 - 1, target_row, UNROLL_MOVE)

    make_coefs(data2, coef2, scaled2, diag2, 1, total2 - 1, 0.0625, False, UNROLL2[2])
    copies.append(copy_rows(coef2, coef2_out, sems.at[3], 2, total2 - 2))
    copies.append(copy_rows(scaled2, scaled2_out, sems.at[4], 3, total2 - 3))
    sweep(scaled2, wa2, coef2, scaled2, slope2, across2, 2, total2 - 2, False, UNROLL2)
    copies.append(copy_rows(wa2, w2_out, sems.at[5], 2, total2 - 2))
    remainders(wa2, diag2, data2, diag2, coef2, slope2, across2, RIM2, RIM2 + rows2, UNROLL2, 1)

    rows3 = rows2 // 2
    width = LANES // rows3
    for first in range(0, NP, 8):
        planes = slice(first, first + 8)
        source = diag2 if first < 32 else data2
        strip = jnp.zeros((8, LANES), F32)
        for i in range(rows3):
            strip = put(strip, restrict_row(source, planes, RIM2 + 2 * i), i * width, width, i * width)
        for d in range(piece.shape[0]):
            piece[d, planes, :] = strip
    for copy in copies:
        copy.wait()


def up_kernel(place, pieces, w0_in, coef0_in, scaled0_in, w1_in, coef1_in, scaled1_in, w2_in, coef2_in, scaled2_in, result,
              data3, coef3, scaled3, wa3, wb3, slope3, across3, w2, coef2, scaled2, wa2, wb2, w1, coef1, scaled1, wa1, wb1,
              w0, coef0, scaled0, wa0, wb0, slope0, across0, result_half, sems):
    slope1, across1 = (v.at[pl.ds(0, wa1.shape[0]), pl.ds(0, 2)] for v in (slope0, across0))
    slope2, across2 = (v.at[pl.ds(0, wa2.shape[0]), pl.ds(0, 1)] for v in (slope0, across0))
    copies = []
    for source, target, first in (
        (w2_in, w2, 2), (coef2_in, coef2, 2), (scaled2_in, scaled2, 3),
        (w1_in, w1, 9), (coef1_in, coef1, 10), (scaled1_in, scaled1, 11),
        (w0_in, w0, 2), (coef0_in, coef0, 2), (scaled0_in, scaled0, 3),
    ):
        copies.append(copy_rows(source, target, sems.at[len(copies)], first, source.shape[0] - first))
    devices_y, devices_x = pieces.shape[0], pieces.shape[1]
    rows3 = devices_y
    width = LANES // devices_y
    whole = devices_x * rows3
    zero = jnp.zeros((NP, LANES), F32)
    for r in range(RIM3):
        for end in (r, RIM3 + whole + r):
            data3[end, 0] = zero
            wa3[end, 0] = zero[:32]
            wb3[end, 0] = zero[:32]
            scaled3[end, 0] = zero[:32]
            slope3[end, 0] = zero[:32]
            coef3[end, 0, 0:16, :] = zero[:16]

    def assemble(d, carry):
        for i in range(rows3):
            line = jnp.zeros((NP, LANES), F32)
            for j in range(devices_y):
                line = put(line, pieces[j, d], (j - i) * width, width, j * width)
            data3[RIM3 + d * rows3 + i, 0] = line
        return carry

    lax.fori_loop(0, devices_x, assemble, 0)
    first, last = RIM3, RIM3 + whole
    make_coefs(data3, coef3, scaled3, None, first, last, 0.25 ** (LEVELS - 1), True, UNROLL3[2])

    def coarse_sweep(source, target):
        def look(r):
            norths, souths = shifted([source[r, 0]], True)
            slope3[r, 0] = norths[0] - souths[0]
            across3[r, 0] = twice(coef3[r, 0, 16:32, :]) * norths[0] + twice(coef3[r, 0, 32:48, :]) * souths[0]

        rows_loop(first, last, look, UNROLL3[0])

        def row(r):
            here, total = off_diagonal(source, coef3, slope3, across3, r, 0)
            target[r, 0] = (1.0 - OMEGA) * here + scaled3[r, 0] + coef3[r, 0, 88:120, :] * total

        rows_loop(first, last, row, UNROLL3[1])

    coarse_sweep(scaled3, wa3)

    def two_sweeps(i, carry):
        coarse_sweep(wa3, wb3)
        coarse_sweep(wb3, wa3)
        return carry

    lax.fori_loop(0, (COARSE_ITERS - 2) // 2, two_sweeps, 0)

    gx, gy, = place[0], place[1]
    lane = lane_ids(32)
    y = jnp.where(lane < 96, lane, lane - LANES)
    column = gy * width + (y + LANES) // 2 - LANES // 2
    inside = (column >= 0) & (column < LANES)
    pick = jnp.where(inside, column, 0)

    for copy in copies[:3]:
        copy.wait()
    rows2 = 2 * rows3
    for i in range(rows3 + 2 * RIM3):
        add = jnp.where(inside, gather_lanes(wa3[gx * rows3 + i, 0], pick), 0.0)
        for r in (2 * i + 2, 2 * i + 3):
            wa2[r, 0] = w2[r, 0] + add
    total2 = rows2 + 2 * RIM2
    sweep(wa2, wb2, coef2, scaled2, slope2, across2, 3, total2 - 3, False, UNROLL2)
    sweep(wb2, wa2, coef2, scaled2, slope2, across2, 4, total2 - 4, False, UNROLL2)


    for copy in copies[3:6]:
        copy.wait()

    def add1(r):
        adds = prolong_row([wa2[r, 0]], 2)
        for t in range(2):
            for fine in (2 * r + 1, 2 * r + 2):
                wa1[fine, t] = w1[fine, t] + adds[t]

    rows_loop(4, total2 - 4, add1, UNROLL_MOVE)
    total1 = 2 * rows2 + 2 * RIM1
    sweep(wa1, wb1, coef1, scaled1, slope1, across1, 11, total1 - 11, False, UNROLL1)
    sweep(wb1, wa1, coef1, scaled1, slope1, across1, 12, total1 - 12, False, UNROLL1)


    for copy in copies[6:]:
        copy.wait()

    def add0(r):
        adds = prolong_row([wa1[r, t] for t in range(2)], 3)
        for t in range(3):
            for fine in (2 * r - 22, 2 * r - 21):
                wa0[fine, t] = w0[fine, t] + adds[t]

    rows_loop(12, total1 - 12, add0, UNROLL_MOVE)
    rows0 = 4 * rows2
    total0 = rows0 + 2 * RIM0
    sweep(wa0, wb0, coef0, scaled0, slope0, across0, 3, total0 - 3, False, UNROLL0)

    def emit(r, t, value):
        for c in range(2):
            for p in range(2):
                start = c * 16 * rows0 + p * rows0 + r - RIM0
                result_half[t, pl.ds(start, 8, stride=2 * rows0), :] = value[16 * c + 8 * p : 16 * c + 8 * p + 8]

    sweep(wb0, None, coef0, scaled0, slope0, across0, RIM0, RIM0 + rows0, False, UNROLL0, tiles=2, emit=emit)
    copies = [
        pltpu.make_async_copy(result_half.at[t], result.at[:, pl.ds(t * LANES, LANES)], sems.at[t]) for t in range(2)
    ]
    for copy in copies:
        copy.start()
    for copy in copies:
        copy.wait()


def shape(*dims):
    return jax.ShapeDtypeStruct(dims, F32)


def stored(*dims):
    return pltpu.HBM(dims, F32)


def in_hbm(arrays):
    return [pltpu.with_memory_space_constraint(v, pltpu.HBM) for v in arrays]


VM = pl.BlockSpec(memory_space=pltpu.VMEM)
SM = pl.BlockSpec(memory_space=pltpu.SMEM)
HB = pl.BlockSpec(memory_space=pl.ANY)
PARAMS = pltpu.CompilerParams(vmem_limit_bytes=VMEM_DOWN)


def buffers(rows, tiles, names):
    planes = {"data": NP, "coef": 8 * NC}
    return [pltpu.VMEM((rows, tiles, planes.get(name, 32), LANES), F32) for name in names]


def per_device(misfit, viscosity, friction, ice_mask, grounded):
    rows, columns = friction.shape
    gx, gy = lax.axis_index("gx"), lax.axis_index("gy")
    nx, ny = lax.axis_size("gx"), lax.axis_size("gy")
    upward = [(i, i + 1) for i in range(nx - 1)]
    downward = [(i + 1, i) for i in range(nx - 1)]

    def beside(strips):
        every = lax.all_gather(strips, "gy", axis=0)
        left = lax.dynamic_index_in_dim(every, jnp.maximum(gy - 1, 0), 0, keepdims=False)[1]
        right = lax.dynamic_index_in_dim(every, jnp.minimum(gy + 1, ny - 1), 0, keepdims=False)[0]
        return jnp.where(gy > 0, left, 0.0), jnp.where(gy < ny - 1, right, 0.0)

    data0, strips0 = pl.pallas_call(
        arrange_kernel,
        out_shape=(shape(rows, 2, NP, LANES), shape(2, NP, LANES)),
        in_specs=[HB] * 5,
        out_specs=(VM, VM),
        scratch_shapes=[
            pltpu.VMEM((2, 2 * 16 * rows, LANES), F32),
            pltpu.VMEM((2, 16 * rows, LANES), F32),
            pltpu.VMEM((rows, columns), F32),
            pltpu.VMEM((rows, columns), jnp.int32),
            pltpu.VMEM((rows, columns), jnp.int32),
            pltpu.SemaphoreType.DMA((7,)),
        ],
        compiler_params=PARAMS,
        name="arrange",
    )(
        *in_hbm(v.reshape(-1, columns) for v in (misfit, viscosity, friction, ice_mask, grounded))
    )
    left, right = beside(strips0)
    rims = [left[None], right[None]]
    low_face = jnp.concatenate([data0[:RIM0].reshape(-1, NP, LANES)] + rims, 0)
    high_face = jnp.concatenate([data0[rows - RIM0 :].reshape(-1, NP, LANES)] + rims, 0)
    from_low = lax.ppermute(high_face, "gx", upward)
    from_high = lax.ppermute(low_face, "gx", downward)

    total0 = rows + 2 * RIM0
    names = ("data", "diag", "slope", "across", "w", "coef", "scaled")
    rows1 = rows // 2
    group = LANES // STRIP1
    field0 = stored(total0, 3, 32, LANES)
    data1, strips1, w0, coef0, scaled0 = pl.pallas_call(
        down0_kernel,
        out_shape=(
            shape(rows1, NP, LANES),
            shape(2, rows1 // group, NP, LANES),
            field0,
            stored(total0, 3, 8 * NC, LANES),
            field0,
        ),
        in_specs=[VM] * 4,
        out_specs=(VM, VM, HB, HB, HB),
        scratch_shapes=buffers(total0, 3, names) + [pltpu.SemaphoreType.DMA((4,))],
        compiler_params=PARAMS,
        name="down0",
    )(data0, low_face, from_low, from_high)

    left, right = beside(strips1)
    low_face = jnp.concatenate([data1[:RIM1], left, right], 0)
    high_face = jnp.concatenate([data1[rows1 - RIM1 :], left, right], 0)
    from_low = lax.ppermute(high_face, "gx", upward)
    from_high = lax.ppermute(low_face, "gx", downward)

    total1 = rows1 + 2 * RIM1
    rows2 = rows1 // 2
    total2 = rows2 + 2 * RIM2
    field1 = stored(total1, 2, 32, LANES)
    field2 = stored(total2, 1, 32, LANES)
    piece, w1, coef1, scaled1, w2, coef2, scaled2 = pl.pallas_call(
        down12_kernel,
        out_shape=(
            shape(nx, NP, LANES),
            field1,
            stored(total1, 2, 8 * NC, LANES),
            field1,
            field2,
            stored(total2, 1, 8 * NC, LANES),
            field2,
        ),
        in_specs=[VM] * 4,
        out_specs=(VM,) + (HB,) * 6,
        scratch_shapes=buffers(total1, 2, names) + buffers(total2, 1, names) + [pltpu.SemaphoreType.DMA((6,))],
        compiler_params=PARAMS,
        name="down12",
    )(data1, low_face, from_low, from_high)

    pieces = lax.all_gather(lax.all_to_all(piece, "gx", 0, 0), "gy", axis=0)

    rows3 = rows2 // 2
    total3 = nx * rows3 + 2 * RIM3
    ups = ("w", "coef", "scaled", "w", "w")
    result = pl.pallas_call(
        up_kernel,
        out_shape=shape(2 * 16 * rows, columns),
        in_specs=[SM, VM] + [HB] * 9,
        out_specs=HB,
        scratch_shapes=buffers(total3, 1, ("data", "coef", "scaled", "w", "w", "slope", "across"))
        + buffers(total2, 1, ups)
        + buffers(total1, 2, ups)
        + buffers(total0, 3, ups)
        + buffers(max(total0, total1), 3, ("slope", "across"))
        + [pltpu.VMEM((2, 2 * 16 * rows, LANES), F32), pltpu.SemaphoreType.DMA((9,))],
        compiler_params=pltpu.CompilerParams(vmem_limit_bytes=VMEM_UP),
        name="up",
    )(
        jnp.stack([gx, gy]).astype(jnp.int32),
        pieces,
        *in_hbm([w0, coef0, scaled0, w1, coef1, scaled1, w2, coef2, scaled2]),
    )
    return result.reshape(misfit.shape)


def solution(mesh):
    placed = (
        P(None, None, "gx", "gy"),
        P(None, "gx", "gy"),
        P("gx", "gy"),
        P("gx", "gy"),
        P("gx", "gy"),
    )
    return jax.shard_map(
        per_device, mesh=mesh, in_specs=placed, out_specs=P(None, None, "gx", "gy"), check_vma=False
    )
```

```python
import functools

import jax
import jax.numpy as jnp
from jax import lax
from jax.experimental import pallas as pl
from jax.experimental.pallas import tpu as pltpu
from jax.sharding import PartitionSpec as P

LEVELS = 4
COARSE_ITERS = 20
OMEGA = 0.6
CROSS = 0.75
NP = 56
LANES = 128
RIM0 = 4
RIM1 = 13
RIM2 = 6
RIM3 = 2
STRIP1 = 16
NC = 15
VMEM_DOWN = 28 * 1024 * 1024
VMEM_UP = 60 * 1024 * 1024
F32 = jnp.float32
UNROLL0 = (18, 6, 4)
UNROLL1 = (18, 6, 4)
UNROLL2 = (18, 6, 4)
UNROLL3 = (32, 32, 2)
UNROLL_MOVE = 8


def rows_loop(first, last, body, unroll):
    count = (last - first) // unroll

    def step(i, carry):
        for j in range(unroll):
            body(first + i * unroll + j)
        return carry

    if count:
        lax.fori_loop(0, count, step, 0)
    for r in range(first + count * unroll, last):
        body(r)


def lane_ids(rows=8):
    return lax.broadcasted_iota(jnp.int32, (rows, LANES), 1)


def shifted(tiles, closed):
    lane = lax.broadcasted_iota(jnp.int32, tiles[0].shape, 1)
    up = [pltpu.roll(v, LANES - 1, 1) for v in tiles]
    down = [pltpu.roll(v, 1, 1) for v in tiles]
    n = len(tiles)
    if closed:
        zero = jnp.zeros_like(tiles[0])
        return (
            [jnp.where(lane == LANES - 1, zero, v) for v in up],
            [jnp.where(lane == 0, zero, v) for v in down],
        )
    if n == 1:
        return up, down
    return (
        [jnp.where(lane == LANES - 1, up[(t + 1) % n], up[t]) for t in range(n)],
        [jnp.where(lane == 0, down[(t - 1) % n], down[t]) for t in range(n)],
    )


def twice(v):
    return jnp.concatenate([v, v], 0)


def make_coefs(data, coef, scaled, diag, first, last, horizontal, closed, unroll):
    nt = data.shape[1]
    sub = lax.broadcasted_iota(jnp.int32, (8, LANES), 0)

    def row(r):
        mids = [data[r, t, 32:48, :] for t in range(nt)]
        norths, souths = shifted(mids, closed)
        for t in range(nt):
            mid = mids[t]
            west = (0.5 * horizontal) * (mid + data[r - 1, t, 32:48, :])
            east = (0.5 * horizontal) * (mid + data[r + 1, t, 32:48, :])
            north = (0.5 * horizontal) * (mid + norths[t])
            south = (0.5 * horizontal) * (mid + souths[t])
            low, high = mid[:8], mid[8:]
            inner = 2.0 * (low + high)
            outer = jnp.where(sub == 7, 0.0, 2.0 * (high + pltpu.roll(low, 7, 0)))
            outer_down = pltpu.roll(outer, 1, 0)
            coef[r, t, 0:16, :] = west
            coef[r, t, 16:32, :] = north
            coef[r, t, 32:48, :] = south
            coef[r, t, 48:64, :] = (CROSS * horizontal) * mid
            coef[r, t, 64:72, :] = inner
            coef[r, t, 72:80, :] = outer
            coef[r, t, 80:88, :] = outer_down
            ice = data[r, t, 48:49, :]
            drag = data[r, t, 49:50, :]
            bottom = jnp.where(sub == 0, drag, 0.0)
            upright = jnp.concatenate([inner + outer_down + bottom, inner + outer], 0)
            along_x = east + west
            along_y = north + south
            rest = 1.0 - ice
            for c, lateral in enumerate((4.0 * along_x + along_y, along_x + 4.0 * along_y)):
                diagonal = ice * (lateral + upright) + rest
                inverse = OMEGA / diagonal
                coef[r, t, 88 + 16 * c : 104 + 16 * c, :] = ice * inverse
                scaled[r, t, 16 * c : 16 * c + 16, :] = inverse * data[r, t, 16 * c : 16 * c + 16, :]
                if diag is not None:
                    diag[r, t, 16 * c : 16 * c + 16, :] = diagonal

    rows_loop(first, last, row, unroll)


def prepare(w, coef, slope, across, first, last, closed, unroll):
    nt = w.shape[1]

    def row(r):
        norths, souths = shifted([w[r, t] for t in range(nt)], closed)
        for t in range(nt):
            slope[r, t] = norths[t] - souths[t]
            across[r, t] = twice(coef[r, t, 16:32, :]) * norths[t] + twice(coef[r, t, 32:48, :]) * souths[t]

    rows_loop(first, last, row, unroll)


def off_diagonal(w, coef, slope, across, r, t):
    here = w[r, t]
    along = twice(coef[r + 1, t, 0:16, :]) * w[r + 1, t] + twice(coef[r, t, 0:16, :]) * w[r - 1, t]
    side = across[r, t]
    mixed = slope[r + 1, t] - slope[r - 1, t]
    cross = coef[r, t, 48:64, :]
    inner = coef[r, t, 64:72, :]
    outer = coef[r, t, 72:80, :]
    outer_down = coef[r, t, 80:88, :]
    parts = []
    for c in range(2):
        mine = slice(16 * c, 16 * c + 16)
        other = slice(16 - 16 * c, 32 - 16 * c)
        low, high = here[16 * c : 16 * c + 8], here[16 * c + 8 : 16 * c + 16]
        column = jnp.concatenate(
            [inner * high + outer_down * pltpu.roll(high, 1, 0), inner * low + outer * pltpu.roll(low, 7, 0)], 0
        )
        if c == 0:
            lateral = 4.0 * along[mine] + side[mine]
        else:
            lateral = along[mine] + 4.0 * side[mine]
        parts.append(lateral + cross * mixed[other] + column)
    return here, jnp.concatenate(parts, 0)


def sweep(w, new, coef, scaled, slope, across, first, last, closed, unroll, tiles=None, emit=None):
    look, unroll, _ = unroll
    nt = w.shape[1]
    prepare(w, coef, slope, across, first - 1, last + 1, closed, look)

    def row(r):
        for t in range(nt if tiles is None else tiles):
            here, total = off_diagonal(w, coef, slope, across, r, t)
            value = (1.0 - OMEGA) * here + scaled[r, t] + coef[r, t, 88:120, :] * total
            if emit is None:
                new[r, t] = value
            else:
                emit(r, t, value)

    rows_loop(first, last, row, unroll)


def remainders(w, out, data, diag, coef, slope, across, first, last, unroll, tiles):
    look, unroll, _ = unroll
    prepare(w, coef, slope, across, first - 1, last + 1, False, look)

    def row(r):
        for t in range(tiles):
            here, total = off_diagonal(w, coef, slope, across, r, t)
            out[r, t] = data[r, t, 0:32, :] + data[r, t, 48:49, :] * total - diag[r, t] * here

    rows_loop(first, last, row, unroll)


def gather_lanes(v, index):
    return jnp.take_along_axis(v, index, axis=1, mode="promise_in_bounds")


def halve(first, second):
    lane = lax.broadcasted_iota(jnp.int32, first.shape, 1)
    even = (2 * lane) % LANES
    low = gather_lanes(first + pltpu.roll(first, LANES - 1, 1), even)
    if second is None:
        return low
    high = gather_lanes(second + pltpu.roll(second, LANES - 1, 1), even)
    return jnp.where(lane < LANES // 2, low, high)


def restrict_row(source, planes, r):
    both = [source[r, t, planes, :] + source[r + 1, t, planes, :] for t in range(min(2, source.shape[1]))]
    return 0.25 * halve(both[0], both[1] if len(both) > 1 else None)


def prolong_row(tiles, fine_tiles):
    lane = lax.broadcasted_iota(jnp.int32, tiles[0].shape, 1)
    low = lane // 2
    high = LANES // 2 + lane // 2
    first = tiles[0]
    last = tiles[-1]
    out = [gather_lanes(first, low)]
    if fine_tiles == 2:
        out.append(gather_lanes(first, high))
    else:
        out.append(gather_lanes(first, high))
        out.append(gather_lanes(last, jnp.where(lane < LANES // 2, low, high)))
    return out


def put(strip, v, shift, width, at):
    lane = lax.broadcasted_iota(jnp.int32, v.shape, 1)
    rolled = pltpu.roll(v, shift % LANES, 1) if shift % LANES else v
    return jnp.where((lane >= at) & (lane < at + width), rolled, strip)


def unpack_rim(left, right, at, width):
    lane = lax.broadcasted_iota(jnp.int32, left.shape, 1)
    to_low = pltpu.roll(right, (LANES - at) % LANES, 1) if at else right
    shift = (2 * LANES - width - at) % LANES
    to_high = pltpu.roll(left, shift, 1) if shift else left
    return jnp.where(lane < LANES // 2, to_low, to_high)


def pair_rows(tiles):
    sub = lax.broadcasted_iota(jnp.int32, (8, LANES), 0)
    out = tiles[0]
    for j in range(1, len(tiles)):
        out = jnp.where(sub >= 2 * j, pltpu.roll(tiles[j], 2 * j, 0), out)
    return out


def pair_row(tile, j):
    return pltpu.roll(tile, 8 - 2 * j, 0) if j else tile


def copy_rows(source, target, sem, first, last):
    rows = pl.ds(first, last - first)
    copy = pltpu.make_async_copy(source.at[rows], target.at[rows], sem)
    copy.start()
    return copy


def arrange_kernel(misfit, viscosity, friction_in, ice_mask_in, grounded_in, data, strips, edges,
                   misfit_half, viscosity_half, friction, ice_mask, grounded, sems):
    rows = friction.shape[0]
    copies = [
        pltpu.make_async_copy(source, target, sems.at[4 + n])
        for n, (source, target) in enumerate(((friction_in, friction), (ice_mask_in, ice_mask), (grounded_in, grounded)))
    ]
    for t in range(2):
        lanes = pl.ds(t * LANES, LANES)
        copies.append(pltpu.make_async_copy(misfit.at[:, lanes], misfit_half.at[t], sems.at[t]))
        copies.append(pltpu.make_async_copy(viscosity.at[:, lanes], viscosity_half.at[t], sems.at[2 + t]))
    for copy in copies:
        copy.start()
    for copy in copies:
        copy.wait()
    sub = lax.broadcasted_iota(jnp.int32, (8, LANES), 0)
    stride = 2 * rows

    def eight(i, carry):
        block = pl.ds(pl.multiple_of(8 * i, 8), 8)
        for t in range(2):
            lanes = pl.ds(t * LANES, LANES)
            ices = ice_mask[block, lanes].astype(F32)
            drags = friction[block, lanes] * grounded[block, lanes].astype(F32)
            for j in range(8):
                r = 8 * i + j
                ice, drag = ices[j : j + 1], drags[j : j + 1]
                for c in range(2):
                    for p in range(2):
                        v = misfit_half[t, pl.ds(c * 16 * rows + p * rows + r, 8, stride=stride), :]
                        data[r, t, 16 * c + 8 * p : 16 * c + 8 * p + 8, :] = v * ice
                for p in range(2):
                    data[r, t, 32 + 8 * p : 40 + 8 * p, :] = viscosity_half[t, pl.ds(p * rows + r, 8, stride=stride), :]
                data[r, t, 48:56, :] = jnp.where(sub == 0, ice, jnp.where(sub == 1, drag, 0.0))
        return carry

    lax.fori_loop(0, rows // 8, eight, 0)
    corner = RIM0 * RIM0
    for side in range(2):
        low = jnp.zeros((8, LANES), F32)
        high = low
        for first in range(0, NP, 8):
            planes = slice(first, first + 8)
            strip = jnp.zeros((8, LANES), F32)
            for r in range(rows):
                at = r * RIM0
                strip = put(strip, data[r, side, planes, :], at if side == 0 else at + RIM0, RIM0, at)
            strips[side, planes, :] = strip
            at = first // 8 * corner
            low = put(low, strip, at, corner, at)
            high = put(high, strip, at + corner, corner, at)
        strips[side, NP : NP + 8, :] = low
        strips[side, NP + 8 : NP + 16, :] = high
    for t in range(2):
        edges[0, 8 * t : 8 * t + 8, :] = pair_rows([data[r, t, 48:56, :] for r in range(RIM0 - 1)])
        edges[1, 8 * t : 8 * t + 8, :] = pair_rows([data[rows - RIM0 + 1 + r, t, 48:56, :] for r in range(RIM0 - 1)])


def down0_kernel(own, left, right, from_low, from_high, coarse, strips1, edges1, w_out, coef_out, scaled_out,
                 data, diag, slope, across, wa, coef, scaled, sems):
    rows = own.shape[0]
    total = rows + 2 * RIM0

    def copy_row(r):
        for t in range(2):
            data[RIM0 + r, t] = own[r, t]

    rows_loop(0, rows, copy_row, 4)
    for r in range(rows):
        data[RIM0 + r, 2] = unpack_rim(left[0:NP, :], right[0:NP, :], r * RIM0, RIM0)
    inner = RIM0 - 1
    thick = 64 * inner
    thin = thick + 32 * RIM0
    corner = thin + 16
    for face, base, skip in ((from_low, 0, 1), (from_high, RIM0 + rows, 0)):
        for t in range(2):
            for r in range(inner):
                at = 32 * (2 * r + t)
                data[base + skip + r, t, 0:32, :] = face[at : at + 32, :]
                data[base + skip + r, t, 48:56, :] = pair_row(face[thin + 8 * t : thin + 8 * t + 8, :], r)
            for r in range(RIM0):
                at = thick + 16 * (2 * r + t)
                data[base + r, t, 32:48, :] = face[at : at + 16, :]
        for q in range(NP // 8):
            for r in range(RIM0):
                at = RIM0 * (RIM0 * q + r)
                data[base + r, 2, 8 * q : 8 * q + 8, :] = unpack_rim(
                    face[corner : corner + 8, :], face[corner + 8 : corner + 16, :], at, RIM0
                )

    half = total // 2 + 1
    make_coefs(data, coef, scaled, diag, 1, half, 1.0, False, UNROLL0[2])
    copies = [copy_rows(coef, coef_out, sems.at[0], 2, half)]
    make_coefs(data, coef, scaled, diag, half, total - 1, 1.0, False, UNROLL0[2])
    copies.append(copy_rows(coef, coef_out, sems.at[1], half, total - 2))
    copies.append(copy_rows(scaled, scaled_out, sems.at[2], 3, total - 3))
    sweep(scaled, wa, coef, scaled, slope, across, 2, total - 2, False, UNROLL0)
    copies.append(copy_rows(wa, w_out, sems.at[3], 2, total - 2))

    def coefs_row(i):
        coarse[i, 32:56, :] = restrict_row(data, slice(32, 56), RIM0 + 2 * i)

    rows_loop(0, rows // 2, coefs_row, UNROLL_MOVE)
    remainders(wa, diag, data, diag, coef, slope, across, RIM0, RIM0 + rows, UNROLL0, 2)

    def target_row(i):
        coarse[i, 0:32, :] = restrict_row(diag, slice(0, 32), RIM0 + 2 * i)

    rows_loop(0, rows // 2, target_row, UNROLL_MOVE)
    group = LANES // STRIP1
    for side in range(2):
        for part in range(rows // 2 // group):
            for first in range(0, NP, 8):
                planes = slice(first, first + 8)
                strip = jnp.zeros((8, LANES), F32)
                for j in range(group):
                    at = j * STRIP1
                    shift = at if side == 0 else at + STRIP1
                    strip = put(strip, coarse[part * group + j, planes, :], shift, STRIP1, at)
                strips1[side, part, planes, :] = strip
    inner1 = RIM1 - 1
    for face, base in enumerate((0, rows // 2 - inner1)):
        for j in range(0, inner1, 4):
            edges1[face, 2 * j : 2 * j + 8, :] = pair_rows([coarse[base + j + n, 48:56, :] for n in range(4)])
    for copy in copies:
        copy.wait()


def down12_kernel(own, left, right, from_low, from_high, piece, w1_out, coef1_out, scaled1_out, w2_out, coef2_out, scaled2_out,
                  data1, diag1, slope1, across1, wa1, coef1, scaled1, data2, diag2, slope2, across2, wa2, coef2, scaled2, sems):
    rows = own.shape[0]
    total = rows + 2 * RIM1
    group = LANES // STRIP1
    parts = rows // group

    def rim(low, high, base, r):
        part, j = r // group, r % group
        at = base + part * NP
        return unpack_rim(low[at : at + NP, :], high[at : at + NP, :], j * STRIP1, STRIP1)

    def copy_row(r):
        data1[RIM1 + r, 0] = own[r]

    rows_loop(0, rows, copy_row, 4)
    for r in range(rows):
        data1[RIM1 + r, 1] = rim(left, right, 0, r)
    inner = RIM1 - 1
    thick = 32 * inner
    thin = thick + 16 * RIM1
    corner = thin + 2 * inner
    for face, base, skip, first in ((from_low, 0, 1, rows - RIM1), (from_high, RIM1 + rows, 0, 0)):
        for r in range(inner):
            data1[base + skip + r, 0, 0:32, :] = face[32 * r : 32 * r + 32, :]
            at = thin + 8 * (r // 4)
            data1[base + skip + r, 0, 48:56, :] = pair_row(face[at : at + 8, :], r % 4)
        for r in range(RIM1):
            at = thick + 16 * r
            data1[base + r, 0, 32:48, :] = face[at : at + 16, :]
            data1[base + r, 1] = rim(face, face.at[pl.ds(parts * NP, face.shape[0] - parts * NP)], corner, first + r)

    make_coefs(data1, coef1, scaled1, diag1, 1, total - 1, 0.25, False, UNROLL1[2])
    copies = [copy_rows(coef1, coef1_out, sems.at[0], 10, total - 10)]
    copies.append(copy_rows(scaled1, scaled1_out, sems.at[1], 11, total - 11))
    sweep(scaled1, wa1, coef1, scaled1, slope1, across1, 2, total - 2, False, UNROLL1)
    copies.append(copy_rows(wa1, w1_out, sems.at[2], 9, total - 9))
    remainders(wa1, diag1, data1, diag1, coef1, slope1, across1, 3, total - 3, UNROLL1, 2)

    rows2 = rows // 2
    total2 = rows2 + 2 * RIM2

    def coefs_row(i):
        data2[i, 0, 32:56, :] = restrict_row(data1, slice(32, 56), 1 + 2 * i)

    rows_loop(0, total2, coefs_row, UNROLL_MOVE)

    def target_row(i):
        data2[i, 0, 0:32, :] = restrict_row(diag1, slice(0, 32), 1 + 2 * i)

    rows_loop(1, total2 - 1, target_row, UNROLL_MOVE)

    make_coefs(data2, coef2, scaled2, diag2, 1, total2 - 1, 0.0625, False, UNROLL2[2])
    copies.append(copy_rows(coef2, coef2_out, sems.at[3], 2, total2 - 2))
    copies.append(copy_rows(scaled2, scaled2_out, sems.at[4], 3, total2 - 3))
    sweep(scaled2, wa2, coef2, scaled2, slope2, across2, 2, total2 - 2, False, UNROLL2)
    copies.append(copy_rows(wa2, w2_out, sems.at[5], 2, total2 - 2))
    remainders(wa2, diag2, data2, diag2, coef2, slope2, across2, RIM2, RIM2 + rows2, UNROLL2, 1)

    rows3 = rows2 // 2
    width = LANES // rows3
    for first in range(0, NP, 8):
        planes = slice(first, first + 8)
        source = diag2 if first < 32 else data2
        strip = jnp.zeros((8, LANES), F32)
        for i in range(rows3):
            strip = put(strip, restrict_row(source, planes, RIM2 + 2 * i), i * width, width, i * width)
        for d in range(piece.shape[0]):
            piece[d, planes, :] = strip
    for copy in copies:
        copy.wait()


def up_kernel(place, pieces, w0_in, coef0_in, scaled0_in, w1_in, coef1_in, scaled1_in, w2_in, coef2_in, scaled2_in, result,
              data3, coef3, scaled3, wa3, wb3, slope3, across3, w2, coef2, scaled2, wa2, wb2, w1, coef1, scaled1, wa1, wb1,
              w0, coef0, scaled0, wa0, wb0, slope0, across0, result_half, sems):
    slope1, across1 = (v.at[pl.ds(0, wa1.shape[0]), pl.ds(0, 2)] for v in (slope0, across0))
    slope2, across2 = (v.at[pl.ds(0, wa2.shape[0]), pl.ds(0, 1)] for v in (slope0, across0))
    copies = []
    for source, target, first in (
        (w2_in, w2, 2), (coef2_in, coef2, 2), (scaled2_in, scaled2, 3),
        (w1_in, w1, 9), (coef1_in, coef1, 10), (scaled1_in, scaled1, 11),
        (w0_in, w0, 2), (coef0_in, coef0, 2), (scaled0_in, scaled0, 3),
    ):
        copies.append(copy_rows(source, target, sems.at[len(copies)], first, source.shape[0] - first))
    devices_y, devices_x = pieces.shape[0], pieces.shape[1]
    rows3 = devices_y
    width = LANES // devices_y
    whole = devices_x * rows3
    zero = jnp.zeros((NP, LANES), F32)
    for r in range(RIM3):
        for end in (r, RIM3 + whole + r):
            data3[end, 0] = zero
            wa3[end, 0] = zero[:32]
            wb3[end, 0] = zero[:32]
            scaled3[end, 0] = zero[:32]
            slope3[end, 0] = zero[:32]
            coef3[end, 0, 0:16, :] = zero[:16]

    def assemble(d, carry):
        for i in range(rows3):
            line = jnp.zeros((NP, LANES), F32)
            for j in range(devices_y):
                line = put(line, pieces[j, d], (j - i) * width, width, j * width)
            data3[RIM3 + d * rows3 + i, 0] = line
        return carry

    lax.fori_loop(0, devices_x, assemble, 0)
    first, last = RIM3, RIM3 + whole
    make_coefs(data3, coef3, scaled3, None, first, last, 0.25 ** (LEVELS - 1), True, UNROLL3[2])

    def coarse_sweep(source, target):
        def look(r):
            norths, souths = shifted([source[r, 0]], True)
            slope3[r, 0] = norths[0] - souths[0]
            across3[r, 0] = twice(coef3[r, 0, 16:32, :]) * norths[0] + twice(coef3[r, 0, 32:48, :]) * souths[0]

        rows_loop(first, last, look, UNROLL3[0])

        def row(r):
            here, total = off_diagonal(source, coef3, slope3, across3, r, 0)
            target[r, 0] = (1.0 - OMEGA) * here + scaled3[r, 0] + coef3[r, 0, 88:120, :] * total

        rows_loop(first, last, row, UNROLL3[1])

    coarse_sweep(scaled3, wa3)

    def two_sweeps(i, carry):
        coarse_sweep(wa3, wb3)
        coarse_sweep(wb3, wa3)
        return carry

    lax.fori_loop(0, (COARSE_ITERS - 2) // 2, two_sweeps, 0)

    gx, gy, = place[0], place[1]
    lane = lane_ids(32)
    y = jnp.where(lane < 96, lane, lane - LANES)
    column = gy * width + (y + LANES) // 2 - LANES // 2
    inside = (column >= 0) & (column < LANES)
    pick = jnp.where(inside, column, 0)

    for copy in copies[:3]:
        copy.wait()
    rows2 = 2 * rows3
    for i in range(rows3 + 2 * RIM3):
        add = jnp.where(inside, gather_lanes(wa3[gx * rows3 + i, 0], pick), 0.0)
        for r in (2 * i + 2, 2 * i + 3):
            wa2[r, 0] = w2[r, 0] + add
    total2 = rows2 + 2 * RIM2
    sweep(wa2, wb2, coef2, scaled2, slope2, across2, 3, total2 - 3, False, UNROLL2)
    sweep(wb2, wa2, coef2, scaled2, slope2, across2, 4, total2 - 4, False, UNROLL2)


    for copy in copies[3:6]:
        copy.wait()

    def add1(r):
        adds = prolong_row([wa2[r, 0]], 2)
        for t in range(2):
            for fine in (2 * r + 1, 2 * r + 2):
                wa1[fine, t] = w1[fine, t] + adds[t]

    rows_loop(4, total2 - 4, add1, UNROLL_MOVE)
    total1 = 2 * rows2 + 2 * RIM1
    sweep(wa1, wb1, coef1, scaled1, slope1, across1, 11, total1 - 11, False, UNROLL1)
    sweep(wb1, wa1, coef1, scaled1, slope1, across1, 12, total1 - 12, False, UNROLL1)


    for copy in copies[6:]:
        copy.wait()

    def add0(r):
        adds = prolong_row([wa1[r, t] for t in range(2)], 3)
        for t in range(3):
            for fine in (2 * r - 22, 2 * r - 21):
                wa0[fine, t] = w0[fine, t] + adds[t]

    rows_loop(12, total1 - 12, add0, UNROLL_MOVE)
    rows0 = 4 * rows2
    total0 = rows0 + 2 * RIM0
    sweep(wa0, wb0, coef0, scaled0, slope0, across0, 3, total0 - 3, False, UNROLL0)

    def emit(r, t, value):
        for c in range(2):
            for p in range(2):
                start = c * 16 * rows0 + p * rows0 + r - RIM0
                result_half[t, pl.ds(start, 8, stride=2 * rows0), :] = value[16 * c + 8 * p : 16 * c + 8 * p + 8]

    sweep(wb0, None, coef0, scaled0, slope0, across0, RIM0, RIM0 + rows0, False, UNROLL0, tiles=2, emit=emit)
    copies = [
        pltpu.make_async_copy(result_half.at[t], result.at[:, pl.ds(t * LANES, LANES)], sems.at[t]) for t in range(2)
    ]
    for copy in copies:
        copy.start()
    for copy in copies:
        copy.wait()


def shape(*dims):
    return jax.ShapeDtypeStruct(dims, F32)


def stored(*dims):
    return pltpu.HBM(dims, F32)


def in_hbm(arrays):
    return [pltpu.with_memory_space_constraint(v, pltpu.HBM) for v in arrays]


VM = pl.BlockSpec(memory_space=pltpu.VMEM)
SM = pl.BlockSpec(memory_space=pltpu.SMEM)
HB = pl.BlockSpec(memory_space=pl.ANY)
PARAMS = pltpu.CompilerParams(vmem_limit_bytes=VMEM_DOWN)


def buffers(rows, tiles, names):
    planes = {"data": NP, "coef": 8 * NC}
    return [pltpu.VMEM((rows, tiles, planes.get(name, 32), LANES), F32) for name in names]


def per_device(misfit, viscosity, friction, ice_mask, grounded):
    rows, columns = friction.shape
    gx, gy = lax.axis_index("gx"), lax.axis_index("gy")
    nx, ny = lax.axis_size("gx"), lax.axis_size("gy")
    upward = [(i, i + 1) for i in range(nx - 1)]
    downward = [(i + 1, i) for i in range(nx - 1)]

    def beside(strips):
        every = lax.all_gather(strips, "gy", axis=0)
        left = lax.dynamic_index_in_dim(every, jnp.maximum(gy - 1, 0), 0, keepdims=False)[1]
        right = lax.dynamic_index_in_dim(every, jnp.minimum(gy + 1, ny - 1), 0, keepdims=False)[0]
        return jnp.where(gy > 0, left, 0.0), jnp.where(gy < ny - 1, right, 0.0)

    data0, strips0, edges0 = pl.pallas_call(
        arrange_kernel,
        out_shape=(shape(rows, 2, NP, LANES), shape(2, NP + 16, LANES), shape(2, 16, LANES)),
        in_specs=[HB] * 5,
        out_specs=(VM, VM, VM),
        scratch_shapes=[
            pltpu.VMEM((2, 2 * 16 * rows, LANES), F32),
            pltpu.VMEM((2, 16 * rows, LANES), F32),
            pltpu.VMEM((rows, columns), F32),
            pltpu.VMEM((rows, columns), jnp.int32),
            pltpu.VMEM((rows, columns), jnp.int32),
            pltpu.SemaphoreType.DMA((7,)),
        ],
        compiler_params=PARAMS,
        name="arrange",
    )(
        *in_hbm(v.reshape(-1, columns) for v in (misfit, viscosity, friction, ice_mask, grounded))
    )
    left, right = beside(strips0)
    inner = RIM0 - 1

    def face0(which, first, first_inner):
        corner = slice(NP + 8 * which, NP + 8 * which + 8)
        parts = (
            data0[first_inner : first_inner + inner, :, 0:32],
            data0[first : first + RIM0, :, 32:48],
            edges0[which],
            left[corner],
            right[corner],
        )
        return jnp.concatenate([v.reshape(-1, LANES) for v in parts], 0)

    low_face = face0(0, 0, 0)
    high_face = face0(1, rows - RIM0, rows - inner)
    from_low = lax.ppermute(high_face, "gx", upward)
    from_high = lax.ppermute(low_face, "gx", downward)

    total0 = rows + 2 * RIM0
    names = ("data", "diag", "slope", "across", "w", "coef", "scaled")
    rows1 = rows // 2
    group = LANES // STRIP1
    field0 = stored(total0, 3, 32, LANES)
    inner1 = RIM1 - 1
    data1, strips1, edges1, w0, coef0, scaled0 = pl.pallas_call(
        down0_kernel,
        out_shape=(
            shape(rows1, NP, LANES),
            shape(2, rows1 // group, NP, LANES),
            shape(2, 2 * inner1, LANES),
            field0,
            stored(total0, 3, 8 * NC, LANES),
            field0,
        ),
        in_specs=[VM] * 5,
        out_specs=(VM, VM, VM, HB, HB, HB),
        scratch_shapes=buffers(total0, 3, names) + [pltpu.SemaphoreType.DMA((4,))],
        compiler_params=PARAMS,
        name="down0",
    )(data0, left, right, from_low, from_high)

    left, right = beside(strips1)
    left, right = left.reshape(-1, LANES), right.reshape(-1, LANES)

    def face1(which, first, first_inner):
        parts = (
            data1[first_inner : first_inner + inner1, 0:32],
            data1[first : first + RIM1, 32:48],
            edges1[which],
            left,
            right,
        )
        return jnp.concatenate([v.reshape(-1, LANES) for v in parts], 0)

    low_face = face1(0, 0, 0)
    high_face = face1(1, rows1 - RIM1, rows1 - inner1)
    from_low = lax.ppermute(high_face, "gx", upward)
    from_high = lax.ppermute(low_face, "gx", downward)

    total1 = rows1 + 2 * RIM1
    rows2 = rows1 // 2
    total2 = rows2 + 2 * RIM2
    field1 = stored(total1, 2, 32, LANES)
    field2 = stored(total2, 1, 32, LANES)
    piece, w1, coef1, scaled1, w2, coef2, scaled2 = pl.pallas_call(
        down12_kernel,
        out_shape=(
            shape(nx, NP, LANES),
            field1,
            stored(total1, 2, 8 * NC, LANES),
            field1,
            field2,
            stored(total2, 1, 8 * NC, LANES),
            field2,
        ),
        in_specs=[VM] * 5,
        out_specs=(VM,) + (HB,) * 6,
        scratch_shapes=buffers(total1, 2, names) + buffers(total2, 1, names) + [pltpu.SemaphoreType.DMA((6,))],
        compiler_params=PARAMS,
        name="down12",
    )(data1, left, right, from_low, from_high)

    pieces = lax.all_gather(lax.all_to_all(piece, "gx", 0, 0), "gy", axis=0)

    rows3 = rows2 // 2
    total3 = nx * rows3 + 2 * RIM3
    ups = ("w", "coef", "scaled", "w", "w")
    result = pl.pallas_call(
        up_kernel,
        out_shape=shape(2 * 16 * rows, columns),
        in_specs=[SM, VM] + [HB] * 9,
        out_specs=HB,
        scratch_shapes=buffers(total3, 1, ("data", "coef", "scaled", "w", "w", "slope", "across"))
        + buffers(total2, 1, ups)
        + buffers(total1, 2, ups)
        + buffers(total0, 3, ups)
        + buffers(max(total0, total1), 3, ("slope", "across"))
        + [pltpu.VMEM((2, 2 * 16 * rows, LANES), F32), pltpu.SemaphoreType.DMA((9,))],
        compiler_params=pltpu.CompilerParams(vmem_limit_bytes=VMEM_UP),
        name="up",
    )(
        jnp.stack([gx, gy]).astype(jnp.int32),
        pieces,
        *in_hbm([w0, coef0, scaled0, w1, coef1, scaled1, w2, coef2, scaled2]),
    )
    return result.reshape(misfit.shape)


def solution(mesh):
    placed = (
        P(None, None, "gx", "gy"),
        P(None, "gx", "gy"),
        P("gx", "gy"),
        P("gx", "gy"),
        P("gx", "gy"),
    )
    return jax.shard_map(
        per_device, mesh=mesh, in_specs=placed, out_specs=P(None, None, "gx", "gy"), check_vma=False
    )
```

```python
import functools

import jax
import jax.numpy as jnp
from jax import lax
from jax.experimental import pallas as pl
from jax.experimental.pallas import tpu as pltpu
from jax.sharding import PartitionSpec as P

LEVELS = 4
COARSE_ITERS = 20
OMEGA = 0.6
CROSS = 0.75
NP = 56
LANES = 128
RIM0 = 4
RIM1 = 13
RIM2 = 6
RIM3 = 2
STRIP1 = 16
NC = 15
PITCH = 40
VMEM_DOWN = 28 * 1024 * 1024
VMEM_UP = 60 * 1024 * 1024
F32 = jnp.float32
UNROLL0 = (18, 6, 4)
UNROLL1 = (38, 12, 8)
UNROLL2 = (18, 6, 4)
UNROLL3 = (32, 32, 8)
UNROLL0_UP = (18, 17)
UNROLL1_UP = (22, 20)
UNROLL_MOVE = 8


def rows_loop(first, last, body, unroll):
    count = (last - first) // unroll

    def step(i, carry):
        for j in range(unroll):
            body(first + i * unroll + j)
        return carry

    if count:
        lax.fori_loop(0, count, step, 0)
    for r in range(first + count * unroll, last):
        body(r)


def lane_ids(rows=8):
    return lax.broadcasted_iota(jnp.int32, (rows, LANES), 1)


def shifted(tiles, closed):
    lane = lax.broadcasted_iota(jnp.int32, tiles[0].shape, 1)
    up = [pltpu.roll(v, LANES - 1, 1) for v in tiles]
    down = [pltpu.roll(v, 1, 1) for v in tiles]
    n = len(tiles)
    if closed:
        zero = jnp.zeros_like(tiles[0])
        return (
            [jnp.where(lane == LANES - 1, zero, v) for v in up],
            [jnp.where(lane == 0, zero, v) for v in down],
        )
    if n == 1:
        return up, down
    return (
        [jnp.where(lane == LANES - 1, up[(t + 1) % n], up[t]) for t in range(n)],
        [jnp.where(lane == 0, down[(t - 1) % n], down[t]) for t in range(n)],
    )


def twice(v):
    return jnp.concatenate([v, v], 0)


def make_coefs(data, coef, scaled, diag, first, last, horizontal, closed, unroll):
    nt = data.shape[1]
    sub = lax.broadcasted_iota(jnp.int32, (8, LANES), 0)

    def row(r):
        mids = [data[r, t, 32:48, :] for t in range(nt)]
        norths, souths = shifted(mids, closed)
        for t in range(nt):
            mid = mids[t]
            west = (0.5 * horizontal) * (mid + data[r - 1, t, 32:48, :])
            east = (0.5 * horizontal) * (mid + data[r + 1, t, 32:48, :])
            north = (0.5 * horizontal) * (mid + norths[t])
            south = (0.5 * horizontal) * (mid + souths[t])
            low, high = mid[:8], mid[8:]
            inner = 2.0 * (low + high)
            outer = jnp.where(sub == 7, 0.0, 2.0 * (high + pltpu.roll(low, 7, 0)))
            outer_down = pltpu.roll(outer, 1, 0)
            coef[r, t, 0:16, :] = west
            coef[r, t, 16:32, :] = north
            coef[r, t, 32:48, :] = south
            coef[r, t, 48:64, :] = (CROSS * horizontal) * mid
            coef[r, t, 64:72, :] = inner
            coef[r, t, 72:80, :] = outer
            coef[r, t, 80:88, :] = outer_down
            ice = data[r, t, 48:49, :]
            drag = data[r, t, 49:50, :]
            bottom = jnp.where(sub == 0, drag, 0.0)
            upright = jnp.concatenate([inner + outer_down + bottom, inner + outer], 0)
            along_x = east + west
            along_y = north + south
            rest = 1.0 - ice
            for c, lateral in enumerate((4.0 * along_x + along_y, along_x + 4.0 * along_y)):
                diagonal = ice * (lateral + upright) + rest
                inverse = OMEGA / diagonal
                coef[r, t, 88 + 16 * c : 104 + 16 * c, :] = ice * inverse
                scaled[r, t, 16 * c : 16 * c + 16, :] = inverse * data[r, t, 16 * c : 16 * c + 16, :]
                if diag is not None:
                    diag[r, t, 16 * c : 16 * c + 16, :] = diagonal

    rows_loop(first, last, row, unroll)


def prepare(w, coef, slope, across, first, last, closed, unroll):
    nt = w.shape[1]

    def row(r):
        norths, souths = shifted([w[r, t] for t in range(nt)], closed)
        for t in range(nt):
            slope[r, t] = norths[t] - souths[t]
            across[r, t] = twice(coef[r, t, 16:32, :]) * norths[t] + twice(coef[r, t, 32:48, :]) * souths[t]

    rows_loop(first, last, row, unroll)


def off_diagonal(w, coef, slope, across, r, t):
    here = w[r, t]
    along = twice(coef[r + 1, t, 0:16, :]) * w[r + 1, t] + twice(coef[r, t, 0:16, :]) * w[r - 1, t]
    side = across[r, t]
    mixed = slope[r + 1, t] - slope[r - 1, t]
    cross = coef[r, t, 48:64, :]
    inner = coef[r, t, 64:72, :]
    outer = coef[r, t, 72:80, :]
    outer_down = coef[r, t, 80:88, :]
    parts = []
    for c in range(2):
        mine = slice(16 * c, 16 * c + 16)
        other = slice(16 - 16 * c, 32 - 16 * c)
        low, high = here[16 * c : 16 * c + 8], here[16 * c + 8 : 16 * c + 16]
        column = jnp.concatenate(
            [inner * high + outer_down * pltpu.roll(high, 1, 0), inner * low + outer * pltpu.roll(low, 7, 0)], 0
        )
        if c == 0:
            lateral = 4.0 * along[mine] + side[mine]
        else:
            lateral = along[mine] + 4.0 * side[mine]
        parts.append(lateral + cross * mixed[other] + column)
    return here, jnp.concatenate(parts, 0)


def sweep(w, new, coef, scaled, slope, across, first, last, closed, unroll, tiles=None, emit=None):
    look, unroll = unroll[:2]
    nt = w.shape[1]
    prepare(w, coef, slope, across, first - 1, last + 1, closed, look)

    def row(r):
        for t in range(nt if tiles is None else tiles):
            here, total = off_diagonal(w, coef, slope, across, r, t)
            value = (1.0 - OMEGA) * here + scaled[r, t] + coef[r, t, 88:120, :] * total
            if emit is None:
                new[r, t] = value
            else:
                emit(r, t, value)

    rows_loop(first, last, row, unroll)


def remainders(w, out, data, diag, coef, slope, across, first, last, unroll, tiles):
    look, unroll = unroll[:2]
    prepare(w, coef, slope, across, first - 1, last + 1, False, look)

    def row(r):
        for t in range(tiles):
            here, total = off_diagonal(w, coef, slope, across, r, t)
            out[r, t] = data[r, t, 0:32, :] + data[r, t, 48:49, :] * total - diag[r, t] * here

    rows_loop(first, last, row, unroll)


def gather_lanes(v, index):
    return jnp.take_along_axis(v, index, axis=1, mode="promise_in_bounds")


def halve(first, second):
    lane = lax.broadcasted_iota(jnp.int32, first.shape, 1)
    even = (2 * lane) % LANES
    low = gather_lanes(first + pltpu.roll(first, LANES - 1, 1), even)
    if second is None:
        return low
    high = gather_lanes(second + pltpu.roll(second, LANES - 1, 1), even)
    return jnp.where(lane < LANES // 2, low, high)


def restrict_row(source, planes, r):
    both = [source[r, t, planes, :] + source[r + 1, t, planes, :] for t in range(min(2, source.shape[1]))]
    return 0.25 * halve(both[0], both[1] if len(both) > 1 else None)


def prolong_row(tiles, fine_tiles):
    lane = lax.broadcasted_iota(jnp.int32, tiles[0].shape, 1)
    low = lane // 2
    high = LANES // 2 + lane // 2
    first = tiles[0]
    last = tiles[-1]
    out = [gather_lanes(first, low)]
    if fine_tiles == 2:
        out.append(gather_lanes(first, high))
    else:
        out.append(gather_lanes(first, high))
        out.append(gather_lanes(last, jnp.where(lane < LANES // 2, low, high)))
    return out


def put(strip, v, shift, width, at):
    lane = lax.broadcasted_iota(jnp.int32, v.shape, 1)
    rolled = pltpu.roll(v, shift % LANES, 1) if shift % LANES else v
    return jnp.where((lane >= at) & (lane < at + width), rolled, strip)


def unpack_rim(left, right, at, width):
    lane = lax.broadcasted_iota(jnp.int32, left.shape, 1)
    to_low = pltpu.roll(right, (LANES - at) % LANES, 1) if at else right
    shift = (2 * LANES - width - at) % LANES
    to_high = pltpu.roll(left, shift, 1) if shift else left
    return jnp.where(lane < LANES // 2, to_low, to_high)


def pair_rows(tiles):
    sub = lax.broadcasted_iota(jnp.int32, (8, LANES), 0)
    out = tiles[0]
    for j in range(1, len(tiles)):
        out = jnp.where(sub >= 2 * j, pltpu.roll(tiles[j], 2 * j, 0), out)
    return out


def pair_row(tile, j):
    return pltpu.roll(tile, 8 - 2 * j, 0) if j else tile


def copy_rows(source, target, sem, first, last):
    rows = pl.ds(first, last - first)
    copy = pltpu.make_async_copy(source.at[rows], target.at[rows], sem)
    copy.start()
    return copy


def arrange_kernel(misfit, viscosity, friction_in, ice_mask_in, grounded_in, data, strips, edges,
                   misfit_half, viscosity_half, friction, ice_mask, grounded, sems):
    rows = friction.shape[0]
    copies = [
        pltpu.make_async_copy(source, target, sems.at[n])
        for n, (source, target) in enumerate(((friction_in, friction), (ice_mask_in, ice_mask), (grounded_in, grounded)))
    ]
    for t in range(2):
        lanes = pl.ds(t * LANES, LANES)
        for p in range(2):
            n = 2 * t + p
            for source, target, sem in ((misfit, misfit_half, 3 + n), (viscosity, viscosity_half, 7 + n)):
                copies.append(
                    pltpu.make_async_copy(source.at[:, p, :, lanes], target.at[n, :, pl.ds(0, rows)], sems.at[sem])
                )
    for copy in copies:
        copy.start()
    for copy in copies:
        copy.wait()
    sub = lax.broadcasted_iota(jnp.int32, (8, LANES), 0)
    misfit_rows = misfit_half.reshape(4, -1, LANES)
    viscosity_rows = viscosity_half.reshape(4, -1, LANES)

    def eight(i, carry):
        block = pl.ds(pl.multiple_of(8 * i, 8), 8)
        for t in range(2):
            lanes = pl.ds(t * LANES, LANES)
            ices = ice_mask[block, lanes].astype(F32)
            drags = friction[block, lanes] * grounded[block, lanes].astype(F32)
            for j in range(8):
                r = 8 * i + j
                ice, drag = ices[j : j + 1], drags[j : j + 1]
                for c in range(2):
                    for p in range(2):
                        v = misfit_rows[2 * t + p, pl.ds(8 * c * PITCH + r, 8, stride=PITCH), :]
                        data[r, t, 16 * c + 8 * p : 16 * c + 8 * p + 8, :] = v * ice
                for p in range(2):
                    data[r, t, 32 + 8 * p : 40 + 8 * p, :] = viscosity_rows[2 * t + p, pl.ds(r, 8, stride=PITCH), :]
                data[r, t, 48:56, :] = jnp.where(sub == 0, ice, jnp.where(sub == 1, drag, 0.0))
        return carry

    lax.fori_loop(0, rows // 8, eight, 0)
    corner = RIM0 * RIM0
    for side in range(2):
        low = jnp.zeros((8, LANES), F32)
        high = low
        for first in range(0, NP, 8):
            planes = slice(first, first + 8)
            strip = jnp.zeros((8, LANES), F32)
            for r in range(rows):
                at = r * RIM0
                strip = put(strip, data[r, side, planes, :], at if side == 0 else at + RIM0, RIM0, at)
            strips[side, planes, :] = strip
            at = first // 8 * corner
            low = put(low, strip, at, corner, at)
            high = put(high, strip, at + corner, corner, at)
        strips[side, NP : NP + 8, :] = low
        strips[side, NP + 8 : NP + 16, :] = high
    for t in range(2):
        edges[0, 8 * t : 8 * t + 8, :] = pair_rows([data[r, t, 48:56, :] for r in range(RIM0 - 1)])
        edges[1, 8 * t : 8 * t + 8, :] = pair_rows([data[rows - RIM0 + 1 + r, t, 48:56, :] for r in range(RIM0 - 1)])


def down0_kernel(own, left, right, from_low, from_high, coarse, strips1, edges1, w_out, coef_out, scaled_out,
                 data, diag, slope, across, wa, coef, scaled, sems):
    rows = own.shape[0]
    total = rows + 2 * RIM0

    def copy_row(r):
        for t in range(2):
            data[RIM0 + r, t] = own[r, t]

    rows_loop(0, rows, copy_row, 4)
    for r in range(rows):
        data[RIM0 + r, 2] = unpack_rim(left[0:NP, :], right[0:NP, :], r * RIM0, RIM0)
    inner = RIM0 - 1
    thick = 64 * inner
    thin = thick + 32 * RIM0
    corner = thin + 16
    for face, base, skip in ((from_low, 0, 1), (from_high, RIM0 + rows, 0)):
        for t in range(2):
            for r in range(inner):
                at = 32 * (2 * r + t)
                data[base + skip + r, t, 0:32, :] = face[at : at + 32, :]
                data[base + skip + r, t, 48:56, :] = pair_row(face[thin + 8 * t : thin + 8 * t + 8, :], r)
            for r in range(RIM0):
                at = thick + 16 * (2 * r + t)
                data[base + r, t, 32:48, :] = face[at : at + 16, :]
        for q in range(NP // 8):
            for r in range(RIM0):
                at = RIM0 * (RIM0 * q + r)
                data[base + r, 2, 8 * q : 8 * q + 8, :] = unpack_rim(
                    face[corner : corner + 8, :], face[corner + 8 : corner + 16, :], at, RIM0
                )

    half = total // 2 + 1
    make_coefs(data, coef, scaled, diag, 1, half, 1.0, False, UNROLL0[2])
    copies = [copy_rows(coef, coef_out, sems.at[0], 2, half)]
    make_coefs(data, coef, scaled, diag, half, total - 1, 1.0, False, UNROLL0[2])
    copies.append(copy_rows(coef, coef_out, sems.at[1], half, total - 2))
    copies.append(copy_rows(scaled, scaled_out, sems.at[2], 3, total - 3))
    sweep(scaled, wa, coef, scaled, slope, across, 2, total - 2, False, UNROLL0)
    copies.append(copy_rows(wa, w_out, sems.at[3], 2, total - 2))

    def coefs_row(i):
        coarse[i, 32:56, :] = restrict_row(data, slice(32, 56), RIM0 + 2 * i)

    rows_loop(0, rows // 2, coefs_row, UNROLL_MOVE)
    remainders(wa, diag, data, diag, coef, slope, across, RIM0, RIM0 + rows, UNROLL0, 2)

    def target_row(i):
        coarse[i, 0:32, :] = restrict_row(diag, slice(0, 32), RIM0 + 2 * i)

    rows_loop(0, rows // 2, target_row, UNROLL_MOVE)
    group = LANES // STRIP1
    for side in range(2):
        for part in range(rows // 2 // group):
            for first in range(0, NP, 8):
                planes = slice(first, first + 8)
                strip = jnp.zeros((8, LANES), F32)
                for j in range(group):
                    at = j * STRIP1
                    shift = at if side == 0 else at + STRIP1
                    strip = put(strip, coarse[part * group + j, planes, :], shift, STRIP1, at)
                strips1[side, part, planes, :] = strip
    inner1 = RIM1 - 1
    for face, base in enumerate((0, rows // 2 - inner1)):
        for j in range(0, inner1, 4):
            edges1[face, 2 * j : 2 * j + 8, :] = pair_rows([coarse[base + j + n, 48:56, :] for n in range(4)])
    for copy in copies:
        copy.wait()


def down12_kernel(own, left, right, from_low, from_high, piece, w1_out, coef1_out, scaled1_out, w2_out, coef2_out, scaled2_out,
                  data1, diag1, slope1, across1, wa1, coef1, scaled1, data2, diag2, slope2, across2, wa2, coef2, scaled2, sems):
    rows = own.shape[0]
    total = rows + 2 * RIM1
    group = LANES // STRIP1
    parts = rows // group

    def rim(low, high, base, r):
        part, j = r // group, r % group
        at = base + part * NP
        return unpack_rim(low[at : at + NP, :], high[at : at + NP, :], j * STRIP1, STRIP1)

    def copy_row(r):
        data1[RIM1 + r, 0] = own[r]

    rows_loop(0, rows, copy_row, 4)
    for r in range(rows):
        data1[RIM1 + r, 1] = rim(left, right, 0, r)
    inner = RIM1 - 1
    thick = 32 * inner
    thin = thick + 16 * RIM1
    corner = thin + 2 * inner
    for face, base, skip, first in ((from_low, 0, 1, rows - RIM1), (from_high, RIM1 + rows, 0, 0)):
        for r in range(inner):
            data1[base + skip + r, 0, 0:32, :] = face[32 * r : 32 * r + 32, :]
            at = thin + 8 * (r // 4)
            data1[base + skip + r, 0, 48:56, :] = pair_row(face[at : at + 8, :], r % 4)
        for r in range(RIM1):
            at = thick + 16 * r
            data1[base + r, 0, 32:48, :] = face[at : at + 16, :]
            data1[base + r, 1] = rim(face, face.at[pl.ds(parts * NP, face.shape[0] - parts * NP)], corner, first + r)

    make_coefs(data1, coef1, scaled1, diag1, 1, total - 1, 0.25, False, UNROLL1[2])
    copies = [copy_rows(coef1, coef1_out, sems.at[0], 10, total - 10)]
    copies.append(copy_rows(scaled1, scaled1_out, sems.at[1], 11, total - 11))
    sweep(scaled1, wa1, coef1, scaled1, slope1, across1, 2, total - 2, False, UNROLL1)
    copies.append(copy_rows(wa1, w1_out, sems.at[2], 9, total - 9))
    remainders(wa1, diag1, data1, diag1, coef1, slope1, across1, 3, total - 3, UNROLL1, 2)

    rows2 = rows // 2
    total2 = rows2 + 2 * RIM2

    def coefs_row(i):
        data2[i, 0, 32:56, :] = restrict_row(data1, slice(32, 56), 1 + 2 * i)

    rows_loop(0, total2, coefs_row, UNROLL_MOVE)

    def target_row(i):
        data2[i, 0, 0:32, :] = restrict_row(diag1, slice(0, 32), 1 + 2 * i)

    rows_loop(1, total2 - 1, target_row, UNROLL_MOVE)

    make_coefs(data2, coef2, scaled2, diag2, 1, total2 - 1, 0.0625, False, UNROLL2[2])
    copies.append(copy_rows(coef2, coef2_out, sems.at[3], 2, total2 - 2))
    copies.append(copy_rows(scaled2, scaled2_out, sems.at[4], 3, total2 - 3))
    sweep(scaled2, wa2, coef2, scaled2, slope2, across2, 2, total2 - 2, False, UNROLL2)
    copies.append(copy_rows(wa2, w2_out, sems.at[5], 2, total2 - 2))
    remainders(wa2, diag2, data2, diag2, coef2, slope2, across2, RIM2, RIM2 + rows2, UNROLL2, 1)

    rows3 = rows2 // 2
    width = LANES // rows3
    for first in range(0, NP, 8):
        planes = slice(first, first + 8)
        source = diag2 if first < 32 else data2
        strip = jnp.zeros((8, LANES), F32)
        for i in range(rows3):
            strip = put(strip, restrict_row(source, planes, RIM2 + 2 * i), i * width, width, i * width)
        for d in range(piece.shape[0]):
            piece[d, planes, :] = strip
    for copy in copies:
        copy.wait()


def up_kernel(place, pieces, w0_in, coef0_in, scaled0_in, w1_in, coef1_in, scaled1_in, w2_in, coef2_in, scaled2_in, result,
              data3, coef3, scaled3, wa3, wb3, slope3, across3, w2, coef2, scaled2, wa2, wb2, w1, coef1, scaled1, wa1, wb1,
              w0, coef0, scaled0, wa0, wb0, slope0, across0, result_half, sems):
    slope1, across1 = (v.at[pl.ds(0, wa1.shape[0]), pl.ds(0, 2)] for v in (slope0, across0))
    slope2, across2 = (v.at[pl.ds(0, wa2.shape[0]), pl.ds(0, 1)] for v in (slope0, across0))
    copies = []
    for source, target, first in (
        (w2_in, w2, 2), (coef2_in, coef2, 2), (scaled2_in, scaled2, 3),
        (w1_in, w1, 9), (coef1_in, coef1, 10), (scaled1_in, scaled1, 11),
        (w0_in, w0, 2), (coef0_in, coef0, 2), (scaled0_in, scaled0, 3),
    ):
        copies.append(copy_rows(source, target, sems.at[len(copies)], first, source.shape[0] - first))
    devices_y, devices_x = pieces.shape[0], pieces.shape[1]
    rows3 = devices_y
    width = LANES // devices_y
    whole = devices_x * rows3
    zero = jnp.zeros((NP, LANES), F32)
    for r in range(RIM3):
        for end in (r, RIM3 + whole + r):
            data3[end, 0] = zero
            wa3[end, 0] = zero[:32]
            wb3[end, 0] = zero[:32]
            scaled3[end, 0] = zero[:32]
            slope3[end, 0] = zero[:32]
            coef3[end, 0] = jnp.zeros((8 * NC, LANES), F32)

    def assemble(d, carry):
        for i in range(rows3):
            line = jnp.zeros((NP, LANES), F32)
            for j in range(devices_y):
                line = put(line, pieces[j, d], (j - i) * width, width, j * width)
            data3[RIM3 + d * rows3 + i, 0] = line
        return carry

    lax.fori_loop(0, devices_x, assemble, 0)
    first, last = RIM3, RIM3 + whole
    make_coefs(data3, coef3, scaled3, None, first, last, 0.25 ** (LEVELS - 1), True, UNROLL3[2])

    gx, gy = place[0], place[1]

    def coarse_sweep(source, target, extent):
        begin, end = (first, last) if extent is None else (0, extent)
        start = 0 if extent is None else first + jnp.clip(gx * rows3 - (extent - rows3) // 2, 0, whole - extent)
        around = 0 if extent is None else 1

        def look(r):
            r = start + r
            norths, souths = shifted([source[r, 0]], True)
            slope3[r, 0] = norths[0] - souths[0]
            across3[r, 0] = twice(coef3[r, 0, 16:32, :]) * norths[0] + twice(coef3[r, 0, 32:48, :]) * souths[0]

        rows_loop(begin - around, end + around, look, UNROLL3[0] if extent is None else extent + 2)

        def row(r):
            r = start + r
            here, total = off_diagonal(source, coef3, slope3, across3, r, 0)
            target[r, 0] = (1.0 - OMEGA) * here + scaled3[r, 0] + coef3[r, 0, 88:120, :] * total

        rows_loop(begin, end, row, UNROLL3[1])

    coarse_sweep(scaled3, wa3, None)
    done = 2
    narrow = [(None, COARSE_ITERS - 9), (rows3 + 20, COARSE_ITERS - 5), (rows3 + 12, COARSE_ITERS)]
    buffers = (wa3, wb3)
    for extent, until in narrow:
        if extent is not None and extent > whole:
            extent = None

        def two_sweeps(i, carry, extent=extent, pair=buffers):
            coarse_sweep(pair[0], pair[1], extent)
            coarse_sweep(pair[1], pair[0], extent)
            return carry

        if (until - done) // 2:
            lax.fori_loop(0, (until - done) // 2, two_sweeps, 0)
        if (until - done) % 2:
            coarse_sweep(buffers[0], buffers[1], extent)
            buffers = buffers[::-1]
        done = until
    solved = buffers[0]

    lane = lane_ids(32)
    y = jnp.where(lane < 96, lane, lane - LANES)
    column = gy * width + (y + LANES) // 2 - LANES // 2
    inside = (column >= 0) & (column < LANES)
    pick = jnp.where(inside, column, 0)

    for copy in copies[:3]:
        copy.wait()
    rows2 = 2 * rows3
    for i in range(rows3 + 2 * RIM3):
        add = jnp.where(inside, gather_lanes(solved[gx * rows3 + i, 0], pick), 0.0)
        for r in (2 * i + 2, 2 * i + 3):
            wa2[r, 0] = w2[r, 0] + add
    total2 = rows2 + 2 * RIM2
    sweep(wa2, wb2, coef2, scaled2, slope2, across2, 3, total2 - 3, False, UNROLL2)
    sweep(wb2, wa2, coef2, scaled2, slope2, across2, 4, total2 - 4, False, UNROLL2)


    for copy in copies[3:6]:
        copy.wait()

    def add1(r):
        adds = prolong_row([wa2[r, 0]], 2)
        for t in range(2):
            for fine in (2 * r + 1, 2 * r + 2):
                wa1[fine, t] = w1[fine, t] + adds[t]

    rows_loop(4, total2 - 4, add1, UNROLL_MOVE)
    total1 = 2 * rows2 + 2 * RIM1
    sweep(wa1, wb1, coef1, scaled1, slope1, across1, 11, total1 - 11, False, UNROLL1_UP)
    sweep(wb1, wa1, coef1, scaled1, slope1, across1, 12, total1 - 12, False, UNROLL1_UP)


    for copy in copies[6:]:
        copy.wait()

    def add0(r):
        adds = prolong_row([wa1[r, t] for t in range(2)], 3)
        for t in range(3):
            for fine in (2 * r - 22, 2 * r - 21):
                wa0[fine, t] = w0[fine, t] + adds[t]

    rows_loop(12, total1 - 12, add0, UNROLL_MOVE)
    rows0 = 4 * rows2
    total0 = rows0 + 2 * RIM0
    sweep(wa0, wb0, coef0, scaled0, slope0, across0, 3, total0 - 3, False, UNROLL0_UP)

    result_rows = result_half.reshape(4, -1, LANES)

    def emit(r, t, value):
        for c in range(2):
            for p in range(2):
                start = 8 * c * PITCH + r - RIM0
                result_rows[2 * t + p, pl.ds(start, 8, stride=PITCH), :] = value[16 * c + 8 * p : 16 * c + 8 * p + 8]

    sweep(wb0, None, coef0, scaled0, slope0, across0, RIM0, RIM0 + rows0, False, UNROLL0_UP, tiles=2, emit=emit)
    copies = [
        pltpu.make_async_copy(
            result_half.at[2 * t + p, :, pl.ds(0, rows0)], result.at[:, p, :, pl.ds(t * LANES, LANES)], sems.at[2 * t + p]
        )
        for t in range(2)
        for p in range(2)
    ]
    for copy in copies:
        copy.start()
    for copy in copies:
        copy.wait()


def shape(*dims):
    return jax.ShapeDtypeStruct(dims, F32)


def stored(*dims):
    return pltpu.HBM(dims, F32)


def in_hbm(arrays):
    return [pltpu.with_memory_space_constraint(v, pltpu.HBM) for v in arrays]


VM = pl.BlockSpec(memory_space=pltpu.VMEM)
SM = pl.BlockSpec(memory_space=pltpu.SMEM)
HB = pl.BlockSpec(memory_space=pl.ANY)
PARAMS = pltpu.CompilerParams(vmem_limit_bytes=VMEM_DOWN)


def buffers(rows, tiles, names):
    planes = {"data": NP, "coef": 8 * NC}
    return [pltpu.VMEM((rows, tiles, planes.get(name, 32), LANES), F32) for name in names]


def per_device(misfit, viscosity, friction, ice_mask, grounded):
    rows, columns = friction.shape
    gx, gy = lax.axis_index("gx"), lax.axis_index("gy")
    nx, ny = lax.axis_size("gx"), lax.axis_size("gy")
    upward = [(i, i + 1) for i in range(nx - 1)]
    downward = [(i + 1, i) for i in range(nx - 1)]

    def beside(strips):
        every = lax.all_gather(strips, "gy", axis=0)
        left = lax.dynamic_index_in_dim(every, jnp.maximum(gy - 1, 0), 0, keepdims=False)[1]
        right = lax.dynamic_index_in_dim(every, jnp.minimum(gy + 1, ny - 1), 0, keepdims=False)[0]
        return jnp.where(gy > 0, left, 0.0), jnp.where(gy < ny - 1, right, 0.0)

    data0, strips0, edges0 = pl.pallas_call(
        arrange_kernel,
        out_shape=(shape(rows, 2, NP, LANES), shape(2, NP + 16, LANES), shape(2, 16, LANES)),
        in_specs=[HB] * 5,
        out_specs=(VM, VM, VM),
        scratch_shapes=[
            pltpu.VMEM((4, 16, PITCH, LANES), F32),
            pltpu.VMEM((4, 8, PITCH, LANES), F32),
            pltpu.VMEM((rows, columns), F32),
            pltpu.VMEM((rows, columns), jnp.int32),
            pltpu.VMEM((rows, columns), jnp.int32),
            pltpu.SemaphoreType.DMA((11,)),
        ],
        compiler_params=PARAMS,
        name="arrange",
    )(
        *in_hbm(
            [v.reshape(-1, 2, rows, columns) for v in (misfit, viscosity)] + [friction, ice_mask, grounded]
        )
    )
    left, right = beside(strips0)
    inner = RIM0 - 1

    def face0(which, first, first_inner):
        corner = slice(NP + 8 * which, NP + 8 * which + 8)
        parts = (
            data0[first_inner : first_inner + inner, :, 0:32],
            data0[first : first + RIM0, :, 32:48],
            edges0[which],
            left[corner],
            right[corner],
        )
        return jnp.concatenate([v.reshape(-1, LANES) for v in parts], 0)

    low_face = face0(0, 0, 0)
    high_face = face0(1, rows - RIM0, rows - inner)
    from_low = lax.ppermute(high_face, "gx", upward)
    from_high = lax.ppermute(low_face, "gx", downward)

    total0 = rows + 2 * RIM0
    names = ("data", "diag", "slope", "across", "w", "coef", "scaled")
    rows1 = rows // 2
    group = LANES // STRIP1
    field0 = stored(total0, 3, 32, LANES)
    inner1 = RIM1 - 1
    data1, strips1, edges1, w0, coef0, scaled0 = pl.pallas_call(
        down0_kernel,
        out_shape=(
            shape(rows1, NP, LANES),
            shape(2, rows1 // group, NP, LANES),
            shape(2, 2 * inner1, LANES),
            field0,
            stored(total0, 3, 8 * NC, LANES),
            field0,
        ),
        in_specs=[VM] * 5,
        out_specs=(VM, VM, VM, HB, HB, HB),
        scratch_shapes=buffers(total0, 3, names) + [pltpu.SemaphoreType.DMA((4,))],
        compiler_params=PARAMS,
        name="down0",
    )(data0, left, right, from_low, from_high)

    left, right = beside(strips1)
    left, right = left.reshape(-1, LANES), right.reshape(-1, LANES)

    def face1(which, first, first_inner):
        parts = (
            data1[first_inner : first_inner + inner1, 0:32],
            data1[first : first + RIM1, 32:48],
            edges1[which],
            left,
            right,
        )
        return jnp.concatenate([v.reshape(-1, LANES) for v in parts], 0)

    low_face = face1(0, 0, 0)
    high_face = face1(1, rows1 - RIM1, rows1 - inner1)
    from_low = lax.ppermute(high_face, "gx", upward)
    from_high = lax.ppermute(low_face, "gx", downward)

    total1 = rows1 + 2 * RIM1
    rows2 = rows1 // 2
    total2 = rows2 + 2 * RIM2
    field1 = stored(total1, 2, 32, LANES)
    field2 = stored(total2, 1, 32, LANES)
    piece, w1, coef1, scaled1, w2, coef2, scaled2 = pl.pallas_call(
        down12_kernel,
        out_shape=(
            shape(nx, NP, LANES),
            field1,
            stored(total1, 2, 8 * NC, LANES),
            field1,
            field2,
            stored(total2, 1, 8 * NC, LANES),
            field2,
        ),
        in_specs=[VM] * 5,
        out_specs=(VM,) + (HB,) * 6,
        scratch_shapes=buffers(total1, 2, names) + buffers(total2, 1, names) + [pltpu.SemaphoreType.DMA((6,))],
        compiler_params=PARAMS,
        name="down12",
    )(data1, left, right, from_low, from_high)

    pieces = lax.all_gather(lax.all_to_all(piece, "gx", 0, 0), "gy", axis=0)

    rows3 = rows2 // 2
    total3 = nx * rows3 + 2 * RIM3
    ups = ("w", "coef", "scaled", "w", "w")
    result = pl.pallas_call(
        up_kernel,
        out_shape=shape(16, 2, rows, columns),
        in_specs=[SM, VM] + [HB] * 9,
        out_specs=HB,
        scratch_shapes=buffers(total3, 1, ("data", "coef", "scaled", "w", "w", "slope", "across"))
        + buffers(total2, 1, ups)
        + buffers(total1, 2, ups)
        + buffers(total0, 3, ups)
        + buffers(max(total0, total1), 3, ("slope", "across"))
        + [pltpu.VMEM((4, 16, PITCH, LANES), F32), pltpu.SemaphoreType.DMA((9,))],
        compiler_params=pltpu.CompilerParams(vmem_limit_bytes=VMEM_UP),
        name="up",
    )(
        jnp.stack([gx, gy]).astype(jnp.int32),
        pieces,
        *in_hbm([w0, coef0, scaled0, w1, coef1, scaled1, w2, coef2, scaled2]),
    )
    return result.reshape(misfit.shape)


def solution(mesh):
    placed = (
        P(None, None, "gx", "gy"),
        P(None, "gx", "gy"),
        P("gx", "gy"),
        P("gx", "gy"),
        P("gx", "gy"),
    )
    return jax.shard_map(
        per_device, mesh=mesh, in_specs=placed, out_specs=P(None, None, "gx", "gy"), check_vma=False
    )
```

```python
import functools

import jax
import jax.numpy as jnp
from jax import lax
from jax.experimental import pallas as pl
from jax.experimental.pallas import tpu as pltpu
from jax.sharding import PartitionSpec as P

LEVELS = 4
COARSE_ITERS = 20
OMEGA = 0.6
CROSS = 0.75
NP = 56
LANES = 128
RIM0 = 4
RIM1 = 13
RIM2 = 6
RIM3 = 2
STRIP1 = 16
NC = 15
PITCH = 40
SPAN = 11
VMEM_DOWN = 28 * 1024 * 1024
VMEM_UP = 60 * 1024 * 1024
F32 = jnp.float32
UNROLL0 = (18, 6, 4)
UNROLL1 = (38, 12, 8)
UNROLL2 = (18, 6, 4)
UNROLL3 = (32, 32, 8)
UNROLL0_UP = (18, 17)
UNROLL1_UP = (22, 20)
UNROLL_MOVE = 8


def rows_loop(first, last, body, unroll):
    count = (last - first) // unroll

    def step(i, carry):
        for j in range(unroll):
            body(first + i * unroll + j)
        return carry

    if count:
        lax.fori_loop(0, count, step, 0)
    for r in range(first + count * unroll, last):
        body(r)


def lane_ids(rows=8):
    return lax.broadcasted_iota(jnp.int32, (rows, LANES), 1)


def shifted(tiles, closed):
    lane = lax.broadcasted_iota(jnp.int32, tiles[0].shape, 1)
    up = [pltpu.roll(v, LANES - 1, 1) for v in tiles]
    down = [pltpu.roll(v, 1, 1) for v in tiles]
    n = len(tiles)
    if closed:
        zero = jnp.zeros_like(tiles[0])
        return (
            [jnp.where(lane == LANES - 1, zero, v) for v in up],
            [jnp.where(lane == 0, zero, v) for v in down],
        )
    if n == 1:
        return up, down
    return (
        [jnp.where(lane == LANES - 1, up[(t + 1) % n], up[t]) for t in range(n)],
        [jnp.where(lane == 0, down[(t - 1) % n], down[t]) for t in range(n)],
    )


def twice(v):
    return jnp.concatenate([v, v], 0)


def make_coefs(data, coef, scaled, diag, first, last, horizontal, closed, unroll):
    nt = data.shape[1]
    sub = lax.broadcasted_iota(jnp.int32, (8, LANES), 0)

    def row(r):
        mids = [data[r, t, 32:48, :] for t in range(nt)]
        norths, souths = shifted(mids, closed)
        for t in range(nt):
            mid = mids[t]
            west = (0.5 * horizontal) * (mid + data[r - 1, t, 32:48, :])
            east = (0.5 * horizontal) * (mid + data[r + 1, t, 32:48, :])
            north = (0.5 * horizontal) * (mid + norths[t])
            south = (0.5 * horizontal) * (mid + souths[t])
            low, high = mid[:8], mid[8:]
            inner = 2.0 * (low + high)
            outer = jnp.where(sub == 7, 0.0, 2.0 * (high + pltpu.roll(low, 7, 0)))
            outer_down = pltpu.roll(outer, 1, 0)
            coef[r, t, 0:16, :] = west
            coef[r, t, 16:32, :] = north
            coef[r, t, 32:48, :] = south
            coef[r, t, 48:64, :] = (CROSS * horizontal) * mid
            coef[r, t, 64:72, :] = inner
            coef[r, t, 72:80, :] = outer
            coef[r, t, 80:88, :] = outer_down
            ice = data[r, t, 48:49, :]
            drag = data[r, t, 49:50, :]
            bottom = jnp.where(sub == 0, drag, 0.0)
            upright = jnp.concatenate([inner + outer_down + bottom, inner + outer], 0)
            along_x = east + west
            along_y = north + south
            rest = 1.0 - ice
            for c, lateral in enumerate((4.0 * along_x + along_y, along_x + 4.0 * along_y)):
                diagonal = ice * (lateral + upright) + rest
                inverse = OMEGA / diagonal
                coef[r, t, 88 + 16 * c : 104 + 16 * c, :] = ice * inverse
                scaled[r, t, 16 * c : 16 * c + 16, :] = inverse * data[r, t, 16 * c : 16 * c + 16, :]
                if diag is not None:
                    diag[r, t, 16 * c : 16 * c + 16, :] = diagonal

    rows_loop(first, last, row, unroll)


def prepare(w, coef, slope, across, first, last, closed, unroll):
    nt = w.shape[1]

    def row(r):
        norths, souths = shifted([w[r, t] for t in range(nt)], closed)
        for t in range(nt):
            slope[r, t] = norths[t] - souths[t]
            across[r, t] = twice(coef[r, t, 16:32, :]) * norths[t] + twice(coef[r, t, 32:48, :]) * souths[t]

    rows_loop(first, last, row, unroll)


def off_diagonal(w, coef, slope, across, r, t):
    here = w[r, t]
    along = twice(coef[r + 1, t, 0:16, :]) * w[r + 1, t] + twice(coef[r, t, 0:16, :]) * w[r - 1, t]
    side = across[r, t]
    mixed = slope[r + 1, t] - slope[r - 1, t]
    cross = coef[r, t, 48:64, :]
    inner = coef[r, t, 64:72, :]
    outer = coef[r, t, 72:80, :]
    outer_down = coef[r, t, 80:88, :]
    parts = []
    for c in range(2):
        mine = slice(16 * c, 16 * c + 16)
        other = slice(16 - 16 * c, 32 - 16 * c)
        low, high = here[16 * c : 16 * c + 8], here[16 * c + 8 : 16 * c + 16]
        column = jnp.concatenate(
            [inner * high + outer_down * pltpu.roll(high, 1, 0), inner * low + outer * pltpu.roll(low, 7, 0)], 0
        )
        if c == 0:
            lateral = 4.0 * along[mine] + side[mine]
        else:
            lateral = along[mine] + 4.0 * side[mine]
        parts.append(lateral + cross * mixed[other] + column)
    return here, jnp.concatenate(parts, 0)


def sweep(w, new, coef, scaled, slope, across, first, last, closed, unroll, tiles=None, emit=None):
    look, unroll = unroll[:2]
    nt = w.shape[1]
    prepare(w, coef, slope, across, first - 1, last + 1, closed, look)

    def row(r):
        for t in range(nt if tiles is None else tiles):
            here, total = off_diagonal(w, coef, slope, across, r, t)
            value = (1.0 - OMEGA) * here + scaled[r, t] + coef[r, t, 88:120, :] * total
            if emit is None:
                new[r, t] = value
            else:
                emit(r, t, value)

    rows_loop(first, last, row, unroll)


def remainders(w, out, data, diag, coef, slope, across, first, last, unroll, tiles):
    look, unroll = unroll[:2]
    prepare(w, coef, slope, across, first - 1, last + 1, False, look)

    def row(r):
        for t in range(tiles):
            here, total = off_diagonal(w, coef, slope, across, r, t)
            out[r, t] = data[r, t, 0:32, :] + data[r, t, 48:49, :] * total - diag[r, t] * here

    rows_loop(first, last, row, unroll)


def gather_lanes(v, index):
    return jnp.take_along_axis(v, index, axis=1, mode="promise_in_bounds")


def halve(first, second):
    lane = lax.broadcasted_iota(jnp.int32, first.shape, 1)
    even = (2 * lane) % LANES
    low = gather_lanes(first + pltpu.roll(first, LANES - 1, 1), even)
    if second is None:
        return low
    high = gather_lanes(second + pltpu.roll(second, LANES - 1, 1), even)
    return jnp.where(lane < LANES // 2, low, high)


def restrict_row(source, planes, r):
    both = [source[r, t, planes, :] + source[r + 1, t, planes, :] for t in range(min(2, source.shape[1]))]
    return 0.25 * halve(both[0], both[1] if len(both) > 1 else None)


def prolong_row(tiles, fine_tiles):
    lane = lax.broadcasted_iota(jnp.int32, tiles[0].shape, 1)
    low = lane // 2
    high = LANES // 2 + lane // 2
    first = tiles[0]
    last = tiles[-1]
    out = [gather_lanes(first, low)]
    if fine_tiles == 2:
        out.append(gather_lanes(first, high))
    else:
        out.append(gather_lanes(first, high))
        out.append(gather_lanes(last, jnp.where(lane < LANES // 2, low, high)))
    return out


def put(strip, v, shift, width, at):
    lane = lax.broadcasted_iota(jnp.int32, v.shape, 1)
    rolled = pltpu.roll(v, shift % LANES, 1) if shift % LANES else v
    return jnp.where((lane >= at) & (lane < at + width), rolled, strip)


def unpack_rim(left, right, at, width):
    lane = lax.broadcasted_iota(jnp.int32, left.shape, 1)
    to_low = pltpu.roll(right, (LANES - at) % LANES, 1) if at else right
    shift = (2 * LANES - width - at) % LANES
    to_high = pltpu.roll(left, shift, 1) if shift else left
    return jnp.where(lane < LANES // 2, to_low, to_high)


def pair_rows(tiles):
    sub = lax.broadcasted_iota(jnp.int32, (8, LANES), 0)
    out = tiles[0]
    for j in range(1, len(tiles)):
        out = jnp.where(sub >= 2 * j, pltpu.roll(tiles[j], 2 * j, 0), out)
    return out


def pair_row(tile, j):
    return pltpu.roll(tile, 8 - 2 * j, 0) if j else tile


def copy_rows(source, target, sem, first, last):
    rows = pl.ds(first, last - first)
    copy = pltpu.make_async_copy(source.at[rows], target.at[rows], sem)
    copy.start()
    return copy


def arrange_kernel(misfit, viscosity, friction_in, ice_mask_in, grounded_in, data, strips, edges,
                   misfit_half, viscosity_half, friction, ice_mask, grounded, sems):
    rows = friction.shape[0]
    copies = [
        pltpu.make_async_copy(source, target, sems.at[n])
        for n, (source, target) in enumerate(((friction_in, friction), (ice_mask_in, ice_mask), (grounded_in, grounded)))
    ]
    for t in range(2):
        lanes = pl.ds(t * LANES, LANES)
        for p in range(2):
            n = 2 * t + p
            for source, target, sem in ((misfit, misfit_half, 3 + n), (viscosity, viscosity_half, 7 + n)):
                copies.append(
                    pltpu.make_async_copy(source.at[:, p, :, lanes], target.at[n, :, pl.ds(0, rows)], sems.at[sem])
                )
    for copy in copies:
        copy.start()
    for copy in copies:
        copy.wait()
    sub = lax.broadcasted_iota(jnp.int32, (8, LANES), 0)
    misfit_rows = misfit_half.reshape(4, -1, LANES)
    viscosity_rows = viscosity_half.reshape(4, -1, LANES)

    def eight(i, carry):
        block = pl.ds(pl.multiple_of(8 * i, 8), 8)
        for t in range(2):
            lanes = pl.ds(t * LANES, LANES)
            ices = ice_mask[block, lanes].astype(F32)
            drags = friction[block, lanes] * grounded[block, lanes].astype(F32)
            for j in range(8):
                r = 8 * i + j
                ice, drag = ices[j : j + 1], drags[j : j + 1]
                for c in range(2):
                    for p in range(2):
                        v = misfit_rows[2 * t + p, pl.ds(8 * c * PITCH + r, 8, stride=PITCH), :]
                        data[r, t, 16 * c + 8 * p : 16 * c + 8 * p + 8, :] = v * ice
                for p in range(2):
                    data[r, t, 32 + 8 * p : 40 + 8 * p, :] = viscosity_rows[2 * t + p, pl.ds(r, 8, stride=PITCH), :]
                data[r, t, 48:56, :] = jnp.where(sub == 0, ice, jnp.where(sub == 1, drag, 0.0))
        return carry

    lax.fori_loop(0, rows // 8, eight, 0)
    corner = RIM0 * RIM0
    for side in range(2):
        low = jnp.zeros((8, LANES), F32)
        high = low
        for first in range(0, NP, 8):
            planes = slice(first, first + 8)
            strip = jnp.zeros((8, LANES), F32)
            for r in range(rows):
                at = r * RIM0
                strip = put(strip, data[r, side, planes, :], at if side == 0 else at + RIM0, RIM0, at)
            strips[side, planes, :] = strip
            at = first // 8 * corner
            low = put(low, strip, at, corner, at)
            high = put(high, strip, at + corner, corner, at)
        strips[side, NP : NP + 8, :] = low
        strips[side, NP + 8 : NP + 16, :] = high
    for t in range(2):
        edges[0, 8 * t : 8 * t + 8, :] = pair_rows([data[r, t, 48:56, :] for r in range(RIM0 - 1)])
        edges[1, 8 * t : 8 * t + 8, :] = pair_rows([data[rows - RIM0 + 1 + r, t, 48:56, :] for r in range(RIM0 - 1)])


def inner0_kernel(own, left, right, coarse, w_out, coef_out, scaled_out, data, diag, slope, across, wa, coef, scaled, sems):
    rows = own.shape[0]
    first, last = RIM0, RIM0 + rows

    def copy_row(r):
        for t in range(2):
            data[first + r, t] = own[r, t]

    rows_loop(0, rows, copy_row, 4)
    for r in range(rows):
        data[first + r, 2] = unpack_rim(left[0:NP, :], right[0:NP, :], r * RIM0, RIM0)
    half = first + rows // 2 - 1
    make_coefs(data, coef, scaled, diag, first + 1, half, 1.0, False, UNROLL0[2])
    copies = [copy_rows(coef, coef_out, sems.at[0], first + 1, half)]
    make_coefs(data, coef, scaled, diag, half, last - 1, 1.0, False, UNROLL0[2])
    copies.append(copy_rows(coef, coef_out, sems.at[1], half, last - 1))
    copies.append(copy_rows(scaled, scaled_out, sems.at[2], first + 1, last - 1))
    sweep(scaled, wa, coef, scaled, slope, across, first + 2, last - 2, False, UNROLL0)
    copies.append(copy_rows(wa, w_out, sems.at[3], first + 2, last - 2))

    def coefs_row(i):
        coarse[i, 32:56, :] = restrict_row(data, slice(32, 56), first + 2 * i)

    rows_loop(0, rows // 2, coefs_row, UNROLL_MOVE)
    remainders(wa, diag, data, diag, coef, slope, across, first + 3, last - 3, UNROLL0, 2)

    def target_row(i):
        coarse[i, 0:32, :] = restrict_row(diag, slice(0, 32), first + 2 * i)

    rows_loop(2, rows // 2 - 2, target_row, UNROLL_MOVE)
    for copy in copies:
        copy.wait()


def outer0_kernel(own, left, right, from_low, from_high, inner_coarse, w_in, coef_in, scaled_in,
                  coarse, strips1, edges1, w_out, coef_out, scaled_out,
                  data, diag, slope, across, wa, coef, scaled, sems):
    rows = own.shape[0]
    mine = SPAN - RIM0
    inner = RIM0 - 1
    thick = 64 * inner
    thin = thick + 32 * RIM0
    corner = thin + 16
    copies = []
    for face, start, rim_at, mine_at, x in (
        (from_low, 0, 0, RIM0, 0),
        (from_high, SPAN, SPAN + mine, SPAN, rows - mine),
    ):
        for r in range(mine):
            for t in range(2):
                data[mine_at + r, t] = own[x + r, t]
            data[mine_at + r, 2] = unpack_rim(left[0:NP, :], right[0:NP, :], (x + r) * RIM0, RIM0)
        skip = 1 if start == 0 else 0
        for t in range(2):
            for r in range(inner):
                at = 32 * (2 * r + t)
                data[rim_at + skip + r, t, 0:32, :] = face[at : at + 32, :]
                data[rim_at + skip + r, t, 48:56, :] = pair_row(face[thin + 8 * t : thin + 8 * t + 8, :], r)
            for r in range(RIM0):
                at = thick + 16 * (2 * r + t)
                data[rim_at + r, t, 32:48, :] = face[at : at + 16, :]
        for q in range(NP // 8):
            for r in range(RIM0):
                at = RIM0 * (RIM0 * q + r)
                data[rim_at + r, 2, 8 * q : 8 * q + 8, :] = unpack_rim(
                    face[corner : corner + 8, :], face[corner + 8 : corner + 16, :], at, RIM0
                )
    for start in (0, SPAN):
        make_coefs(data, coef, scaled, diag, start + 1, start + SPAN - 1, 1.0, False, 9)
    total = rows + 2 * RIM0
    shift = total - 2 * SPAN
    ranges = ((2, RIM0 + 1), (3, RIM0 + 1), (2, RIM0 + 2))
    arrays = ((coef, coef_out), (scaled, scaled_out), (wa, w_out))

    def store(n):
        (source, target), (low, high) = arrays[n], ranges[n]
        for side in range(2):
            begin = low if side == 0 else 2 * SPAN - high
            place = begin + (0 if side == 0 else shift)
            copy = pltpu.make_async_copy(
                source.at[pl.ds(begin, high - low)], target.at[pl.ds(place, high - low)], sems.at[2 * n + side]
            )
            copy.start()
            copies.append(copy)

    store(0)
    store(1)
    for start in (0, SPAN):
        sweep(scaled, wa, coef, scaled, slope, across, start + 2, start + SPAN - 2, False, (9, 7))
    store(2)

    def copy_coarse(i):
        coarse[i] = inner_coarse[i]

    rows_loop(0, rows // 2, copy_coarse, 4)
    for start in (0, SPAN):
        remainders(wa, diag, data, diag, coef, slope, across, start + 3, start + SPAN - 3, (7, 5), 2)
    for i in range(2):
        coarse[i, 0:32, :] = restrict_row(diag, slice(0, 32), RIM0 + 2 * i)
        coarse[rows // 2 - 2 + i, 0:32, :] = restrict_row(diag, slice(0, 32), SPAN + mine - 4 + 2 * i)
    group = LANES // STRIP1
    for side in range(2):
        for part in range(rows // 2 // group):
            for first in range(0, NP, 8):
                planes = slice(first, first + 8)
                strip = jnp.zeros((8, LANES), F32)
                for j in range(group):
                    at = j * STRIP1
                    shift1 = at if side == 0 else at + STRIP1
                    strip = put(strip, coarse[part * group + j, planes, :], shift1, STRIP1, at)
                strips1[side, part, planes, :] = strip
    inner1 = RIM1 - 1
    for face, base in enumerate((0, rows // 2 - inner1)):
        for j in range(0, inner1, 4):
            edges1[face, 2 * j : 2 * j + 8, :] = pair_rows([coarse[base + j + n, 48:56, :] for n in range(4)])
    for copy in copies:
        copy.wait()


def down12_kernel(own, left, right, from_low, from_high, piece, w1_out, coef1_out, scaled1_out, w2_out, coef2_out, scaled2_out,
                  data1, diag1, slope1, across1, wa1, coef1, scaled1, data2, diag2, slope2, across2, wa2, coef2, scaled2, sems):
    rows = own.shape[0]
    total = rows + 2 * RIM1
    group = LANES // STRIP1
    parts = rows // group

    def rim(low, high, base, r):
        part, j = r // group, r % group
        at = base + part * NP
        return unpack_rim(low[at : at + NP, :], high[at : at + NP, :], j * STRIP1, STRIP1)

    def copy_row(r):
        data1[RIM1 + r, 0] = own[r]

    rows_loop(0, rows, copy_row, 4)
    for r in range(rows):
        data1[RIM1 + r, 1] = rim(left, right, 0, r)
    inner = RIM1 - 1
    thick = 32 * inner
    thin = thick + 16 * RIM1
    corner = thin + 2 * inner
    for face, base, skip, first in ((from_low, 0, 1, rows - RIM1), (from_high, RIM1 + rows, 0, 0)):
        for r in range(inner):
            data1[base + skip + r, 0, 0:32, :] = face[32 * r : 32 * r + 32, :]
            at = thin + 8 * (r // 4)
            data1[base + skip + r, 0, 48:56, :] = pair_row(face[at : at + 8, :], r % 4)
        for r in range(RIM1):
            at = thick + 16 * r
            data1[base + r, 0, 32:48, :] = face[at : at + 16, :]
            data1[base + r, 1] = rim(face, face.at[pl.ds(parts * NP, face.shape[0] - parts * NP)], corner, first + r)

    make_coefs(data1, coef1, scaled1, diag1, 1, total - 1, 0.25, False, UNROLL1[2])
    copies = [copy_rows(coef1, coef1_out, sems.at[0], 10, total - 10)]
    copies.append(copy_rows(scaled1, scaled1_out, sems.at[1], 11, total - 11))
    sweep(scaled1, wa1, coef1, scaled1, slope1, across1, 2, total - 2, False, UNROLL1)
    copies.append(copy_rows(wa1, w1_out, sems.at[2], 9, total - 9))
    remainders(wa1, diag1, data1, diag1, coef1, slope1, across1, 3, total - 3, UNROLL1, 2)

    rows2 = rows // 2
    total2 = rows2 + 2 * RIM2

    def coefs_row(i):
        data2[i, 0, 32:56, :] = restrict_row(data1, slice(32, 56), 1 + 2 * i)

    rows_loop(0, total2, coefs_row, UNROLL_MOVE)

    def target_row(i):
        data2[i, 0, 0:32, :] = restrict_row(diag1, slice(0, 32), 1 + 2 * i)

    rows_loop(1, total2 - 1, target_row, UNROLL_MOVE)

    make_coefs(data2, coef2, scaled2, diag2, 1, total2 - 1, 0.0625, False, UNROLL2[2])
    copies.append(copy_rows(coef2, coef2_out, sems.at[3], 2, total2 - 2))
    copies.append(copy_rows(scaled2, scaled2_out, sems.at[4], 3, total2 - 3))
    sweep(scaled2, wa2, coef2, scaled2, slope2, across2, 2, total2 - 2, False, UNROLL2)
    copies.append(copy_rows(wa2, w2_out, sems.at[5], 2, total2 - 2))
    remainders(wa2, diag2, data2, diag2, coef2, slope2, across2, RIM2, RIM2 + rows2, UNROLL2, 1)

    rows3 = rows2 // 2
    width = LANES // rows3
    for first in range(0, NP, 8):
        planes = slice(first, first + 8)
        source = diag2 if first < 32 else data2
        strip = jnp.zeros((8, LANES), F32)
        for i in range(rows3):
            strip = put(strip, restrict_row(source, planes, RIM2 + 2 * i), i * width, width, i * width)
        for d in range(piece.shape[0]):
            piece[d, planes, :] = strip
    for copy in copies:
        copy.wait()


def up_kernel(place, pieces, w0_in, coef0_in, scaled0_in, w1_in, coef1_in, scaled1_in, w2_in, coef2_in, scaled2_in, result,
              data3, coef3, scaled3, wa3, wb3, slope3, across3, w2, coef2, scaled2, wa2, wb2, w1, coef1, scaled1, wa1, wb1,
              w0, coef0, scaled0, wa0, wb0, slope0, across0, result_half, sems):
    slope1, across1 = (v.at[pl.ds(0, wa1.shape[0]), pl.ds(0, 2)] for v in (slope0, across0))
    slope2, across2 = (v.at[pl.ds(0, wa2.shape[0]), pl.ds(0, 1)] for v in (slope0, across0))
    copies = []
    for source, target, first in (
        (w2_in, w2, 2), (coef2_in, coef2, 2), (scaled2_in, scaled2, 3),
        (w1_in, w1, 9), (coef1_in, coef1, 10), (scaled1_in, scaled1, 11),
        (w0_in, w0, 2), (coef0_in, coef0, 2), (scaled0_in, scaled0, 3),
    ):
        copies.append(copy_rows(source, target, sems.at[len(copies)], first, source.shape[0] - first))
    devices_y, devices_x = pieces.shape[0], pieces.shape[1]
    rows3 = devices_y
    width = LANES // devices_y
    whole = devices_x * rows3
    zero = jnp.zeros((NP, LANES), F32)
    for r in range(RIM3):
        for end in (r, RIM3 + whole + r):
            data3[end, 0] = zero
            wa3[end, 0] = zero[:32]
            wb3[end, 0] = zero[:32]
            scaled3[end, 0] = zero[:32]
            slope3[end, 0] = zero[:32]
            coef3[end, 0] = jnp.zeros((8 * NC, LANES), F32)

    def assemble(d, carry):
        for i in range(rows3):
            line = jnp.zeros((NP, LANES), F32)
            for j in range(devices_y):
                line = put(line, pieces[j, d], (j - i) * width, width, j * width)
            data3[RIM3 + d * rows3 + i, 0] = line
        return carry

    lax.fori_loop(0, devices_x, assemble, 0)
    first, last = RIM3, RIM3 + whole
    make_coefs(data3, coef3, scaled3, None, first, last, 0.25 ** (LEVELS - 1), True, UNROLL3[2])

    gx, gy = place[0], place[1]

    def coarse_sweep(source, target, extent):
        begin, end = (first, last) if extent is None else (0, extent)
        start = 0 if extent is None else first + jnp.clip(gx * rows3 - (extent - rows3) // 2, 0, whole - extent)
        around = 0 if extent is None else 1

        def look(r):
            r = start + r
            norths, souths = shifted([source[r, 0]], True)
            slope3[r, 0] = norths[0] - souths[0]
            across3[r, 0] = twice(coef3[r, 0, 16:32, :]) * norths[0] + twice(coef3[r, 0, 32:48, :]) * souths[0]

        rows_loop(begin - around, end + around, look, UNROLL3[0] if extent is None else extent + 2)

        def row(r):
            r = start + r
            here, total = off_diagonal(source, coef3, slope3, across3, r, 0)
            target[r, 0] = (1.0 - OMEGA) * here + scaled3[r, 0] + coef3[r, 0, 88:120, :] * total

        rows_loop(begin, end, row, UNROLL3[1])

    coarse_sweep(scaled3, wa3, None)
    done = 2
    narrow = [(None, COARSE_ITERS - 9), (rows3 + 20, COARSE_ITERS - 5), (rows3 + 12, COARSE_ITERS)]
    buffers = (wa3, wb3)
    for extent, until in narrow:
        if extent is not None and extent > whole:
            extent = None

        def two_sweeps(i, carry, extent=extent, pair=buffers):
            coarse_sweep(pair[0], pair[1], extent)
            coarse_sweep(pair[1], pair[0], extent)
            return carry

        if (until - done) // 2:
            lax.fori_loop(0, (until - done) // 2, two_sweeps, 0)
        if (until - done) % 2:
            coarse_sweep(buffers[0], buffers[1], extent)
            buffers = buffers[::-1]
        done = until
    solved = buffers[0]

    lane = lane_ids(32)
    y = jnp.where(lane < 96, lane, lane - LANES)
    column = gy * width + (y + LANES) // 2 - LANES // 2
    inside = (column >= 0) & (column < LANES)
    pick = jnp.where(inside, column, 0)

    for copy in copies[:3]:
        copy.wait()
    rows2 = 2 * rows3
    for i in range(rows3 + 2 * RIM3):
        add = jnp.where(inside, gather_lanes(solved[gx * rows3 + i, 0], pick), 0.0)
        for r in (2 * i + 2, 2 * i + 3):
            wa2[r, 0] = w2[r, 0] + add
    total2 = rows2 + 2 * RIM2
    sweep(wa2, wb2, coef2, scaled2, slope2, across2, 3, total2 - 3, False, UNROLL2)
    sweep(wb2, wa2, coef2, scaled2, slope2, across2, 4, total2 - 4, False, UNROLL2)


    for copy in copies[3:6]:
        copy.wait()

    def add1(r):
        adds = prolong_row([wa2[r, 0]], 2)
        for t in range(2):
            for fine in (2 * r + 1, 2 * r + 2):
                wa1[fine, t] = w1[fine, t] + adds[t]

    rows_loop(4, total2 - 4, add1, UNROLL_MOVE)
    total1 = 2 * rows2 + 2 * RIM1
    sweep(wa1, wb1, coef1, scaled1, slope1, across1, 11, total1 - 11, False, UNROLL1_UP)
    sweep(wb1, wa1, coef1, scaled1, slope1, across1, 12, total1 - 12, False, UNROLL1_UP)


    for copy in copies[6:]:
        copy.wait()

    def add0(r):
        adds = prolong_row([wa1[r, t] for t in range(2)], 3)
        for t in range(3):
            for fine in (2 * r - 22, 2 * r - 21):
                wa0[fine, t] = w0[fine, t] + adds[t]

    rows_loop(12, total1 - 12, add0, UNROLL_MOVE)
    rows0 = 4 * rows2
    total0 = rows0 + 2 * RIM0
    sweep(wa0, wb0, coef0, scaled0, slope0, across0, 3, total0 - 3, False, UNROLL0_UP)

    result_rows = result_half.reshape(4, -1, LANES)

    def emit(r, t, value):
        for c in range(2):
            for p in range(2):
                start = 8 * c * PITCH + r - RIM0
                result_rows[2 * t + p, pl.ds(start, 8, stride=PITCH), :] = value[16 * c + 8 * p : 16 * c + 8 * p + 8]

    sweep(wb0, None, coef0, scaled0, slope0, across0, RIM0, RIM0 + rows0, False, UNROLL0_UP, tiles=2, emit=emit)
    copies = [
        pltpu.make_async_copy(
            result_half.at[2 * t + p, :, pl.ds(0, rows0)], result.at[:, p, :, pl.ds(t * LANES, LANES)], sems.at[2 * t + p]
        )
        for t in range(2)
        for p in range(2)
    ]
    for copy in copies:
        copy.start()
    for copy in copies:
        copy.wait()


def shape(*dims):
    return jax.ShapeDtypeStruct(dims, F32)


def stored(*dims):
    return pltpu.HBM(dims, F32)


def in_hbm(arrays):
    return [pltpu.with_memory_space_constraint(v, pltpu.HBM) for v in arrays]


VM = pl.BlockSpec(memory_space=pltpu.VMEM)
SM = pl.BlockSpec(memory_space=pltpu.SMEM)
HB = pl.BlockSpec(memory_space=pl.ANY)
PARAMS = pltpu.CompilerParams(vmem_limit_bytes=VMEM_DOWN)


def buffers(rows, tiles, names):
    planes = {"data": NP, "coef": 8 * NC}
    return [pltpu.VMEM((rows, tiles, planes.get(name, 32), LANES), F32) for name in names]


def per_device(misfit, viscosity, friction, ice_mask, grounded):
    rows, columns = friction.shape
    gx, gy = lax.axis_index("gx"), lax.axis_index("gy")
    nx, ny = lax.axis_size("gx"), lax.axis_size("gy")
    upward = [(i, i + 1) for i in range(nx - 1)]
    downward = [(i + 1, i) for i in range(nx - 1)]

    def beside(strips):
        every = lax.all_gather(strips, "gy", axis=0)
        left = lax.dynamic_index_in_dim(every, jnp.maximum(gy - 1, 0), 0, keepdims=False)[1]
        right = lax.dynamic_index_in_dim(every, jnp.minimum(gy + 1, ny - 1), 0, keepdims=False)[0]
        return jnp.where(gy > 0, left, 0.0), jnp.where(gy < ny - 1, right, 0.0)

    data0, strips0, edges0 = pl.pallas_call(
        arrange_kernel,
        out_shape=(shape(rows, 2, NP, LANES), shape(2, NP + 16, LANES), shape(2, 16, LANES)),
        in_specs=[HB] * 5,
        out_specs=(VM, VM, VM),
        scratch_shapes=[
            pltpu.VMEM((4, 16, PITCH, LANES), F32),
            pltpu.VMEM((4, 8, PITCH, LANES), F32),
            pltpu.VMEM((rows, columns), F32),
            pltpu.VMEM((rows, columns), jnp.int32),
            pltpu.VMEM((rows, columns), jnp.int32),
            pltpu.SemaphoreType.DMA((11,)),
        ],
        compiler_params=PARAMS,
        name="arrange",
    )(
        *in_hbm(
            [v.reshape(-1, 2, rows, columns) for v in (misfit, viscosity)] + [friction, ice_mask, grounded]
        )
    )
    left, right = beside(strips0)
    inner = RIM0 - 1

    def face0(which, first, first_inner):
        corner = slice(NP + 8 * which, NP + 8 * which + 8)
        parts = (
            data0[first_inner : first_inner + inner, :, 0:32],
            data0[first : first + RIM0, :, 32:48],
            edges0[which],
            left[corner],
            right[corner],
        )
        return jnp.concatenate([v.reshape(-1, LANES) for v in parts], 0)

    low_face = face0(0, 0, 0)
    high_face = face0(1, rows - RIM0, rows - inner)
    from_low = lax.ppermute(high_face, "gx", upward)
    from_high = lax.ppermute(low_face, "gx", downward)

    total0 = rows + 2 * RIM0
    names = ("data", "diag", "slope", "across", "w", "coef", "scaled")
    rows1 = rows // 2
    group = LANES // STRIP1
    field0 = stored(total0, 3, 32, LANES)
    up0 = (field0, stored(total0, 3, 8 * NC, LANES), field0)
    inner1 = RIM1 - 1
    inner_coarse, *ups0 = pl.pallas_call(
        inner0_kernel,
        out_shape=(shape(rows1, NP, LANES),) + up0,
        in_specs=[VM] * 3,
        out_specs=(VM, HB, HB, HB),
        scratch_shapes=buffers(total0, 3, names) + [pltpu.SemaphoreType.DMA((4,))],
        compiler_params=PARAMS,
        cost_estimate=pl.CostEstimate(flops=40_000_000, bytes_accessed=20_000_000, transcendentals=0),
        name="inner0",
    )(data0, left, right)
    data1, strips1, edges1, w0, coef0, scaled0 = pl.pallas_call(
        outer0_kernel,
        out_shape=(
            shape(rows1, NP, LANES),
            shape(2, rows1 // group, NP, LANES),
            shape(2, 2 * inner1, LANES),
        )
        + up0,
        in_specs=[VM] * 6 + [HB] * 3,
        out_specs=(VM, VM, VM, HB, HB, HB),
        input_output_aliases={6: 3, 7: 4, 8: 5},
        scratch_shapes=buffers(2 * SPAN, 3, names) + [pltpu.SemaphoreType.DMA((6,))],
        compiler_params=PARAMS,
        name="outer0",
    )(data0, left, right, from_low, from_high, inner_coarse, *in_hbm(ups0))

    left, right = beside(strips1)
    left, right = left.reshape(-1, LANES), right.reshape(-1, LANES)

    def face1(which, first, first_inner):
        parts = (
            data1[first_inner : first_inner + inner1, 0:32],
            data1[first : first + RIM1, 32:48],
            edges1[which],
            left,
            right,
        )
        return jnp.concatenate([v.reshape(-1, LANES) for v in parts], 0)

    low_face = face1(0, 0, 0)
    high_face = face1(1, rows1 - RIM1, rows1 - inner1)
    from_low = lax.ppermute(high_face, "gx", upward)
    from_high = lax.ppermute(low_face, "gx", downward)

    total1 = rows1 + 2 * RIM1
    rows2 = rows1 // 2
    total2 = rows2 + 2 * RIM2
    field1 = stored(total1, 2, 32, LANES)
    field2 = stored(total2, 1, 32, LANES)
    piece, w1, coef1, scaled1, w2, coef2, scaled2 = pl.pallas_call(
        down12_kernel,
        out_shape=(
            shape(nx, NP, LANES),
            field1,
            stored(total1, 2, 8 * NC, LANES),
            field1,
            field2,
            stored(total2, 1, 8 * NC, LANES),
            field2,
        ),
        in_specs=[VM] * 5,
        out_specs=(VM,) + (HB,) * 6,
        scratch_shapes=buffers(total1, 2, names) + buffers(total2, 1, names) + [pltpu.SemaphoreType.DMA((6,))],
        compiler_params=PARAMS,
        name="down12",
    )(data1, left, right, from_low, from_high)

    pieces = lax.all_gather(lax.all_to_all(piece, "gx", 0, 0), "gy", axis=0)

    rows3 = rows2 // 2
    total3 = nx * rows3 + 2 * RIM3
    ups = ("w", "coef", "scaled", "w", "w")
    result = pl.pallas_call(
        up_kernel,
        out_shape=shape(16, 2, rows, columns),
        in_specs=[SM, VM] + [HB] * 9,
        out_specs=HB,
        scratch_shapes=buffers(total3, 1, ("data", "coef", "scaled", "w", "w", "slope", "across"))
        + buffers(total2, 1, ups)
        + buffers(total1, 2, ups)
        + buffers(total0, 3, ups)
        + buffers(max(total0, total1), 3, ("slope", "across"))
        + [pltpu.VMEM((4, 16, PITCH, LANES), F32), pltpu.SemaphoreType.DMA((9,))],
        compiler_params=pltpu.CompilerParams(vmem_limit_bytes=VMEM_UP),
        name="up",
    )(
        jnp.stack([gx, gy]).astype(jnp.int32),
        pieces,
        *in_hbm([w0, coef0, scaled0, w1, coef1, scaled1, w2, coef2, scaled2]),
    )
    return result.reshape(misfit.shape)


def solution(mesh):
    placed = (
        P(None, None, "gx", "gy"),
        P(None, "gx", "gy"),
        P("gx", "gy"),
        P("gx", "gy"),
        P("gx", "gy"),
    )
    return jax.shard_map(
        per_device, mesh=mesh, in_specs=placed, out_specs=P(None, None, "gx", "gy"), check_vma=False
    )
```

```python
import functools

import jax
import jax.numpy as jnp
from jax import lax
from jax.experimental import pallas as pl
from jax.experimental.pallas import tpu as pltpu
from jax.sharding import PartitionSpec as P

LEVELS = 4
COARSE_ITERS = 20
OMEGA = 0.6
CROSS = 0.75
NP = 56
LANES = 128
RIM0 = 4
RIM1 = 13
RIM2 = 6
RIM3 = 2
STRIP1 = 16
NC = 15
PITCH = 40
SPAN = 11
VMEM_DOWN = 28 * 1024 * 1024
VMEM_UP = 60 * 1024 * 1024
F32 = jnp.float32
UNROLL0 = (18, 6, 4)
UNROLL1 = (38, 12, 8)
UNROLL2 = (18, 6, 4)
UNROLL3 = (32, 32, 8)
UNROLL0_UP = (18, 17)
UNROLL1_UP = (22, 20)
UNROLL_MOVE = 8


def rows_loop(first, last, body, unroll):
    count = (last - first) // unroll

    def step(i, carry):
        for j in range(unroll):
            body(first + i * unroll + j)
        return carry

    if count:
        lax.fori_loop(0, count, step, 0)
    for r in range(first + count * unroll, last):
        body(r)


def lane_ids(rows=8):
    return lax.broadcasted_iota(jnp.int32, (rows, LANES), 1)


def shifted(tiles, closed):
    lane = lax.broadcasted_iota(jnp.int32, tiles[0].shape, 1)
    up = [pltpu.roll(v, LANES - 1, 1) for v in tiles]
    down = [pltpu.roll(v, 1, 1) for v in tiles]
    n = len(tiles)
    if closed:
        zero = jnp.zeros_like(tiles[0])
        return (
            [jnp.where(lane == LANES - 1, zero, v) for v in up],
            [jnp.where(lane == 0, zero, v) for v in down],
        )
    if n == 1:
        return up, down
    return (
        [jnp.where(lane == LANES - 1, up[(t + 1) % n], up[t]) for t in range(n)],
        [jnp.where(lane == 0, down[(t - 1) % n], down[t]) for t in range(n)],
    )


def twice(v):
    return jnp.concatenate([v, v], 0)


def make_coefs(data, coef, scaled, diag, first, last, horizontal, closed, unroll):
    nt = data.shape[1]
    sub = lax.broadcasted_iota(jnp.int32, (8, LANES), 0)

    def row(r):
        mids = [data[r, t, 32:48, :] for t in range(nt)]
        norths, souths = shifted(mids, closed)
        for t in range(nt):
            mid = mids[t]
            west = (0.5 * horizontal) * (mid + data[r - 1, t, 32:48, :])
            east = (0.5 * horizontal) * (mid + data[r + 1, t, 32:48, :])
            north = (0.5 * horizontal) * (mid + norths[t])
            south = (0.5 * horizontal) * (mid + souths[t])
            low, high = mid[:8], mid[8:]
            inner = 2.0 * (low + high)
            outer = jnp.where(sub == 7, 0.0, 2.0 * (high + pltpu.roll(low, 7, 0)))
            outer_down = pltpu.roll(outer, 1, 0)
            coef[r, t, 0:16, :] = west
            coef[r, t, 16:32, :] = north
            coef[r, t, 32:48, :] = south
            coef[r, t, 48:64, :] = (CROSS * horizontal) * mid
            coef[r, t, 64:72, :] = inner
            coef[r, t, 72:80, :] = outer
            coef[r, t, 80:88, :] = outer_down
            ice = data[r, t, 48:49, :]
            drag = data[r, t, 49:50, :]
            bottom = jnp.where(sub == 0, drag, 0.0)
            upright = jnp.concatenate([inner + outer_down + bottom, inner + outer], 0)
            along_x = east + west
            along_y = north + south
            rest = 1.0 - ice
            for c, lateral in enumerate((4.0 * along_x + along_y, along_x + 4.0 * along_y)):
                diagonal = ice * (lateral + upright) + rest
                inverse = OMEGA / diagonal
                coef[r, t, 88 + 16 * c : 104 + 16 * c, :] = ice * inverse
                scaled[r, t, 16 * c : 16 * c + 16, :] = inverse * data[r, t, 16 * c : 16 * c + 16, :]
                if diag is not None:
                    diag[r, t, 16 * c : 16 * c + 16, :] = diagonal

    rows_loop(first, last, row, unroll)


def prepare(w, coef, slope, across, first, last, closed, unroll):
    nt = w.shape[1]

    def row(r):
        norths, souths = shifted([w[r, t] for t in range(nt)], closed)
        for t in range(nt):
            slope[r, t] = norths[t] - souths[t]
            across[r, t] = twice(coef[r, t, 16:32, :]) * norths[t] + twice(coef[r, t, 32:48, :]) * souths[t]

    rows_loop(first, last, row, unroll)


def off_diagonal(w, coef, slope, across, r, t):
    here = w[r, t]
    along = twice(coef[r + 1, t, 0:16, :]) * w[r + 1, t] + twice(coef[r, t, 0:16, :]) * w[r - 1, t]
    side = across[r, t]
    mixed = slope[r + 1, t] - slope[r - 1, t]
    cross = coef[r, t, 48:64, :]
    inner = coef[r, t, 64:72, :]
    outer = coef[r, t, 72:80, :]
    outer_down = coef[r, t, 80:88, :]
    parts = []
    for c in range(2):
        mine = slice(16 * c, 16 * c + 16)
        other = slice(16 - 16 * c, 32 - 16 * c)
        low, high = here[16 * c : 16 * c + 8], here[16 * c + 8 : 16 * c + 16]
        column = jnp.concatenate(
            [inner * high + outer_down * pltpu.roll(high, 1, 0), inner * low + outer * pltpu.roll(low, 7, 0)], 0
        )
        if c == 0:
            lateral = 4.0 * along[mine] + side[mine]
        else:
            lateral = along[mine] + 4.0 * side[mine]
        parts.append(lateral + cross * mixed[other] + column)
    return here, jnp.concatenate(parts, 0)


def sweep(w, new, coef, scaled, slope, across, first, last, closed, unroll, tiles=None, emit=None):
    look, unroll = unroll[:2]
    nt = w.shape[1]
    prepare(w, coef, slope, across, first - 1, last + 1, closed, look)

    def row(r):
        for t in range(nt if tiles is None else tiles):
            here, total = off_diagonal(w, coef, slope, across, r, t)
            value = (1.0 - OMEGA) * here + scaled[r, t] + coef[r, t, 88:120, :] * total
            if emit is None:
                new[r, t] = value
            else:
                emit(r, t, value)

    rows_loop(first, last, row, unroll)


def remainders(w, out, data, diag, coef, slope, across, first, last, unroll, tiles):
    look, unroll = unroll[:2]
    prepare(w, coef, slope, across, first - 1, last + 1, False, look)

    def row(r):
        for t in range(tiles):
            here, total = off_diagonal(w, coef, slope, across, r, t)
            out[r, t] = data[r, t, 0:32, :] + data[r, t, 48:49, :] * total - diag[r, t] * here

    rows_loop(first, last, row, unroll)


def gather_lanes(v, index):
    return jnp.take_along_axis(v, index, axis=1, mode="promise_in_bounds")


def halve(first, second):
    lane = lax.broadcasted_iota(jnp.int32, first.shape, 1)
    even = (2 * lane) % LANES
    low = gather_lanes(first + pltpu.roll(first, LANES - 1, 1), even)
    if second is None:
        return low
    high = gather_lanes(second + pltpu.roll(second, LANES - 1, 1), even)
    return jnp.where(lane < LANES // 2, low, high)


def restrict_row(source, planes, r):
    both = [source[r, t, planes, :] + source[r + 1, t, planes, :] for t in range(min(2, source.shape[1]))]
    return 0.25 * halve(both[0], both[1] if len(both) > 1 else None)


def prolong_row(tiles, fine_tiles):
    lane = lax.broadcasted_iota(jnp.int32, tiles[0].shape, 1)
    low = lane // 2
    high = LANES // 2 + lane // 2
    first = tiles[0]
    last = tiles[-1]
    out = [gather_lanes(first, low)]
    if fine_tiles == 2:
        out.append(gather_lanes(first, high))
    else:
        out.append(gather_lanes(first, high))
        out.append(gather_lanes(last, jnp.where(lane < LANES // 2, low, high)))
    return out


def put(strip, v, shift, width, at):
    lane = lax.broadcasted_iota(jnp.int32, v.shape, 1)
    rolled = pltpu.roll(v, shift % LANES, 1) if shift % LANES else v
    return jnp.where((lane >= at) & (lane < at + width), rolled, strip)


def unpack_rim(left, right, at, width):
    lane = lax.broadcasted_iota(jnp.int32, left.shape, 1)
    to_low = pltpu.roll(right, (LANES - at) % LANES, 1) if at else right
    shift = (2 * LANES - width - at) % LANES
    to_high = pltpu.roll(left, shift, 1) if shift else left
    return jnp.where(lane < LANES // 2, to_low, to_high)


def pair_rows(tiles):
    sub = lax.broadcasted_iota(jnp.int32, (8, LANES), 0)
    out = tiles[0]
    for j in range(1, len(tiles)):
        out = jnp.where(sub >= 2 * j, pltpu.roll(tiles[j], 2 * j, 0), out)
    return out


def pair_row(tile, j):
    return pltpu.roll(tile, 8 - 2 * j, 0) if j else tile


def copy_rows(source, target, sem, first, last):
    rows = pl.ds(first, last - first)
    copy = pltpu.make_async_copy(source.at[rows], target.at[rows], sem)
    copy.start()
    return copy


def arrange_kernel(misfit, viscosity, friction_in, ice_mask_in, grounded_in, data, strips, edges,
                   misfit_half, viscosity_half, friction, ice_mask, grounded, sems):
    rows = friction.shape[0]
    copies = [
        pltpu.make_async_copy(source, target, sems.at[n])
        for n, (source, target) in enumerate(((friction_in, friction), (ice_mask_in, ice_mask), (grounded_in, grounded)))
    ]
    for t in range(2):
        lanes = pl.ds(t * LANES, LANES)
        for p in range(2):
            n = 2 * t + p
            for source, target, sem in ((misfit, misfit_half, 3 + n), (viscosity, viscosity_half, 7 + n)):
                copies.append(
                    pltpu.make_async_copy(source.at[:, p, :, lanes], target.at[n, :, pl.ds(0, rows)], sems.at[sem])
                )
    for copy in copies:
        copy.start()
    for copy in copies:
        copy.wait()
    sub = lax.broadcasted_iota(jnp.int32, (8, LANES), 0)
    misfit_rows = misfit_half.reshape(4, -1, LANES)
    viscosity_rows = viscosity_half.reshape(4, -1, LANES)

    def eight(i, carry):
        block = pl.ds(pl.multiple_of(8 * i, 8), 8)
        for t in range(2):
            lanes = pl.ds(t * LANES, LANES)
            ices = ice_mask[block, lanes].astype(F32)
            drags = friction[block, lanes] * grounded[block, lanes].astype(F32)
            for j in range(8):
                r = 8 * i + j
                ice, drag = ices[j : j + 1], drags[j : j + 1]
                for c in range(2):
                    for p in range(2):
                        v = misfit_rows[2 * t + p, pl.ds(8 * c * PITCH + r, 8, stride=PITCH), :]
                        data[r, t, 16 * c + 8 * p : 16 * c + 8 * p + 8, :] = v * ice
                for p in range(2):
                    data[r, t, 32 + 8 * p : 40 + 8 * p, :] = viscosity_rows[2 * t + p, pl.ds(r, 8, stride=PITCH), :]
                data[r, t, 48:56, :] = jnp.where(sub == 0, ice, jnp.where(sub == 1, drag, 0.0))
        return carry

    lax.fori_loop(0, rows // 8, eight, 0)
    corner = RIM0 * RIM0
    for side in range(2):
        low = jnp.zeros((8, LANES), F32)
        high = low
        for first in range(0, NP, 8):
            planes = slice(first, first + 8)
            strip = jnp.zeros((8, LANES), F32)
            for r in range(rows):
                at = r * RIM0
                strip = put(strip, data[r, side, planes, :], at if side == 0 else at + RIM0, RIM0, at)
            strips[side, planes, :] = strip
            at = first // 8 * corner
            low = put(low, strip, at, corner, at)
            high = put(high, strip, at + corner, corner, at)
        strips[side, NP : NP + 8, :] = low
        strips[side, NP + 8 : NP + 16, :] = high
    for t in range(2):
        edges[0, 8 * t : 8 * t + 8, :] = pair_rows([data[r, t, 48:56, :] for r in range(RIM0 - 1)])
        edges[1, 8 * t : 8 * t + 8, :] = pair_rows([data[rows - RIM0 + 1 + r, t, 48:56, :] for r in range(RIM0 - 1)])


def inner0_kernel(own, left, right, coarse, w_out, coef_out, scaled_out, data, diag, slope, across, wa, coef, scaled, sems):
    rows = own.shape[0]
    first, last = RIM0, RIM0 + rows

    def copy_row(r):
        for t in range(2):
            data[first + r, t] = own[r, t]

    rows_loop(0, rows, copy_row, 4)
    for r in range(rows):
        data[first + r, 2] = unpack_rim(left[0:NP, :], right[0:NP, :], r * RIM0, RIM0)
    half = first + rows // 2 - 1
    make_coefs(data, coef, scaled, diag, first + 1, half, 1.0, False, UNROLL0[2])
    copies = [copy_rows(coef, coef_out, sems.at[0], first + 1, half)]
    make_coefs(data, coef, scaled, diag, half, last - 1, 1.0, False, UNROLL0[2])
    copies.append(copy_rows(coef, coef_out, sems.at[1], half, last - 1))
    copies.append(copy_rows(scaled, scaled_out, sems.at[2], first + 1, last - 1))
    sweep(scaled, wa, coef, scaled, slope, across, first + 2, last - 2, False, UNROLL0)
    copies.append(copy_rows(wa, w_out, sems.at[3], first + 2, last - 2))

    def coefs_row(i):
        coarse[i, 32:56, :] = restrict_row(data, slice(32, 56), first + 2 * i)

    rows_loop(0, rows // 2, coefs_row, UNROLL_MOVE)
    remainders(wa, diag, data, diag, coef, slope, across, first + 3, last - 3, UNROLL0, 2)

    def target_row(i):
        coarse[i, 0:32, :] = restrict_row(diag, slice(0, 32), first + 2 * i)

    rows_loop(2, rows // 2 - 2, target_row, UNROLL_MOVE)
    for copy in copies:
        copy.wait()


def outer0_kernel(own, left, right, from_low, from_high, inner_coarse, w_in, coef_in, scaled_in,
                  coarse, strips1, edges1, w_out, coef_out, scaled_out,
                  data, diag, slope, across, wa, coef, scaled, sems):
    rows = own.shape[0]
    mine = SPAN - RIM0
    inner = RIM0 - 1
    thick = 64 * inner
    thin = thick + 32 * RIM0
    corner = thin + 16
    copies = []
    for face, start, rim_at, mine_at, x in (
        (from_low, 0, 0, RIM0, 0),
        (from_high, SPAN, SPAN + mine, SPAN, rows - mine),
    ):
        for r in range(mine):
            for t in range(2):
                data[mine_at + r, t] = own[x + r, t]
            data[mine_at + r, 2] = unpack_rim(left[0:NP, :], right[0:NP, :], (x + r) * RIM0, RIM0)
        skip = 1 if start == 0 else 0
        for t in range(2):
            for r in range(inner):
                at = 32 * (2 * r + t)
                data[rim_at + skip + r, t, 0:32, :] = face[at : at + 32, :]
                data[rim_at + skip + r, t, 48:56, :] = pair_row(face[thin + 8 * t : thin + 8 * t + 8, :], r)
            for r in range(RIM0):
                at = thick + 16 * (2 * r + t)
                data[rim_at + r, t, 32:48, :] = face[at : at + 16, :]
        for q in range(NP // 8):
            for r in range(RIM0):
                at = RIM0 * (RIM0 * q + r)
                data[rim_at + r, 2, 8 * q : 8 * q + 8, :] = unpack_rim(
                    face[corner : corner + 8, :], face[corner + 8 : corner + 16, :], at, RIM0
                )
    for start in (0, SPAN):
        make_coefs(data, coef, scaled, diag, start + 1, start + SPAN - 1, 1.0, False, 9)
    total = rows + 2 * RIM0
    shift = total - 2 * SPAN
    ranges = ((2, RIM0 + 1), (3, RIM0 + 1), (2, RIM0 + 2))
    arrays = ((coef, coef_out), (scaled, scaled_out), (wa, w_out))

    def store(n):
        (source, target), (low, high) = arrays[n], ranges[n]
        for side in range(2):
            begin = low if side == 0 else 2 * SPAN - high
            place = begin + (0 if side == 0 else shift)
            copy = pltpu.make_async_copy(
                source.at[pl.ds(begin, high - low)], target.at[pl.ds(place, high - low)], sems.at[2 * n + side]
            )
            copy.start()
            copies.append(copy)

    store(0)
    store(1)
    for start in (0, SPAN):
        sweep(scaled, wa, coef, scaled, slope, across, start + 2, start + SPAN - 2, False, (9, 7))
    store(2)

    def copy_coarse(i):
        coarse[i] = inner_coarse[i]

    rows_loop(0, rows // 2, copy_coarse, 4)
    for start in (0, SPAN):
        remainders(wa, diag, data, diag, coef, slope, across, start + 3, start + SPAN - 3, (7, 5), 2)
    for i in range(2):
        coarse[i, 0:32, :] = restrict_row(diag, slice(0, 32), RIM0 + 2 * i)
        coarse[rows // 2 - 2 + i, 0:32, :] = restrict_row(diag, slice(0, 32), SPAN + mine - 4 + 2 * i)
    group = LANES // STRIP1
    for side in range(2):
        for part in range(rows // 2 // group):
            for first in range(0, NP, 8):
                planes = slice(first, first + 8)
                strip = jnp.zeros((8, LANES), F32)
                for j in range(group):
                    at = j * STRIP1
                    shift1 = at if side == 0 else at + STRIP1
                    strip = put(strip, coarse[part * group + j, planes, :], shift1, STRIP1, at)
                strips1[side, part, planes, :] = strip
    inner1 = RIM1 - 1
    for face, base in enumerate((0, rows // 2 - inner1)):
        for j in range(0, inner1, 4):
            edges1[face, 2 * j : 2 * j + 8, :] = pair_rows([coarse[base + j + n, 48:56, :] for n in range(4)])
    for copy in copies:
        copy.wait()


def down12_kernel(own, sides, from_low, from_high, sides_low, sides_high, piece, w1_out, coef1_out, scaled1_out, w2_out, coef2_out, scaled2_out,
                  data1, diag1, slope1, across1, wa1, coef1, scaled1, data2, diag2, slope2, across2, wa2, coef2, scaled2, sems):
    rows = own.shape[0]
    total = rows + 2 * RIM1
    group = LANES // STRIP1
    parts = rows // group

    def rim(strips, r):
        part, j = r // group, r % group
        low, high = part * NP, (parts + part) * NP
        return unpack_rim(strips[low : low + NP, :], strips[high : high + NP, :], j * STRIP1, STRIP1)

    def copy_row(r):
        data1[RIM1 + r, 0] = own[r]

    rows_loop(0, rows, copy_row, 4)
    for r in range(rows):
        data1[RIM1 + r, 1] = rim(sides, r)
    inner = RIM1 - 1
    thick = 32 * inner
    thin = thick + 16 * RIM1
    for face, strips, base, skip, first in (
        (from_low, sides_low, 0, 1, rows - RIM1),
        (from_high, sides_high, RIM1 + rows, 0, 0),
    ):
        for r in range(inner):
            data1[base + skip + r, 0, 0:32, :] = face[32 * r : 32 * r + 32, :]
            at = thin + 8 * (r // 4)
            data1[base + skip + r, 0, 48:56, :] = pair_row(face[at : at + 8, :], r % 4)
        for r in range(RIM1):
            at = thick + 16 * r
            data1[base + r, 0, 32:48, :] = face[at : at + 16, :]
            data1[base + r, 1] = rim(strips, first + r)

    make_coefs(data1, coef1, scaled1, diag1, 1, total - 1, 0.25, False, UNROLL1[2])
    copies = [copy_rows(coef1, coef1_out, sems.at[0], 10, total - 10)]
    copies.append(copy_rows(scaled1, scaled1_out, sems.at[1], 11, total - 11))
    sweep(scaled1, wa1, coef1, scaled1, slope1, across1, 2, total - 2, False, UNROLL1)
    copies.append(copy_rows(wa1, w1_out, sems.at[2], 9, total - 9))
    remainders(wa1, diag1, data1, diag1, coef1, slope1, across1, 3, total - 3, UNROLL1, 2)

    rows2 = rows // 2
    total2 = rows2 + 2 * RIM2

    def coefs_row(i):
        data2[i, 0, 32:56, :] = restrict_row(data1, slice(32, 56), 1 + 2 * i)

    rows_loop(0, total2, coefs_row, UNROLL_MOVE)

    def target_row(i):
        data2[i, 0, 0:32, :] = restrict_row(diag1, slice(0, 32), 1 + 2 * i)

    rows_loop(1, total2 - 1, target_row, UNROLL_MOVE)

    make_coefs(data2, coef2, scaled2, diag2, 1, total2 - 1, 0.0625, False, UNROLL2[2])
    copies.append(copy_rows(coef2, coef2_out, sems.at[3], 2, total2 - 2))
    copies.append(copy_rows(scaled2, scaled2_out, sems.at[4], 3, total2 - 3))
    sweep(scaled2, wa2, coef2, scaled2, slope2, across2, 2, total2 - 2, False, UNROLL2)
    copies.append(copy_rows(wa2, w2_out, sems.at[5], 2, total2 - 2))
    remainders(wa2, diag2, data2, diag2, coef2, slope2, across2, RIM2, RIM2 + rows2, UNROLL2, 1)

    rows3 = rows2 // 2
    width = LANES // rows3
    for first in range(0, NP, 8):
        planes = slice(first, first + 8)
        source = diag2 if first < 32 else data2
        strip = jnp.zeros((8, LANES), F32)
        for i in range(rows3):
            strip = put(strip, restrict_row(source, planes, RIM2 + 2 * i), i * width, width, i * width)
        for d in range(piece.shape[0]):
            piece[d, planes, :] = strip
    for copy in copies:
        copy.wait()


def up_kernel(place, pieces, w0_in, coef0_in, scaled0_in, w1_in, coef1_in, scaled1_in, w2_in, coef2_in, scaled2_in, result,
              data3, coef3, scaled3, wa3, wb3, slope3, across3, w2, coef2, scaled2, wa2, wb2, w1, coef1, scaled1, wa1, wb1,
              w0, coef0, scaled0, wa0, wb0, slope0, across0, result_half, sems):
    slope1, across1 = (v.at[pl.ds(0, wa1.shape[0]), pl.ds(0, 2)] for v in (slope0, across0))
    slope2, across2 = (v.at[pl.ds(0, wa2.shape[0]), pl.ds(0, 1)] for v in (slope0, across0))
    copies = []
    for source, target, first in (
        (w2_in, w2, 2), (coef2_in, coef2, 2), (scaled2_in, scaled2, 3),
        (w1_in, w1, 9), (coef1_in, coef1, 10), (scaled1_in, scaled1, 11),
        (w0_in, w0, 2), (coef0_in, coef0, 2), (scaled0_in, scaled0, 3),
    ):
        copies.append(copy_rows(source, target, sems.at[len(copies)], first, source.shape[0] - first))
    devices_y, devices_x = pieces.shape[0], pieces.shape[1]
    rows3 = devices_y
    width = LANES // devices_y
    whole = devices_x * rows3
    zero = jnp.zeros((NP, LANES), F32)
    for r in range(RIM3):
        for end in (r, RIM3 + whole + r):
            data3[end, 0] = zero
            wa3[end, 0] = zero[:32]
            wb3[end, 0] = zero[:32]
            scaled3[end, 0] = zero[:32]
            slope3[end, 0] = zero[:32]
            coef3[end, 0] = jnp.zeros((8 * NC, LANES), F32)

    def assemble(d, carry):
        for i in range(rows3):
            line = jnp.zeros((NP, LANES), F32)
            for j in range(devices_y):
                line = put(line, pieces[j, d], (j - i) * width, width, j * width)
            data3[RIM3 + d * rows3 + i, 0] = line
        return carry

    lax.fori_loop(0, devices_x, assemble, 0)
    first, last = RIM3, RIM3 + whole
    make_coefs(data3, coef3, scaled3, None, first, last, 0.25 ** (LEVELS - 1), True, UNROLL3[2])

    gx, gy = place[0], place[1]

    def coarse_sweep(source, target, extent):
        begin, end = (first, last) if extent is None else (0, extent)
        start = 0 if extent is None else first + jnp.clip(gx * rows3 - (extent - rows3) // 2, 0, whole - extent)
        around = 0 if extent is None else 1

        def look(r):
            r = start + r
            norths, souths = shifted([source[r, 0]], True)
            slope3[r, 0] = norths[0] - souths[0]
            across3[r, 0] = twice(coef3[r, 0, 16:32, :]) * norths[0] + twice(coef3[r, 0, 32:48, :]) * souths[0]

        rows_loop(begin - around, end + around, look, UNROLL3[0] if extent is None else extent + 2)

        def row(r):
            r = start + r
            here, total = off_diagonal(source, coef3, slope3, across3, r, 0)
            target[r, 0] = (1.0 - OMEGA) * here + scaled3[r, 0] + coef3[r, 0, 88:120, :] * total

        rows_loop(begin, end, row, UNROLL3[1])

    coarse_sweep(scaled3, wa3, None)
    done = 2
    narrow = [(None, COARSE_ITERS - 9), (rows3 + 20, COARSE_ITERS - 5), (rows3 + 12, COARSE_ITERS)]
    buffers = (wa3, wb3)
    for extent, until in narrow:
        if extent is not None and extent > whole:
            extent = None

        def two_sweeps(i, carry, extent=extent, pair=buffers):
            coarse_sweep(pair[0], pair[1], extent)
            coarse_sweep(pair[1], pair[0], extent)
            return carry

        if (until - done) // 2:
            lax.fori_loop(0, (until - done) // 2, two_sweeps, 0)
        if (until - done) % 2:
            coarse_sweep(buffers[0], buffers[1], extent)
            buffers = buffers[::-1]
        done = until
    solved = buffers[0]

    lane = lane_ids(32)
    y = jnp.where(lane < 96, lane, lane - LANES)
    column = gy * width + (y + LANES) // 2 - LANES // 2
    inside = (column >= 0) & (column < LANES)
    pick = jnp.where(inside, column, 0)

    for copy in copies[:3]:
        copy.wait()
    rows2 = 2 * rows3
    for i in range(rows3 + 2 * RIM3):
        add = jnp.where(inside, gather_lanes(solved[gx * rows3 + i, 0], pick), 0.0)
        for r in (2 * i + 2, 2 * i + 3):
            wa2[r, 0] = w2[r, 0] + add
    total2 = rows2 + 2 * RIM2
    sweep(wa2, wb2, coef2, scaled2, slope2, across2, 3, total2 - 3, False, UNROLL2)
    sweep(wb2, wa2, coef2, scaled2, slope2, across2, 4, total2 - 4, False, UNROLL2)


    for copy in copies[3:6]:
        copy.wait()

    def add1(r):
        adds = prolong_row([wa2[r, 0]], 2)
        for t in range(2):
            for fine in (2 * r + 1, 2 * r + 2):
                wa1[fine, t] = w1[fine, t] + adds[t]

    rows_loop(4, total2 - 4, add1, UNROLL_MOVE)
    total1 = 2 * rows2 + 2 * RIM1
    sweep(wa1, wb1, coef1, scaled1, slope1, across1, 11, total1 - 11, False, UNROLL1_UP)
    sweep(wb1, wa1, coef1, scaled1, slope1, across1, 12, total1 - 12, False, UNROLL1_UP)


    for copy in copies[6:]:
        copy.wait()

    def add0(r):
        adds = prolong_row([wa1[r, t] for t in range(2)], 3)
        for t in range(3):
            for fine in (2 * r - 22, 2 * r - 21):
                wa0[fine, t] = w0[fine, t] + adds[t]

    rows_loop(12, total1 - 12, add0, UNROLL_MOVE)
    rows0 = 4 * rows2
    total0 = rows0 + 2 * RIM0
    sweep(wa0, wb0, coef0, scaled0, slope0, across0, 3, total0 - 3, False, UNROLL0_UP)

    result_rows = result_half.reshape(4, -1, LANES)

    def emit(r, t, value):
        for c in range(2):
            for p in range(2):
                start = 8 * c * PITCH + r - RIM0
                result_rows[2 * t + p, pl.ds(start, 8, stride=PITCH), :] = value[16 * c + 8 * p : 16 * c + 8 * p + 8]

    sweep(wb0, None, coef0, scaled0, slope0, across0, RIM0, RIM0 + rows0, False, UNROLL0_UP, tiles=2, emit=emit)
    copies = [
        pltpu.make_async_copy(
            result_half.at[2 * t + p, :, pl.ds(0, rows0)], result.at[:, p, :, pl.ds(t * LANES, LANES)], sems.at[2 * t + p]
        )
        for t in range(2)
        for p in range(2)
    ]
    for copy in copies:
        copy.start()
    for copy in copies:
        copy.wait()


def shape(*dims):
    return jax.ShapeDtypeStruct(dims, F32)


def stored(*dims):
    return pltpu.HBM(dims, F32)


def in_hbm(arrays):
    return [pltpu.with_memory_space_constraint(v, pltpu.HBM) for v in arrays]


VM = pl.BlockSpec(memory_space=pltpu.VMEM)
SM = pl.BlockSpec(memory_space=pltpu.SMEM)
HB = pl.BlockSpec(memory_space=pl.ANY)
PARAMS = pltpu.CompilerParams(vmem_limit_bytes=VMEM_DOWN)


def buffers(rows, tiles, names):
    planes = {"data": NP, "coef": 8 * NC}
    return [pltpu.VMEM((rows, tiles, planes.get(name, 32), LANES), F32) for name in names]


def per_device(misfit, viscosity, friction, ice_mask, grounded):
    rows, columns = friction.shape
    gx, gy = lax.axis_index("gx"), lax.axis_index("gy")
    nx, ny = lax.axis_size("gx"), lax.axis_size("gy")
    upward = [(i, i + 1) for i in range(nx - 1)]
    downward = [(i + 1, i) for i in range(nx - 1)]

    def beside(strips):
        every = lax.all_gather(strips, "gy", axis=0)
        left = lax.dynamic_index_in_dim(every, jnp.maximum(gy - 1, 0), 0, keepdims=False)[1]
        right = lax.dynamic_index_in_dim(every, jnp.minimum(gy + 1, ny - 1), 0, keepdims=False)[0]
        return jnp.where(gy > 0, left, 0.0), jnp.where(gy < ny - 1, right, 0.0)

    data0, strips0, edges0 = pl.pallas_call(
        arrange_kernel,
        out_shape=(shape(rows, 2, NP, LANES), shape(2, NP + 16, LANES), shape(2, 16, LANES)),
        in_specs=[HB] * 5,
        out_specs=(VM, VM, VM),
        scratch_shapes=[
            pltpu.VMEM((4, 16, PITCH, LANES), F32),
            pltpu.VMEM((4, 8, PITCH, LANES), F32),
            pltpu.VMEM((rows, columns), F32),
            pltpu.VMEM((rows, columns), jnp.int32),
            pltpu.VMEM((rows, columns), jnp.int32),
            pltpu.SemaphoreType.DMA((11,)),
        ],
        compiler_params=PARAMS,
        name="arrange",
    )(
        *in_hbm(
            [v.reshape(-1, 2, rows, columns) for v in (misfit, viscosity)] + [friction, ice_mask, grounded]
        )
    )
    left, right = beside(strips0)
    inner = RIM0 - 1

    def face0(which, first, first_inner):
        corner = slice(NP + 8 * which, NP + 8 * which + 8)
        parts = (
            data0[first_inner : first_inner + inner, :, 0:32],
            data0[first : first + RIM0, :, 32:48],
            edges0[which],
            left[corner],
            right[corner],
        )
        return jnp.concatenate([v.reshape(-1, LANES) for v in parts], 0)

    low_face = face0(0, 0, 0)
    high_face = face0(1, rows - RIM0, rows - inner)
    from_low = lax.ppermute(high_face, "gx", upward)
    from_high = lax.ppermute(low_face, "gx", downward)

    total0 = rows + 2 * RIM0
    names = ("data", "diag", "slope", "across", "w", "coef", "scaled")
    rows1 = rows // 2
    group = LANES // STRIP1
    field0 = stored(total0, 3, 32, LANES)
    up0 = (field0, stored(total0, 3, 8 * NC, LANES), field0)
    inner1 = RIM1 - 1
    inner_coarse, *ups0 = pl.pallas_call(
        inner0_kernel,
        out_shape=(shape(rows1, NP, LANES),) + up0,
        in_specs=[VM] * 3,
        out_specs=(VM, HB, HB, HB),
        scratch_shapes=buffers(total0, 3, names) + [pltpu.SemaphoreType.DMA((4,))],
        compiler_params=PARAMS,
        cost_estimate=pl.CostEstimate(flops=40_000_000, bytes_accessed=20_000_000, transcendentals=0),
        name="inner0",
    )(data0, left, right)
    data1, strips1, edges1, w0, coef0, scaled0 = pl.pallas_call(
        outer0_kernel,
        out_shape=(
            shape(rows1, NP, LANES),
            shape(2, rows1 // group, NP, LANES),
            shape(2, 2 * inner1, LANES),
        )
        + up0,
        in_specs=[VM] * 6 + [HB] * 3,
        out_specs=(VM, VM, VM, HB, HB, HB),
        input_output_aliases={6: 3, 7: 4, 8: 5},
        scratch_shapes=buffers(2 * SPAN, 3, names) + [pltpu.SemaphoreType.DMA((6,))],
        compiler_params=PARAMS,
        name="outer0",
    )(data0, left, right, from_low, from_high, inner_coarse, *in_hbm(ups0))

    def face1(which, first, first_inner):
        parts = (data1[first_inner : first_inner + inner1, 0:32], data1[first : first + RIM1, 32:48], edges1[which])
        return jnp.concatenate([v.reshape(-1, LANES) for v in parts], 0)

    from_low = lax.ppermute(face1(1, rows1 - RIM1, rows1 - inner1), "gx", upward)
    from_high = lax.ppermute(face1(0, 0, 0), "gx", downward)
    left, right = (v.reshape(-1, LANES) for v in beside(strips1))
    sides = jnp.concatenate([left, right], 0)
    sides_low = lax.ppermute(sides, "gx", upward)
    sides_high = lax.ppermute(sides, "gx", downward)

    total1 = rows1 + 2 * RIM1
    rows2 = rows1 // 2
    total2 = rows2 + 2 * RIM2
    field1 = stored(total1, 2, 32, LANES)
    field2 = stored(total2, 1, 32, LANES)
    piece, w1, coef1, scaled1, w2, coef2, scaled2 = pl.pallas_call(
        down12_kernel,
        out_shape=(
            shape(nx, NP, LANES),
            field1,
            stored(total1, 2, 8 * NC, LANES),
            field1,
            field2,
            stored(total2, 1, 8 * NC, LANES),
            field2,
        ),
        in_specs=[VM] * 6,
        out_specs=(VM,) + (HB,) * 6,
        scratch_shapes=buffers(total1, 2, names) + buffers(total2, 1, names) + [pltpu.SemaphoreType.DMA((6,))],
        compiler_params=PARAMS,
        name="down12",
    )(data1, sides, from_low, from_high, sides_low, sides_high)

    pieces = lax.all_gather(lax.all_to_all(piece, "gx", 0, 0), "gy", axis=0)

    rows3 = rows2 // 2
    total3 = nx * rows3 + 2 * RIM3
    ups = ("w", "coef", "scaled", "w", "w")
    result = pl.pallas_call(
        up_kernel,
        out_shape=shape(16, 2, rows, columns),
        in_specs=[SM, VM] + [HB] * 9,
        out_specs=HB,
        scratch_shapes=buffers(total3, 1, ("data", "coef", "scaled", "w", "w", "slope", "across"))
        + buffers(total2, 1, ups)
        + buffers(total1, 2, ups)
        + buffers(total0, 3, ups)
        + buffers(max(total0, total1), 3, ("slope", "across"))
        + [pltpu.VMEM((4, 16, PITCH, LANES), F32), pltpu.SemaphoreType.DMA((9,))],
        compiler_params=pltpu.CompilerParams(vmem_limit_bytes=VMEM_UP),
        name="up",
    )(
        jnp.stack([gx, gy]).astype(jnp.int32),
        pieces,
        *in_hbm([w0, coef0, scaled0, w1, coef1, scaled1, w2, coef2, scaled2]),
    )
    return result.reshape(misfit.shape)


def solution(mesh):
    placed = (
        P(None, None, "gx", "gy"),
        P(None, "gx", "gy"),
        P("gx", "gy"),
        P("gx", "gy"),
        P("gx", "gy"),
    )
    return jax.shard_map(
        per_device, mesh=mesh, in_specs=placed, out_specs=P(None, None, "gx", "gy"), check_vma=False
    )
```

```python
import functools

import jax
import jax.numpy as jnp
from jax import lax
from jax.experimental import pallas as pl
from jax.experimental.pallas import tpu as pltpu
from jax.sharding import PartitionSpec as P

LEVELS = 4
COARSE_ITERS = 20
OMEGA = 0.6
CROSS = 0.75
NP = 56
LANES = 128
RIM0 = 4
RIM1 = 13
RIM2 = 6
RIM3 = 2
STRIP1 = 16
NC = 15
PITCH = 40
SPAN = 11
VMEM_DOWN = 28 * 1024 * 1024
VMEM_UP = 60 * 1024 * 1024
F32 = jnp.float32
UNROLL0 = (18, 6, 4)
UNROLL1 = (38, 18, 20)
UNROLL2 = (18, 16, 18)
UNROLL3 = (32, 32, 16)
UNROLL0_UP = (36, 34)
UNROLL1_UP = (22, 20)
UNROLL_MOVE = 8


def rows_loop(first, last, body, unroll):
    count = (last - first) // unroll

    def step(i, carry):
        for j in range(unroll):
            body(first + i * unroll + j)
        return carry

    if count:
        lax.fori_loop(0, count, step, 0)
    for r in range(first + count * unroll, last):
        body(r)


def lane_ids(rows=8):
    return lax.broadcasted_iota(jnp.int32, (rows, LANES), 1)


def shifted(tiles, closed):
    lane = lax.broadcasted_iota(jnp.int32, tiles[0].shape, 1)
    up = [pltpu.roll(v, LANES - 1, 1) for v in tiles]
    down = [pltpu.roll(v, 1, 1) for v in tiles]
    n = len(tiles)
    if closed:
        zero = jnp.zeros_like(tiles[0])
        return (
            [jnp.where(lane == LANES - 1, zero, v) for v in up],
            [jnp.where(lane == 0, zero, v) for v in down],
        )
    if n == 1:
        return up, down
    return (
        [jnp.where(lane == LANES - 1, up[(t + 1) % n], up[t]) for t in range(n)],
        [jnp.where(lane == 0, down[(t - 1) % n], down[t]) for t in range(n)],
    )


def twice(v):
    return jnp.concatenate([v, v], 0)


def make_coefs(data, coef, scaled, diag, first, last, horizontal, closed, unroll):
    nt = data.shape[1]
    sub = lax.broadcasted_iota(jnp.int32, (8, LANES), 0)

    def row(r):
        mids = [data[r, t, 32:48, :] for t in range(nt)]
        norths, souths = shifted(mids, closed)
        for t in range(nt):
            mid = mids[t]
            west = (0.5 * horizontal) * (mid + data[r - 1, t, 32:48, :])
            east = (0.5 * horizontal) * (mid + data[r + 1, t, 32:48, :])
            north = (0.5 * horizontal) * (mid + norths[t])
            south = (0.5 * horizontal) * (mid + souths[t])
            low, high = mid[:8], mid[8:]
            inner = 2.0 * (low + high)
            outer = jnp.where(sub == 7, 0.0, 2.0 * (high + pltpu.roll(low, 7, 0)))
            outer_down = pltpu.roll(outer, 1, 0)
            coef[r, t, 0:16, :] = west
            coef[r, t, 16:32, :] = north
            coef[r, t, 32:48, :] = south
            coef[r, t, 48:64, :] = (CROSS * horizontal) * mid
            coef[r, t, 64:72, :] = inner
            coef[r, t, 72:80, :] = outer
            coef[r, t, 80:88, :] = outer_down
            ice = data[r, t, 48:49, :]
            drag = data[r, t, 49:50, :]
            bottom = jnp.where(sub == 0, drag, 0.0)
            upright = jnp.concatenate([inner + outer_down + bottom, inner + outer], 0)
            along_x = east + west
            along_y = north + south
            rest = 1.0 - ice
            for c, lateral in enumerate((4.0 * along_x + along_y, along_x + 4.0 * along_y)):
                diagonal = ice * (lateral + upright) + rest
                inverse = OMEGA / diagonal
                coef[r, t, 88 + 16 * c : 104 + 16 * c, :] = ice * inverse
                scaled[r, t, 16 * c : 16 * c + 16, :] = inverse * data[r, t, 16 * c : 16 * c + 16, :]
                if diag is not None:
                    diag[r, t, 16 * c : 16 * c + 16, :] = diagonal

    rows_loop(first, last, row, unroll)


def prepare(w, coef, slope, across, first, last, closed, unroll):
    nt = w.shape[1]

    def row(r):
        norths, souths = shifted([w[r, t] for t in range(nt)], closed)
        for t in range(nt):
            slope[r, t] = norths[t] - souths[t]
            across[r, t] = twice(coef[r, t, 16:32, :]) * norths[t] + twice(coef[r, t, 32:48, :]) * souths[t]

    rows_loop(first, last, row, unroll)


def off_diagonal(w, coef, slope, across, r, t):
    here = w[r, t]
    along = twice(coef[r + 1, t, 0:16, :]) * w[r + 1, t] + twice(coef[r, t, 0:16, :]) * w[r - 1, t]
    side = across[r, t]
    mixed = slope[r + 1, t] - slope[r - 1, t]
    cross = coef[r, t, 48:64, :]
    inner = coef[r, t, 64:72, :]
    outer = coef[r, t, 72:80, :]
    outer_down = coef[r, t, 80:88, :]
    parts = []
    for c in range(2):
        mine = slice(16 * c, 16 * c + 16)
        other = slice(16 - 16 * c, 32 - 16 * c)
        low, high = here[16 * c : 16 * c + 8], here[16 * c + 8 : 16 * c + 16]
        column = jnp.concatenate(
            [inner * high + outer_down * pltpu.roll(high, 1, 0), inner * low + outer * pltpu.roll(low, 7, 0)], 0
        )
        if c == 0:
            lateral = 4.0 * along[mine] + side[mine]
        else:
            lateral = along[mine] + 4.0 * side[mine]
        parts.append(lateral + cross * mixed[other] + column)
    return here, jnp.concatenate(parts, 0)


def sweep(w, new, coef, scaled, slope, across, first, last, closed, unroll, tiles=None, emit=None):
    look, unroll = unroll[:2]
    nt = w.shape[1]
    prepare(w, coef, slope, across, first - 1, last + 1, closed, look)

    def row(r):
        for t in range(nt if tiles is None else tiles):
            here, total = off_diagonal(w, coef, slope, across, r, t)
            value = (1.0 - OMEGA) * here + scaled[r, t] + coef[r, t, 88:120, :] * total
            if emit is None:
                new[r, t] = value
            else:
                emit(r, t, value)

    rows_loop(first, last, row, unroll)


def remainders(w, out, data, diag, coef, slope, across, first, last, unroll, tiles):
    look, unroll = unroll[:2]
    prepare(w, coef, slope, across, first - 1, last + 1, False, look)

    def row(r):
        for t in range(tiles):
            here, total = off_diagonal(w, coef, slope, across, r, t)
            out[r, t] = data[r, t, 0:32, :] + data[r, t, 48:49, :] * total - diag[r, t] * here

    rows_loop(first, last, row, unroll)


def gather_lanes(v, index):
    return jnp.take_along_axis(v, index, axis=1, mode="promise_in_bounds")


def halve(first, second):
    lane = lax.broadcasted_iota(jnp.int32, first.shape, 1)
    even = (2 * lane) % LANES
    low = gather_lanes(first + pltpu.roll(first, LANES - 1, 1), even)
    if second is None:
        return low
    high = gather_lanes(second + pltpu.roll(second, LANES - 1, 1), even)
    return jnp.where(lane < LANES // 2, low, high)


def restrict_row(source, planes, r):
    both = [source[r, t, planes, :] + source[r + 1, t, planes, :] for t in range(min(2, source.shape[1]))]
    return 0.25 * halve(both[0], both[1] if len(both) > 1 else None)


def prolong_row(tiles, fine_tiles):
    lane = lax.broadcasted_iota(jnp.int32, tiles[0].shape, 1)
    low = lane // 2
    high = LANES // 2 + lane // 2
    first = tiles[0]
    last = tiles[-1]
    out = [gather_lanes(first, low)]
    if fine_tiles == 2:
        out.append(gather_lanes(first, high))
    else:
        out.append(gather_lanes(first, high))
        out.append(gather_lanes(last, jnp.where(lane < LANES // 2, low, high)))
    return out


def put(strip, v, shift, width, at):
    lane = lax.broadcasted_iota(jnp.int32, v.shape, 1)
    rolled = pltpu.roll(v, shift % LANES, 1) if shift % LANES else v
    return jnp.where((lane >= at) & (lane < at + width), rolled, strip)


def unpack_rim(left, right, at, width):
    lane = lax.broadcasted_iota(jnp.int32, left.shape, 1)
    to_low = pltpu.roll(right, (LANES - at) % LANES, 1) if at else right
    shift = (2 * LANES - width - at) % LANES
    to_high = pltpu.roll(left, shift, 1) if shift else left
    return jnp.where(lane < LANES // 2, to_low, to_high)


def pair_rows(tiles):
    sub = lax.broadcasted_iota(jnp.int32, (8, LANES), 0)
    out = tiles[0]
    for j in range(1, len(tiles)):
        out = jnp.where(sub >= 2 * j, pltpu.roll(tiles[j], 2 * j, 0), out)
    return out


def pair_row(tile, j):
    return pltpu.roll(tile, 8 - 2 * j, 0) if j else tile


def copy_rows(source, target, sem, first, last):
    rows = pl.ds(first, last - first)
    copy = pltpu.make_async_copy(source.at[rows], target.at[rows], sem)
    copy.start()
    return copy


def arrange_kernel(misfit, viscosity, friction_in, ice_mask_in, grounded_in, data, strips, edges,
                   misfit_half, viscosity_half, friction, ice_mask, grounded, sems):
    rows = friction.shape[0]
    copies = [
        pltpu.make_async_copy(source, target, sems.at[n])
        for n, (source, target) in enumerate(((friction_in, friction), (ice_mask_in, ice_mask), (grounded_in, grounded)))
    ]
    for t in range(2):
        lanes = pl.ds(t * LANES, LANES)
        for p in range(2):
            n = 2 * t + p
            for source, target, sem in ((misfit, misfit_half, 3 + n), (viscosity, viscosity_half, 7 + n)):
                copies.append(
                    pltpu.make_async_copy(source.at[:, p, :, lanes], target.at[n, :, pl.ds(0, rows)], sems.at[sem])
                )
    for copy in copies:
        copy.start()
    for copy in copies:
        copy.wait()
    sub = lax.broadcasted_iota(jnp.int32, (8, LANES), 0)
    misfit_rows = misfit_half.reshape(4, -1, LANES)
    viscosity_rows = viscosity_half.reshape(4, -1, LANES)

    def eight(i, carry):
        block = pl.ds(pl.multiple_of(8 * i, 8), 8)
        for t in range(2):
            lanes = pl.ds(t * LANES, LANES)
            ices = ice_mask[block, lanes].astype(F32)
            drags = friction[block, lanes] * grounded[block, lanes].astype(F32)
            for j in range(8):
                r = 8 * i + j
                ice, drag = ices[j : j + 1], drags[j : j + 1]
                for c in range(2):
                    for p in range(2):
                        v = misfit_rows[2 * t + p, pl.ds(8 * c * PITCH + r, 8, stride=PITCH), :]
                        data[r, t, 16 * c + 8 * p : 16 * c + 8 * p + 8, :] = v * ice
                for p in range(2):
                    data[r, t, 32 + 8 * p : 40 + 8 * p, :] = viscosity_rows[2 * t + p, pl.ds(r, 8, stride=PITCH), :]
                data[r, t, 48:56, :] = jnp.where(sub == 0, ice, jnp.where(sub == 1, drag, 0.0))
        return carry

    lax.fori_loop(0, rows // 8, eight, 0)
    corner = RIM0 * RIM0
    for side in range(2):
        low = jnp.zeros((8, LANES), F32)
        high = low
        for first in range(0, NP, 8):
            planes = slice(first, first + 8)
            strip = jnp.zeros((8, LANES), F32)
            for r in range(rows):
                at = r * RIM0
                strip = put(strip, data[r, side, planes, :], at if side == 0 else at + RIM0, RIM0, at)
            strips[side, planes, :] = strip
            at = first // 8 * corner
            low = put(low, strip, at, corner, at)
            high = put(high, strip, at + corner, corner, at)
        strips[side, NP : NP + 8, :] = low
        strips[side, NP + 8 : NP + 16, :] = high
    for t in range(2):
        edges[0, 8 * t : 8 * t + 8, :] = pair_rows([data[r, t, 48:56, :] for r in range(RIM0 - 1)])
        edges[1, 8 * t : 8 * t + 8, :] = pair_rows([data[rows - RIM0 + 1 + r, t, 48:56, :] for r in range(RIM0 - 1)])


def inner0_kernel(own, left, right, coarse, w_out, coef_out, scaled_out, data, diag, slope, across, wa, coef, scaled, sems):
    rows = own.shape[0]
    first, last = RIM0, RIM0 + rows

    def copy_row(r):
        for t in range(2):
            data[first + r, t] = own[r, t]

    rows_loop(0, rows, copy_row, 4)
    for r in range(rows):
        data[first + r, 2] = unpack_rim(left[0:NP, :], right[0:NP, :], r * RIM0, RIM0)
    half = first + rows // 2 - 1
    make_coefs(data, coef, scaled, diag, first + 1, half, 1.0, False, UNROLL0[2])
    copies = [copy_rows(coef, coef_out, sems.at[0], first + 1, half)]
    make_coefs(data, coef, scaled, diag, half, last - 1, 1.0, False, UNROLL0[2])
    copies.append(copy_rows(coef, coef_out, sems.at[1], half, last - 1))
    copies.append(copy_rows(scaled, scaled_out, sems.at[2], first + 1, last - 1))
    sweep(scaled, wa, coef, scaled, slope, across, first + 2, last - 2, False, UNROLL0)
    copies.append(copy_rows(wa, w_out, sems.at[3], first + 2, last - 2))

    def coefs_row(i):
        coarse[i, 32:56, :] = restrict_row(data, slice(32, 56), first + 2 * i)

    rows_loop(0, rows // 2, coefs_row, UNROLL_MOVE)
    remainders(wa, diag, data, diag, coef, slope, across, first + 3, last - 3, UNROLL0, 2)

    def target_row(i):
        coarse[i, 0:32, :] = restrict_row(diag, slice(0, 32), first + 2 * i)

    rows_loop(2, rows // 2 - 2, target_row, UNROLL_MOVE)
    for copy in copies:
        copy.wait()


def outer0_kernel(own, left, right, from_low, from_high, inner_coarse, w_in, coef_in, scaled_in,
                  coarse, strips1, edges1, w_out, coef_out, scaled_out,
                  data, diag, slope, across, wa, coef, scaled, sems):
    rows = own.shape[0]
    mine = SPAN - RIM0
    inner = RIM0 - 1
    thick = 64 * inner
    thin = thick + 32 * RIM0
    corner = thin + 16
    copies = []
    for face, start, rim_at, mine_at, x in (
        (from_low, 0, 0, RIM0, 0),
        (from_high, SPAN, SPAN + mine, SPAN, rows - mine),
    ):
        for r in range(mine):
            for t in range(2):
                data[mine_at + r, t] = own[x + r, t]
            data[mine_at + r, 2] = unpack_rim(left[0:NP, :], right[0:NP, :], (x + r) * RIM0, RIM0)
        skip = 1 if start == 0 else 0
        for t in range(2):
            for r in range(inner):
                at = 32 * (2 * r + t)
                data[rim_at + skip + r, t, 0:32, :] = face[at : at + 32, :]
                data[rim_at + skip + r, t, 48:56, :] = pair_row(face[thin + 8 * t : thin + 8 * t + 8, :], r)
            for r in range(RIM0):
                at = thick + 16 * (2 * r + t)
                data[rim_at + r, t, 32:48, :] = face[at : at + 16, :]
        for q in range(NP // 8):
            for r in range(RIM0):
                at = RIM0 * (RIM0 * q + r)
                data[rim_at + r, 2, 8 * q : 8 * q + 8, :] = unpack_rim(
                    face[corner : corner + 8, :], face[corner + 8 : corner + 16, :], at, RIM0
                )
    for start in (0, SPAN):
        make_coefs(data, coef, scaled, diag, start + 1, start + SPAN - 1, 1.0, False, 9)
    total = rows + 2 * RIM0
    shift = total - 2 * SPAN
    ranges = ((2, RIM0 + 1), (3, RIM0 + 1), (2, RIM0 + 2))
    arrays = ((coef, coef_out), (scaled, scaled_out), (wa, w_out))

    def store(n):
        (source, target), (low, high) = arrays[n], ranges[n]
        for side in range(2):
            begin = low if side == 0 else 2 * SPAN - high
            place = begin + (0 if side == 0 else shift)
            copy = pltpu.make_async_copy(
                source.at[pl.ds(begin, high - low)], target.at[pl.ds(place, high - low)], sems.at[2 * n + side]
            )
            copy.start()
            copies.append(copy)

    store(0)
    store(1)
    for start in (0, SPAN):
        sweep(scaled, wa, coef, scaled, slope, across, start + 2, start + SPAN - 2, False, (9, 7))
    store(2)

    def copy_coarse(i):
        coarse[i] = inner_coarse[i]

    rows_loop(0, rows // 2, copy_coarse, 4)
    for start in (0, SPAN):
        remainders(wa, diag, data, diag, coef, slope, across, start + 3, start + SPAN - 3, (7, 5), 2)
    for i in range(2):
        coarse[i, 0:32, :] = restrict_row(diag, slice(0, 32), RIM0 + 2 * i)
        coarse[rows // 2 - 2 + i, 0:32, :] = restrict_row(diag, slice(0, 32), SPAN + mine - 4 + 2 * i)
    group = LANES // STRIP1
    for side in range(2):
        for part in range(rows // 2 // group):
            for first in range(0, NP, 8):
                planes = slice(first, first + 8)
                strip = jnp.zeros((8, LANES), F32)
                for j in range(group):
                    at = j * STRIP1
                    shift1 = at if side == 0 else at + STRIP1
                    strip = put(strip, coarse[part * group + j, planes, :], shift1, STRIP1, at)
                strips1[side, part, planes, :] = strip
    inner1 = RIM1 - 1
    for face, base in enumerate((0, rows // 2 - inner1)):
        for j in range(0, inner1, 4):
            edges1[face, 2 * j : 2 * j + 8, :] = pair_rows([coarse[base + j + n, 48:56, :] for n in range(4)])
    for copy in copies:
        copy.wait()


def down12_kernel(own, sides, from_low, from_high, sides_low, sides_high, piece, w1_out, coef1_out, scaled1_out, w2_out, coef2_out, scaled2_out,
                  data1, diag1, slope1, across1, wa1, coef1, scaled1, data2, diag2, slope2, across2, wa2, coef2, scaled2, sems):
    rows = own.shape[0]
    total = rows + 2 * RIM1
    group = LANES // STRIP1
    parts = rows // group

    def rim(strips, r):
        part, j = r // group, r % group
        low, high = part * NP, (parts + part) * NP
        return unpack_rim(strips[low : low + NP, :], strips[high : high + NP, :], j * STRIP1, STRIP1)

    def copy_row(r):
        data1[RIM1 + r, 0] = own[r]

    rows_loop(0, rows, copy_row, 4)
    for r in range(rows):
        data1[RIM1 + r, 1] = rim(sides, r)
    inner = RIM1 - 1
    thick = 32 * inner
    thin = thick + 16 * RIM1
    for face, strips, base, skip, first in (
        (from_low, sides_low, 0, 1, rows - RIM1),
        (from_high, sides_high, RIM1 + rows, 0, 0),
    ):
        for r in range(inner):
            data1[base + skip + r, 0, 0:32, :] = face[32 * r : 32 * r + 32, :]
            at = thin + 8 * (r // 4)
            data1[base + skip + r, 0, 48:56, :] = pair_row(face[at : at + 8, :], r % 4)
        for r in range(RIM1):
            at = thick + 16 * r
            data1[base + r, 0, 32:48, :] = face[at : at + 16, :]
            data1[base + r, 1] = rim(strips, first + r)

    make_coefs(data1, coef1, scaled1, diag1, 1, total - 1, 0.25, False, UNROLL1[2])
    copies = [copy_rows(coef1, coef1_out, sems.at[0], 10, total - 10)]
    copies.append(copy_rows(scaled1, scaled1_out, sems.at[1], 11, total - 11))
    sweep(scaled1, wa1, coef1, scaled1, slope1, across1, 2, total - 2, False, UNROLL1)
    copies.append(copy_rows(wa1, w1_out, sems.at[2], 9, total - 9))
    remainders(wa1, diag1, data1, diag1, coef1, slope1, across1, 3, total - 3, UNROLL1, 2)

    rows2 = rows // 2
    total2 = rows2 + 2 * RIM2

    def coefs_row(i):
        data2[i, 0, 32:56, :] = restrict_row(data1, slice(32, 56), 1 + 2 * i)

    rows_loop(0, total2, coefs_row, UNROLL_MOVE)

    def target_row(i):
        data2[i, 0, 0:32, :] = restrict_row(diag1, slice(0, 32), 1 + 2 * i)

    rows_loop(1, total2 - 1, target_row, UNROLL_MOVE)

    make_coefs(data2, coef2, scaled2, diag2, 1, total2 - 1, 0.0625, False, UNROLL2[2])
    copies.append(copy_rows(coef2, coef2_out, sems.at[3], 2, total2 - 2))
    copies.append(copy_rows(scaled2, scaled2_out, sems.at[4], 3, total2 - 3))
    sweep(scaled2, wa2, coef2, scaled2, slope2, across2, 2, total2 - 2, False, UNROLL2)
    copies.append(copy_rows(wa2, w2_out, sems.at[5], 2, total2 - 2))
    remainders(wa2, diag2, data2, diag2, coef2, slope2, across2, RIM2, RIM2 + rows2, UNROLL2, 1)

    rows3 = rows2 // 2
    width = LANES // rows3
    for first in range(0, NP, 8):
        planes = slice(first, first + 8)
        source = diag2 if first < 32 else data2
        strip = jnp.zeros((8, LANES), F32)
        for i in range(rows3):
            strip = put(strip, restrict_row(source, planes, RIM2 + 2 * i), i * width, width, i * width)
        for d in range(piece.shape[0]):
            piece[d, planes, :] = strip
    for copy in copies:
        copy.wait()


def up_kernel(place, pieces, w0_in, coef0_in, scaled0_in, w1_in, coef1_in, scaled1_in, w2_in, coef2_in, scaled2_in, result,
              data3, coef3, scaled3, wa3, wb3, slope3, across3, w2, coef2, scaled2, wa2, wb2, w1, coef1, scaled1, wa1, wb1,
              w0, coef0, scaled0, wa0, wb0, slope0, across0, result_half, sems):
    slope1, across1 = (v.at[pl.ds(0, wa1.shape[0]), pl.ds(0, 2)] for v in (slope0, across0))
    slope2, across2 = (v.at[pl.ds(0, wa2.shape[0]), pl.ds(0, 1)] for v in (slope0, across0))
    copies = []
    for source, target, first in (
        (w2_in, w2, 2), (coef2_in, coef2, 2), (scaled2_in, scaled2, 3),
        (w1_in, w1, 9), (coef1_in, coef1, 10), (scaled1_in, scaled1, 11),
        (w0_in, w0, 2), (coef0_in, coef0, 2), (scaled0_in, scaled0, 3),
    ):
        copies.append(copy_rows(source, target, sems.at[len(copies)], first, source.shape[0] - first))
    devices_y, devices_x = pieces.shape[0], pieces.shape[1]
    rows3 = devices_y
    width = LANES // devices_y
    whole = devices_x * rows3
    zero = jnp.zeros((NP, LANES), F32)
    for r in range(RIM3):
        for end in (r, RIM3 + whole + r):
            data3[end, 0] = zero
            wa3[end, 0] = zero[:32]
            wb3[end, 0] = zero[:32]
            scaled3[end, 0] = zero[:32]
            slope3[end, 0] = zero[:32]
            coef3[end, 0] = jnp.zeros((8 * NC, LANES), F32)

    def assemble(d):
        for i in range(rows3):
            line = jnp.zeros((NP, LANES), F32)
            for j in range(devices_y):
                line = put(line, pieces[j, d], (j - i) * width, width, j * width)
            data3[RIM3 + d * rows3 + i, 0] = line

    rows_loop(0, devices_x, assemble, 4)
    first, last = RIM3, RIM3 + whole
    make_coefs(data3, coef3, scaled3, None, first, last, 0.25 ** (LEVELS - 1), True, UNROLL3[2])

    gx, gy = place[0], place[1]

    def coarse_sweep(source, target, extent):
        begin, end = (first, last) if extent is None else (0, extent)
        start = 0 if extent is None else first + jnp.clip(gx * rows3 - (extent - rows3) // 2, 0, whole - extent)
        around = 0 if extent is None else 1

        def look(r):
            r = start + r
            norths, souths = shifted([source[r, 0]], True)
            slope3[r, 0] = norths[0] - souths[0]
            across3[r, 0] = twice(coef3[r, 0, 16:32, :]) * norths[0] + twice(coef3[r, 0, 32:48, :]) * souths[0]

        rows_loop(begin - around, end + around, look, UNROLL3[0] if extent is None else extent + 2)

        def row(r):
            r = start + r
            here, total = off_diagonal(source, coef3, slope3, across3, r, 0)
            target[r, 0] = (1.0 - OMEGA) * here + scaled3[r, 0] + coef3[r, 0, 88:120, :] * total

        rows_loop(begin, end, row, UNROLL3[1])

    coarse_sweep(scaled3, wa3, None)
    done = 2
    narrow = [(None, COARSE_ITERS - 9), (rows3 + 20, COARSE_ITERS - 5), (rows3 + 12, COARSE_ITERS)]
    buffers = (wa3, wb3)
    for extent, until in narrow:
        if extent is not None and extent > whole:
            extent = None

        def two_sweeps(i, carry, extent=extent, pair=buffers):
            coarse_sweep(pair[0], pair[1], extent)
            coarse_sweep(pair[1], pair[0], extent)
            return carry

        if (until - done) // 2:
            lax.fori_loop(0, (until - done) // 2, two_sweeps, 0)
        if (until - done) % 2:
            coarse_sweep(buffers[0], buffers[1], extent)
            buffers = buffers[::-1]
        done = until
    solved = buffers[0]

    lane = lane_ids(32)
    y = jnp.where(lane < 96, lane, lane - LANES)
    column = gy * width + (y + LANES) // 2 - LANES // 2
    inside = (column >= 0) & (column < LANES)
    pick = jnp.where(inside, column, 0)

    for copy in copies[:3]:
        copy.wait()
    rows2 = 2 * rows3
    for i in range(rows3 + 2 * RIM3):
        add = jnp.where(inside, gather_lanes(solved[gx * rows3 + i, 0], pick), 0.0)
        for r in (2 * i + 2, 2 * i + 3):
            wa2[r, 0] = w2[r, 0] + add
    total2 = rows2 + 2 * RIM2
    sweep(wa2, wb2, coef2, scaled2, slope2, across2, 3, total2 - 3, False, UNROLL2)
    sweep(wb2, wa2, coef2, scaled2, slope2, across2, 4, total2 - 4, False, UNROLL2)


    for copy in copies[3:6]:
        copy.wait()

    def add1(r):
        adds = prolong_row([wa2[r, 0]], 2)
        for t in range(2):
            for fine in (2 * r + 1, 2 * r + 2):
                wa1[fine, t] = w1[fine, t] + adds[t]

    rows_loop(4, total2 - 4, add1, 12)
    total1 = 2 * rows2 + 2 * RIM1
    sweep(wa1, wb1, coef1, scaled1, slope1, across1, 11, total1 - 11, False, UNROLL1_UP)
    sweep(wb1, wa1, coef1, scaled1, slope1, across1, 12, total1 - 12, False, UNROLL1_UP)


    for copy in copies[6:]:
        copy.wait()

    def add0(r):
        adds = prolong_row([wa1[r, t] for t in range(2)], 3)
        for t in range(3):
            for fine in (2 * r - 22, 2 * r - 21):
                wa0[fine, t] = w0[fine, t] + adds[t]

    rows_loop(12, total1 - 12, add0, 18)
    rows0 = 4 * rows2
    total0 = rows0 + 2 * RIM0
    sweep(wa0, wb0, coef0, scaled0, slope0, across0, 3, total0 - 3, False, UNROLL0_UP)

    result_rows = result_half.reshape(4, -1, LANES)

    def emit(r, t, value):
        for c in range(2):
            for p in range(2):
                start = 8 * c * PITCH + r - RIM0
                result_rows[2 * t + p, pl.ds(start, 8, stride=PITCH), :] = value[16 * c + 8 * p : 16 * c + 8 * p + 8]

    sweep(wb0, None, coef0, scaled0, slope0, across0, RIM0, RIM0 + rows0, False, UNROLL0_UP, tiles=2, emit=emit)
    copies = [
        pltpu.make_async_copy(
            result_half.at[2 * t + p, :, pl.ds(0, rows0)], result.at[:, p, :, pl.ds(t * LANES, LANES)], sems.at[2 * t + p]
        )
        for t in range(2)
        for p in range(2)
    ]
    for copy in copies:
        copy.start()
    for copy in copies:
        copy.wait()


def shape(*dims):
    return jax.ShapeDtypeStruct(dims, F32)


def stored(*dims):
    return pltpu.HBM(dims, F32)


def in_hbm(arrays):
    return [pltpu.with_memory_space_constraint(v, pltpu.HBM) for v in arrays]


VM = pl.BlockSpec(memory_space=pltpu.VMEM)
SM = pl.BlockSpec(memory_space=pltpu.SMEM)
HB = pl.BlockSpec(memory_space=pl.ANY)
PARAMS = pltpu.CompilerParams(vmem_limit_bytes=VMEM_DOWN)


def buffers(rows, tiles, names):
    planes = {"data": NP, "coef": 8 * NC}
    return [pltpu.VMEM((rows, tiles, planes.get(name, 32), LANES), F32) for name in names]


def per_device(misfit, viscosity, friction, ice_mask, grounded):
    rows, columns = friction.shape
    gx, gy = lax.axis_index("gx"), lax.axis_index("gy")
    nx, ny = lax.axis_size("gx"), lax.axis_size("gy")
    upward = [(i, i + 1) for i in range(nx - 1)]
    downward = [(i + 1, i) for i in range(nx - 1)]

    def beside(strips):
        every = lax.all_gather(strips, "gy", axis=0)
        left = lax.dynamic_index_in_dim(every, jnp.maximum(gy - 1, 0), 0, keepdims=False)[1]
        right = lax.dynamic_index_in_dim(every, jnp.minimum(gy + 1, ny - 1), 0, keepdims=False)[0]
        return jnp.where(gy > 0, left, 0.0), jnp.where(gy < ny - 1, right, 0.0)

    data0, strips0, edges0 = pl.pallas_call(
        arrange_kernel,
        out_shape=(shape(rows, 2, NP, LANES), shape(2, NP + 16, LANES), shape(2, 16, LANES)),
        in_specs=[HB] * 5,
        out_specs=(VM, VM, VM),
        scratch_shapes=[
            pltpu.VMEM((4, 16, PITCH, LANES), F32),
            pltpu.VMEM((4, 8, PITCH, LANES), F32),
            pltpu.VMEM((rows, columns), F32),
            pltpu.VMEM((rows, columns), jnp.int32),
            pltpu.VMEM((rows, columns), jnp.int32),
            pltpu.SemaphoreType.DMA((11,)),
        ],
        compiler_params=PARAMS,
        name="arrange",
    )(
        *in_hbm(
            [v.reshape(-1, 2, rows, columns) for v in (misfit, viscosity)] + [friction, ice_mask, grounded]
        )
    )
    left, right = beside(strips0)
    inner = RIM0 - 1

    def face0(which, first, first_inner):
        corner = slice(NP + 8 * which, NP + 8 * which + 8)
        parts = (
            data0[first_inner : first_inner + inner, :, 0:32],
            data0[first : first + RIM0, :, 32:48],
            edges0[which],
            left[corner],
            right[corner],
        )
        return jnp.concatenate([v.reshape(-1, LANES) for v in parts], 0)

    low_face = face0(0, 0, 0)
    high_face = face0(1, rows - RIM0, rows - inner)
    from_low = lax.ppermute(high_face, "gx", upward)
    from_high = lax.ppermute(low_face, "gx", downward)

    total0 = rows + 2 * RIM0
    names = ("data", "diag", "slope", "across", "w", "coef", "scaled")
    rows1 = rows // 2
    group = LANES // STRIP1
    field0 = stored(total0, 3, 32, LANES)
    up0 = (field0, stored(total0, 3, 8 * NC, LANES), field0)
    inner1 = RIM1 - 1
    inner_coarse, *ups0 = pl.pallas_call(
        inner0_kernel,
        out_shape=(shape(rows1, NP, LANES),) + up0,
        in_specs=[VM] * 3,
        out_specs=(VM, HB, HB, HB),
        scratch_shapes=buffers(total0, 3, names) + [pltpu.SemaphoreType.DMA((4,))],
        compiler_params=PARAMS,
        cost_estimate=pl.CostEstimate(flops=40_000_000, bytes_accessed=20_000_000, transcendentals=0),
        name="inner0",
    )(data0, left, right)
    data1, strips1, edges1, w0, coef0, scaled0 = pl.pallas_call(
        outer0_kernel,
        out_shape=(
            shape(rows1, NP, LANES),
            shape(2, rows1 // group, NP, LANES),
            shape(2, 2 * inner1, LANES),
        )
        + up0,
        in_specs=[VM] * 6 + [HB] * 3,
        out_specs=(VM, VM, VM, HB, HB, HB),
        input_output_aliases={6: 3, 7: 4, 8: 5},
        scratch_shapes=buffers(2 * SPAN, 3, names) + [pltpu.SemaphoreType.DMA((6,))],
        compiler_params=PARAMS,
        name="outer0",
    )(data0, left, right, from_low, from_high, inner_coarse, *in_hbm(ups0))

    def face1(which, first, first_inner):
        parts = (data1[first_inner : first_inner + inner1, 0:32], data1[first : first + RIM1, 32:48], edges1[which])
        return jnp.concatenate([v.reshape(-1, LANES) for v in parts], 0)

    from_low = lax.ppermute(face1(1, rows1 - RIM1, rows1 - inner1), "gx", upward)
    from_high = lax.ppermute(face1(0, 0, 0), "gx", downward)
    left, right = (v.reshape(-1, LANES) for v in beside(strips1))
    sides = jnp.concatenate([left, right], 0)
    sides_low = lax.ppermute(sides, "gx", upward)
    sides_high = lax.ppermute(sides, "gx", downward)

    total1 = rows1 + 2 * RIM1
    rows2 = rows1 // 2
    total2 = rows2 + 2 * RIM2
    field1 = stored(total1, 2, 32, LANES)
    field2 = stored(total2, 1, 32, LANES)
    piece, w1, coef1, scaled1, w2, coef2, scaled2 = pl.pallas_call(
        down12_kernel,
        out_shape=(
            shape(nx, NP, LANES),
            field1,
            stored(total1, 2, 8 * NC, LANES),
            field1,
            field2,
            stored(total2, 1, 8 * NC, LANES),
            field2,
        ),
        in_specs=[VM] * 6,
        out_specs=(VM,) + (HB,) * 6,
        scratch_shapes=buffers(total1, 2, names) + buffers(total2, 1, names) + [pltpu.SemaphoreType.DMA((6,))],
        compiler_params=PARAMS,
        name="down12",
    )(data1, sides, from_low, from_high, sides_low, sides_high)

    pieces = lax.all_gather(lax.all_to_all(piece, "gx", 0, 0), "gy", axis=0)

    rows3 = rows2 // 2
    total3 = nx * rows3 + 2 * RIM3
    ups = ("w", "coef", "scaled", "w", "w")
    result = pl.pallas_call(
        up_kernel,
        out_shape=shape(16, 2, rows, columns),
        in_specs=[SM, VM] + [HB] * 9,
        out_specs=HB,
        scratch_shapes=buffers(total3, 1, ("data", "coef", "scaled", "w", "w", "slope", "across"))
        + buffers(total2, 1, ups)
        + buffers(total1, 2, ups)
        + buffers(total0, 3, ups)
        + buffers(max(total0, total1), 3, ("slope", "across"))
        + [pltpu.VMEM((4, 16, PITCH, LANES), F32), pltpu.SemaphoreType.DMA((9,))],
        compiler_params=pltpu.CompilerParams(vmem_limit_bytes=VMEM_UP),
        name="up",
    )(
        jnp.stack([gx, gy]).astype(jnp.int32),
        pieces,
        *in_hbm([w0, coef0, scaled0, w1, coef1, scaled1, w2, coef2, scaled2]),
    )
    return result.reshape(misfit.shape)


def solution(mesh):
    placed = (
        P(None, None, "gx", "gy"),
        P(None, "gx", "gy"),
        P("gx", "gy"),
        P("gx", "gy"),
        P("gx", "gy"),
    )
    return jax.shard_map(
        per_device, mesh=mesh, in_specs=placed, out_specs=P(None, None, "gx", "gy"), check_vma=False
    )
```

```python
import functools

import jax
import jax.numpy as jnp
from jax import lax
from jax.experimental import pallas as pl
from jax.experimental.pallas import tpu as pltpu
from jax.sharding import PartitionSpec as P

LEVELS = 4
COARSE_ITERS = 20
OMEGA = 0.6
CROSS = 0.75
NP = 56
LANES = 128
RIM0 = 4
RIM1 = 13
RIM2 = 6
RIM3 = 2
STRIP1 = 16
NC = 15
PITCH = 40
SPAN = 11
VMEM_DOWN = 28 * 1024 * 1024
VMEM_UP = 60 * 1024 * 1024
F32 = jnp.float32
UNROLL0 = (18, 6, 4)
UNROLL1 = (38, 18, 20)
UNROLL2 = (18, 16, 18)
UNROLL3 = (32, 32, 16)
UNROLL0_UP = (36, 34)
UNROLL1_UP = (22, 20)
UNROLL_MOVE = 8


def rows_loop(first, last, body, unroll):
    count = (last - first) // unroll

    def step(i, carry):
        for j in range(unroll):
            body(first + i * unroll + j)
        return carry

    if count:
        lax.fori_loop(0, count, step, 0)
    for r in range(first + count * unroll, last):
        body(r)


def lane_ids(rows=8):
    return lax.broadcasted_iota(jnp.int32, (rows, LANES), 1)


def shifted(tiles, closed):
    lane = lax.broadcasted_iota(jnp.int32, tiles[0].shape, 1)
    up = [pltpu.roll(v, LANES - 1, 1) for v in tiles]
    down = [pltpu.roll(v, 1, 1) for v in tiles]
    n = len(tiles)
    if closed:
        zero = jnp.zeros_like(tiles[0])
        return (
            [jnp.where(lane == LANES - 1, zero, v) for v in up],
            [jnp.where(lane == 0, zero, v) for v in down],
        )
    if n == 1:
        return up, down
    return (
        [jnp.where(lane == LANES - 1, up[(t + 1) % n], up[t]) for t in range(n)],
        [jnp.where(lane == 0, down[(t - 1) % n], down[t]) for t in range(n)],
    )


def twice(v):
    return jnp.concatenate([v, v], 0)


def make_coefs(data, coef, scaled, diag, first, last, horizontal, closed, unroll):
    nt = data.shape[1]
    sub = lax.broadcasted_iota(jnp.int32, (8, LANES), 0)

    def row(r):
        mids = [data[r, t, 32:48, :] for t in range(nt)]
        norths, souths = shifted(mids, closed)
        for t in range(nt):
            mid = mids[t]
            west = (0.5 * horizontal) * (mid + data[r - 1, t, 32:48, :])
            east = (0.5 * horizontal) * (mid + data[r + 1, t, 32:48, :])
            north = (0.5 * horizontal) * (mid + norths[t])
            south = (0.5 * horizontal) * (mid + souths[t])
            low, high = mid[:8], mid[8:]
            inner = 2.0 * (low + high)
            outer = jnp.where(sub == 7, 0.0, 2.0 * (high + pltpu.roll(low, 7, 0)))
            outer_down = pltpu.roll(outer, 1, 0)
            coef[r, t, 0:16, :] = west
            coef[r, t, 16:32, :] = north
            coef[r, t, 32:48, :] = south
            coef[r, t, 48:64, :] = (CROSS * horizontal) * mid
            coef[r, t, 64:72, :] = inner
            coef[r, t, 72:80, :] = outer
            coef[r, t, 80:88, :] = outer_down
            ice = data[r, t, 48:49, :]
            drag = data[r, t, 49:50, :]
            bottom = jnp.where(sub == 0, drag, 0.0)
            upright = jnp.concatenate([inner + outer_down + bottom, inner + outer], 0)
            along_x = east + west
            along_y = north + south
            rest = 1.0 - ice
            for c, lateral in enumerate((4.0 * along_x + along_y, along_x + 4.0 * along_y)):
                diagonal = ice * (lateral + upright) + rest
                inverse = OMEGA / diagonal
                coef[r, t, 88 + 16 * c : 104 + 16 * c, :] = ice * inverse
                scaled[r, t, 16 * c : 16 * c + 16, :] = inverse * data[r, t, 16 * c : 16 * c + 16, :]
                if diag is not None:
                    diag[r, t, 16 * c : 16 * c + 16, :] = diagonal

    rows_loop(first, last, row, unroll)


def prepare(w, coef, slope, across, first, last, closed, unroll):
    nt = w.shape[1]

    def row(r):
        norths, souths = shifted([w[r, t] for t in range(nt)], closed)
        for t in range(nt):
            slope[r, t] = norths[t] - souths[t]
            across[r, t] = twice(coef[r, t, 16:32, :]) * norths[t] + twice(coef[r, t, 32:48, :]) * souths[t]

    rows_loop(first, last, row, unroll)


def off_diagonal(w, coef, slope, across, r, t):
    here = w[r, t]
    along = twice(coef[r + 1, t, 0:16, :]) * w[r + 1, t] + twice(coef[r, t, 0:16, :]) * w[r - 1, t]
    side = across[r, t]
    mixed = slope[r + 1, t] - slope[r - 1, t]
    cross = coef[r, t, 48:64, :]
    inner = coef[r, t, 64:72, :]
    outer = coef[r, t, 72:80, :]
    outer_down = coef[r, t, 80:88, :]
    parts = []
    for c in range(2):
        mine = slice(16 * c, 16 * c + 16)
        other = slice(16 - 16 * c, 32 - 16 * c)
        low, high = here[16 * c : 16 * c + 8], here[16 * c + 8 : 16 * c + 16]
        column = jnp.concatenate(
            [inner * high + outer_down * pltpu.roll(high, 1, 0), inner * low + outer * pltpu.roll(low, 7, 0)], 0
        )
        if c == 0:
            lateral = 4.0 * along[mine] + side[mine]
        else:
            lateral = along[mine] + 4.0 * side[mine]
        parts.append(lateral + cross * mixed[other] + column)
    return here, jnp.concatenate(parts, 0)


def sweep(w, new, coef, scaled, slope, across, first, last, closed, unroll, tiles=None, emit=None):
    look, unroll = unroll[:2]
    nt = w.shape[1]
    prepare(w, coef, slope, across, first - 1, last + 1, closed, look)

    def row(r):
        for t in range(nt if tiles is None else tiles):
            here, total = off_diagonal(w, coef, slope, across, r, t)
            value = (1.0 - OMEGA) * here + scaled[r, t] + coef[r, t, 88:120, :] * total
            if emit is None:
                new[r, t] = value
            else:
                emit(r, t, value)

    rows_loop(first, last, row, unroll)


def remainders(w, out, data, diag, coef, slope, across, first, last, unroll, tiles):
    look, unroll = unroll[:2]
    prepare(w, coef, slope, across, first - 1, last + 1, False, look)

    def row(r):
        for t in range(tiles):
            here, total = off_diagonal(w, coef, slope, across, r, t)
            out[r, t] = data[r, t, 0:32, :] + data[r, t, 48:49, :] * total - diag[r, t] * here

    rows_loop(first, last, row, unroll)


def gather_lanes(v, index):
    return jnp.take_along_axis(v, index, axis=1, mode="promise_in_bounds")


def halve(first, second):
    lane = lax.broadcasted_iota(jnp.int32, first.shape, 1)
    even = (2 * lane) % LANES
    low = gather_lanes(first + pltpu.roll(first, LANES - 1, 1), even)
    if second is None:
        return low
    high = gather_lanes(second + pltpu.roll(second, LANES - 1, 1), even)
    return jnp.where(lane < LANES // 2, low, high)


def restrict_row(source, planes, r):
    both = [source[r, t, planes, :] + source[r + 1, t, planes, :] for t in range(min(2, source.shape[1]))]
    return 0.25 * halve(both[0], both[1] if len(both) > 1 else None)


def prolong_row(tiles, fine_tiles):
    lane = lax.broadcasted_iota(jnp.int32, tiles[0].shape, 1)
    low = lane // 2
    high = LANES // 2 + lane // 2
    first = tiles[0]
    last = tiles[-1]
    out = [gather_lanes(first, low)]
    if fine_tiles == 2:
        out.append(gather_lanes(first, high))
    else:
        out.append(gather_lanes(first, high))
        out.append(gather_lanes(last, jnp.where(lane < LANES // 2, low, high)))
    return out


def put(strip, v, shift, width, at):
    lane = lax.broadcasted_iota(jnp.int32, v.shape, 1)
    rolled = pltpu.roll(v, shift % LANES, 1) if shift % LANES else v
    return jnp.where((lane >= at) & (lane < at + width), rolled, strip)


def unpack_rim(left, right, at, width):
    lane = lax.broadcasted_iota(jnp.int32, left.shape, 1)
    to_low = pltpu.roll(right, (LANES - at) % LANES, 1) if at else right
    shift = (2 * LANES - width - at) % LANES
    to_high = pltpu.roll(left, shift, 1) if shift else left
    return jnp.where(lane < LANES // 2, to_low, to_high)


def pair_rows(tiles):
    sub = lax.broadcasted_iota(jnp.int32, (8, LANES), 0)
    out = tiles[0]
    for j in range(1, len(tiles)):
        out = jnp.where(sub >= 2 * j, pltpu.roll(tiles[j], 2 * j, 0), out)
    return out


def pair_row(tile, j):
    return pltpu.roll(tile, 8 - 2 * j, 0) if j else tile


def copy_rows(source, target, sem, first, last):
    rows = pl.ds(first, last - first)
    copy = pltpu.make_async_copy(source.at[rows], target.at[rows], sem)
    copy.start()
    return copy


def arrange_kernel(misfit, viscosity, friction_in, ice_mask_in, grounded_in, data, strips, edges,
                   misfit_half, viscosity_half, friction, ice_mask, grounded, sems):
    rows = friction.shape[0]
    copies = [
        pltpu.make_async_copy(source, target, sems.at[n])
        for n, (source, target) in enumerate(((friction_in, friction), (ice_mask_in, ice_mask), (grounded_in, grounded)))
    ]
    for t in range(2):
        lanes = pl.ds(t * LANES, LANES)
        for p in range(2):
            n = 2 * t + p
            for source, target, sem in ((misfit, misfit_half, 3 + n), (viscosity, viscosity_half, 7 + n)):
                copies.append(
                    pltpu.make_async_copy(source.at[:, p, :, lanes], target.at[n, :, pl.ds(0, rows)], sems.at[sem])
                )
    for copy in copies:
        copy.start()
    sub = lax.broadcasted_iota(jnp.int32, (8, LANES), 0)
    misfit_rows = misfit_half.reshape(4, -1, LANES)
    viscosity_rows = viscosity_half.reshape(4, -1, LANES)

    def eight(t, i, carry):
        block = pl.ds(pl.multiple_of(8 * i, 8), 8)
        lanes = pl.ds(t * LANES, LANES)
        ices = ice_mask[block, lanes].astype(F32)
        drags = friction[block, lanes] * grounded[block, lanes].astype(F32)
        for j in range(8):
            r = 8 * i + j
            ice, drag = ices[j : j + 1], drags[j : j + 1]
            for c in range(2):
                for p in range(2):
                    v = misfit_rows[2 * t + p, pl.ds(8 * c * PITCH + r, 8, stride=PITCH), :]
                    data[r, t, 16 * c + 8 * p : 16 * c + 8 * p + 8, :] = v * ice
            for p in range(2):
                data[r, t, 32 + 8 * p : 40 + 8 * p, :] = viscosity_rows[2 * t + p, pl.ds(r, 8, stride=PITCH), :]
            data[r, t, 48:56, :] = jnp.where(sub == 0, ice, jnp.where(sub == 1, drag, 0.0))
        return carry

    for copy in copies[:3]:
        copy.wait()
    for t in range(2):
        for copy in copies[3 + 4 * t : 7 + 4 * t]:
            copy.wait()
        lax.fori_loop(0, rows // 8, functools.partial(eight, t), 0)
    corner = RIM0 * RIM0
    for side in range(2):
        low = jnp.zeros((8, LANES), F32)
        high = low
        for first in range(0, NP, 8):
            planes = slice(first, first + 8)
            strip = jnp.zeros((8, LANES), F32)
            for r in range(rows):
                at = r * RIM0
                strip = put(strip, data[r, side, planes, :], at if side == 0 else at + RIM0, RIM0, at)
            strips[side, planes, :] = strip
            at = first // 8 * corner
            low = put(low, strip, at, corner, at)
            high = put(high, strip, at + corner, corner, at)
        strips[side, NP : NP + 8, :] = low
        strips[side, NP + 8 : NP + 16, :] = high
    for t in range(2):
        edges[0, 8 * t : 8 * t + 8, :] = pair_rows([data[r, t, 48:56, :] for r in range(RIM0 - 1)])
        edges[1, 8 * t : 8 * t + 8, :] = pair_rows([data[rows - RIM0 + 1 + r, t, 48:56, :] for r in range(RIM0 - 1)])


def inner0_kernel(own, left, right, coarse, w_out, coef_out, scaled_out, data, diag, slope, across, wa, coef, scaled, sems):
    rows = own.shape[0]
    first, last = RIM0, RIM0 + rows

    def copy_row(r):
        for t in range(2):
            data[first + r, t] = own[r, t]

    rows_loop(0, rows, copy_row, 4)
    for r in range(rows):
        data[first + r, 2] = unpack_rim(left[0:NP, :], right[0:NP, :], r * RIM0, RIM0)
    half = first + rows // 2 - 1
    make_coefs(data, coef, scaled, diag, first + 1, half, 1.0, False, UNROLL0[2])
    copies = [copy_rows(coef, coef_out, sems.at[0], first + 1, half)]
    make_coefs(data, coef, scaled, diag, half, last - 1, 1.0, False, UNROLL0[2])
    copies.append(copy_rows(coef, coef_out, sems.at[1], half, last - 1))
    copies.append(copy_rows(scaled, scaled_out, sems.at[2], first + 1, last - 1))
    sweep(scaled, wa, coef, scaled, slope, across, first + 2, last - 2, False, UNROLL0)
    copies.append(copy_rows(wa, w_out, sems.at[3], first + 2, last - 2))

    def coefs_row(i):
        coarse[i, 32:56, :] = restrict_row(data, slice(32, 56), first + 2 * i)

    rows_loop(0, rows // 2, coefs_row, UNROLL_MOVE)
    remainders(wa, diag, data, diag, coef, slope, across, first + 3, last - 3, UNROLL0, 2)

    def target_row(i):
        coarse[i, 0:32, :] = restrict_row(diag, slice(0, 32), first + 2 * i)

    rows_loop(2, rows // 2 - 2, target_row, UNROLL_MOVE)
    for copy in copies:
        copy.wait()


def outer0_kernel(own, left, right, from_low, from_high, inner_coarse, w_in, coef_in, scaled_in,
                  coarse, strips1, edges1, w_out, coef_out, scaled_out,
                  data, diag, slope, across, wa, coef, scaled, sems):
    rows = own.shape[0]
    mine = SPAN - RIM0
    inner = RIM0 - 1
    thick = 64 * inner
    thin = thick + 32 * RIM0
    corner = thin + 16
    copies = []
    for face, start, rim_at, mine_at, x in (
        (from_low, 0, 0, RIM0, 0),
        (from_high, SPAN, SPAN + mine, SPAN, rows - mine),
    ):
        for r in range(mine):
            for t in range(2):
                data[mine_at + r, t] = own[x + r, t]
            data[mine_at + r, 2] = unpack_rim(left[0:NP, :], right[0:NP, :], (x + r) * RIM0, RIM0)
        skip = 1 if start == 0 else 0
        for t in range(2):
            for r in range(inner):
                at = 32 * (2 * r + t)
                data[rim_at + skip + r, t, 0:32, :] = face[at : at + 32, :]
                data[rim_at + skip + r, t, 48:56, :] = pair_row(face[thin + 8 * t : thin + 8 * t + 8, :], r)
            for r in range(RIM0):
                at = thick + 16 * (2 * r + t)
                data[rim_at + r, t, 32:48, :] = face[at : at + 16, :]
        for q in range(NP // 8):
            for r in range(RIM0):
                at = RIM0 * (RIM0 * q + r)
                data[rim_at + r, 2, 8 * q : 8 * q + 8, :] = unpack_rim(
                    face[corner : corner + 8, :], face[corner + 8 : corner + 16, :], at, RIM0
                )
    for start in (0, SPAN):
        make_coefs(data, coef, scaled, diag, start + 1, start + SPAN - 1, 1.0, False, 9)
    total = rows + 2 * RIM0
    shift = total - 2 * SPAN
    ranges = ((2, RIM0 + 1), (3, RIM0 + 1), (2, RIM0 + 2))
    arrays = ((coef, coef_out), (scaled, scaled_out), (wa, w_out))

    def store(n):
        (source, target), (low, high) = arrays[n], ranges[n]
        for side in range(2):
            begin = low if side == 0 else 2 * SPAN - high
            place = begin + (0 if side == 0 else shift)
            copy = pltpu.make_async_copy(
                source.at[pl.ds(begin, high - low)], target.at[pl.ds(place, high - low)], sems.at[2 * n + side]
            )
            copy.start()
            copies.append(copy)

    store(0)
    store(1)
    for start in (0, SPAN):
        sweep(scaled, wa, coef, scaled, slope, across, start + 2, start + SPAN - 2, False, (9, 7))
    store(2)

    def copy_coarse(i):
        coarse[i] = inner_coarse[i]

    rows_loop(0, rows // 2, copy_coarse, 4)
    for start in (0, SPAN):
        remainders(wa, diag, data, diag, coef, slope, across, start + 3, start + SPAN - 3, (7, 5), 2)
    for i in range(2):
        coarse[i, 0:32, :] = restrict_row(diag, slice(0, 32), RIM0 + 2 * i)
        coarse[rows // 2 - 2 + i, 0:32, :] = restrict_row(diag, slice(0, 32), SPAN + mine - 4 + 2 * i)
    group = LANES // STRIP1
    for side in range(2):
        for part in range(rows // 2 // group):
            for first in range(0, NP, 8):
                planes = slice(first, first + 8)
                strip = jnp.zeros((8, LANES), F32)
                for j in range(group):
                    at = j * STRIP1
                    shift1 = at if side == 0 else at + STRIP1
                    strip = put(strip, coarse[part * group + j, planes, :], shift1, STRIP1, at)
                strips1[side, part, planes, :] = strip
    inner1 = RIM1 - 1
    for face, base in enumerate((0, rows // 2 - inner1)):
        for j in range(0, inner1, 4):
            edges1[face, 2 * j : 2 * j + 8, :] = pair_rows([coarse[base + j + n, 48:56, :] for n in range(4)])
    for copy in copies:
        copy.wait()


def down12_kernel(own, sides, from_low, from_high, sides_low, sides_high, piece, w1_out, coef1_out, scaled1_out, w2_out, coef2_out, scaled2_out,
                  data1, diag1, slope1, across1, wa1, coef1, scaled1, data2, diag2, slope2, across2, wa2, coef2, scaled2, sems):
    rows = own.shape[0]
    total = rows + 2 * RIM1
    group = LANES // STRIP1
    parts = rows // group

    def rim(strips, r):
        part, j = r // group, r % group
        low, high = part * NP, (parts + part) * NP
        return unpack_rim(strips[low : low + NP, :], strips[high : high + NP, :], j * STRIP1, STRIP1)

    def copy_row(r):
        data1[RIM1 + r, 0] = own[r]

    rows_loop(0, rows, copy_row, 4)
    for r in range(rows):
        data1[RIM1 + r, 1] = rim(sides, r)
    inner = RIM1 - 1
    thick = 32 * inner
    thin = thick + 16 * RIM1
    for face, strips, base, skip, first in (
        (from_low, sides_low, 0, 1, rows - RIM1),
        (from_high, sides_high, RIM1 + rows, 0, 0),
    ):
        for r in range(inner):
            data1[base + skip + r, 0, 0:32, :] = face[32 * r : 32 * r + 32, :]
            at = thin + 8 * (r // 4)
            data1[base + skip + r, 0, 48:56, :] = pair_row(face[at : at + 8, :], r % 4)
        for r in range(RIM1):
            at = thick + 16 * r
            data1[base + r, 0, 32:48, :] = face[at : at + 16, :]
            data1[base + r, 1] = rim(strips, first + r)

    make_coefs(data1, coef1, scaled1, diag1, 1, total - 1, 0.25, False, UNROLL1[2])
    copies = [copy_rows(coef1, coef1_out, sems.at[0], 10, total - 10)]
    copies.append(copy_rows(scaled1, scaled1_out, sems.at[1], 11, total - 11))
    sweep(scaled1, wa1, coef1, scaled1, slope1, across1, 2, total - 2, False, UNROLL1)
    copies.append(copy_rows(wa1, w1_out, sems.at[2], 9, total - 9))
    remainders(wa1, diag1, data1, diag1, coef1, slope1, across1, 3, total - 3, UNROLL1, 2)

    rows2 = rows // 2
    total2 = rows2 + 2 * RIM2

    def coefs_row(i):
        data2[i, 0, 32:56, :] = restrict_row(data1, slice(32, 56), 1 + 2 * i)

    rows_loop(0, total2, coefs_row, UNROLL_MOVE)

    def target_row(i):
        data2[i, 0, 0:32, :] = restrict_row(diag1, slice(0, 32), 1 + 2 * i)

    rows_loop(1, total2 - 1, target_row, UNROLL_MOVE)

    make_coefs(data2, coef2, scaled2, diag2, 1, total2 - 1, 0.0625, False, UNROLL2[2])
    copies.append(copy_rows(coef2, coef2_out, sems.at[3], 2, total2 - 2))
    copies.append(copy_rows(scaled2, scaled2_out, sems.at[4], 3, total2 - 3))
    sweep(scaled2, wa2, coef2, scaled2, slope2, across2, 2, total2 - 2, False, UNROLL2)
    copies.append(copy_rows(wa2, w2_out, sems.at[5], 2, total2 - 2))
    remainders(wa2, diag2, data2, diag2, coef2, slope2, across2, RIM2, RIM2 + rows2, UNROLL2, 1)

    rows3 = rows2 // 2
    width = LANES // rows3
    for first in range(0, NP, 8):
        planes = slice(first, first + 8)
        source = diag2 if first < 32 else data2
        strip = jnp.zeros((8, LANES), F32)
        for i in range(rows3):
            strip = put(strip, restrict_row(source, planes, RIM2 + 2 * i), i * width, width, i * width)
        for d in range(piece.shape[0]):
            piece[d, planes, :] = strip
    for copy in copies:
        copy.wait()


def up_kernel(place, pieces, w0_in, coef0_in, scaled0_in, w1_in, coef1_in, scaled1_in, w2_in, coef2_in, scaled2_in, result,
              data3, coef3, scaled3, wa3, wb3, slope3, across3, w2, coef2, scaled2, wa2, wb2, w1, coef1, scaled1, wa1, wb1,
              w0, coef0, scaled0, wa0, wb0, slope0, across0, result_half, sems):
    slope1, across1 = (v.at[pl.ds(0, wa1.shape[0]), pl.ds(0, 2)] for v in (slope0, across0))
    slope2, across2 = (v.at[pl.ds(0, wa2.shape[0]), pl.ds(0, 1)] for v in (slope0, across0))
    copies = []
    for source, target, first in (
        (w2_in, w2, 2), (coef2_in, coef2, 2), (scaled2_in, scaled2, 3),
        (w1_in, w1, 9), (coef1_in, coef1, 10), (scaled1_in, scaled1, 11),
        (w0_in, w0, 2), (coef0_in, coef0, 2), (scaled0_in, scaled0, 3),
    ):
        copies.append(copy_rows(source, target, sems.at[len(copies)], first, source.shape[0] - first))
    devices_y, devices_x = pieces.shape[0], pieces.shape[1]
    rows3 = devices_y
    width = LANES // devices_y
    whole = devices_x * rows3
    zero = jnp.zeros((NP, LANES), F32)
    for r in range(RIM3):
        for end in (r, RIM3 + whole + r):
            data3[end, 0] = zero
            wa3[end, 0] = zero[:32]
            wb3[end, 0] = zero[:32]
            scaled3[end, 0] = zero[:32]
            slope3[end, 0] = zero[:32]
            coef3[end, 0] = jnp.zeros((8 * NC, LANES), F32)

    def assemble(d):
        for i in range(rows3):
            line = jnp.zeros((NP, LANES), F32)
            for j in range(devices_y):
                line = put(line, pieces[j, d], (j - i) * width, width, j * width)
            data3[RIM3 + d * rows3 + i, 0] = line

    rows_loop(0, devices_x, assemble, 4)
    first, last = RIM3, RIM3 + whole
    make_coefs(data3, coef3, scaled3, None, first, last, 0.25 ** (LEVELS - 1), True, UNROLL3[2])

    gx, gy = place[0], place[1]

    def coarse_sweep(source, target, extent):
        begin, end = (first, last) if extent is None else (0, extent)
        start = 0 if extent is None else first + jnp.clip(gx * rows3 - (extent - rows3) // 2, 0, whole - extent)
        around = 0 if extent is None else 1

        def look(r):
            r = start + r
            norths, souths = shifted([source[r, 0]], True)
            slope3[r, 0] = norths[0] - souths[0]
            across3[r, 0] = twice(coef3[r, 0, 16:32, :]) * norths[0] + twice(coef3[r, 0, 32:48, :]) * souths[0]

        rows_loop(begin - around, end + around, look, UNROLL3[0] if extent is None else extent + 2)

        def row(r):
            r = start + r
            here, total = off_diagonal(source, coef3, slope3, across3, r, 0)
            target[r, 0] = (1.0 - OMEGA) * here + scaled3[r, 0] + coef3[r, 0, 88:120, :] * total

        rows_loop(begin, end, row, UNROLL3[1])

    coarse_sweep(scaled3, wa3, None)
    done = 2
    narrow = [(None, COARSE_ITERS - 9), (rows3 + 20, COARSE_ITERS - 5), (rows3 + 12, COARSE_ITERS)]
    buffers = (wa3, wb3)
    for extent, until in narrow:
        if extent is not None and extent > whole:
            extent = None

        def two_sweeps(i, carry, extent=extent, pair=buffers):
            coarse_sweep(pair[0], pair[1], extent)
            coarse_sweep(pair[1], pair[0], extent)
            return carry

        if (until - done) // 2:
            lax.fori_loop(0, (until - done) // 2, two_sweeps, 0)
        if (until - done) % 2:
            coarse_sweep(buffers[0], buffers[1], extent)
            buffers = buffers[::-1]
        done = until
    solved = buffers[0]

    lane = lane_ids(32)
    y = jnp.where(lane < 96, lane, lane - LANES)
    column = gy * width + (y + LANES) // 2 - LANES // 2
    inside = (column >= 0) & (column < LANES)
    pick = jnp.where(inside, column, 0)

    for copy in copies[:3]:
        copy.wait()
    rows2 = 2 * rows3
    for i in range(rows3 + 2 * RIM3):
        add = jnp.where(inside, gather_lanes(solved[gx * rows3 + i, 0], pick), 0.0)
        for r in (2 * i + 2, 2 * i + 3):
            wa2[r, 0] = w2[r, 0] + add
    total2 = rows2 + 2 * RIM2
    sweep(wa2, wb2, coef2, scaled2, slope2, across2, 3, total2 - 3, False, UNROLL2)
    sweep(wb2, wa2, coef2, scaled2, slope2, across2, 4, total2 - 4, False, UNROLL2)


    for copy in copies[3:6]:
        copy.wait()

    def add1(r):
        adds = prolong_row([wa2[r, 0]], 2)
        for t in range(2):
            for fine in (2 * r + 1, 2 * r + 2):
                wa1[fine, t] = w1[fine, t] + adds[t]

    rows_loop(4, total2 - 4, add1, 12)
    total1 = 2 * rows2 + 2 * RIM1
    sweep(wa1, wb1, coef1, scaled1, slope1, across1, 11, total1 - 11, False, UNROLL1_UP)
    sweep(wb1, wa1, coef1, scaled1, slope1, across1, 12, total1 - 12, False, UNROLL1_UP)


    for copy in copies[6:]:
        copy.wait()

    def add0(r):
        adds = prolong_row([wa1[r, t] for t in range(2)], 3)
        for t in range(3):
            for fine in (2 * r - 22, 2 * r - 21):
                wa0[fine, t] = w0[fine, t] + adds[t]

    rows_loop(12, total1 - 12, add0, 18)
    rows0 = 4 * rows2
    total0 = rows0 + 2 * RIM0
    sweep(wa0, wb0, coef0, scaled0, slope0, across0, 3, total0 - 3, False, UNROLL0_UP)

    result_rows = result_half.reshape(4, -1, LANES)

    def emit(r, t, value):
        for c in range(2):
            for p in range(2):
                start = 8 * c * PITCH + r - RIM0
                result_rows[2 * t + p, pl.ds(start, 8, stride=PITCH), :] = value[16 * c + 8 * p : 16 * c + 8 * p + 8]

    sweep(wb0, None, coef0, scaled0, slope0, across0, RIM0, RIM0 + rows0, False, UNROLL0_UP, tiles=2, emit=emit)
    copies = [
        pltpu.make_async_copy(
            result_half.at[2 * t + p, :, pl.ds(0, rows0)], result.at[:, p, :, pl.ds(t * LANES, LANES)], sems.at[2 * t + p]
        )
        for t in range(2)
        for p in range(2)
    ]
    for copy in copies:
        copy.start()
    for copy in copies:
        copy.wait()


def shape(*dims):
    return jax.ShapeDtypeStruct(dims, F32)


def stored(*dims):
    return pltpu.HBM(dims, F32)


def in_hbm(arrays):
    return [pltpu.with_memory_space_constraint(v, pltpu.HBM) for v in arrays]


VM = pl.BlockSpec(memory_space=pltpu.VMEM)
SM = pl.BlockSpec(memory_space=pltpu.SMEM)
HB = pl.BlockSpec(memory_space=pl.ANY)
PARAMS = pltpu.CompilerParams(vmem_limit_bytes=VMEM_DOWN)


def buffers(rows, tiles, names):
    planes = {"data": NP, "coef": 8 * NC}
    return [pltpu.VMEM((rows, tiles, planes.get(name, 32), LANES), F32) for name in names]


def per_device(misfit, viscosity, friction, ice_mask, grounded):
    rows, columns = friction.shape
    gx, gy = lax.axis_index("gx"), lax.axis_index("gy")
    nx, ny = lax.axis_size("gx"), lax.axis_size("gy")
    upward = [(i, i + 1) for i in range(nx - 1)]
    downward = [(i + 1, i) for i in range(nx - 1)]

    def beside(strips):
        every = lax.all_gather(strips, "gy", axis=0)
        left = lax.dynamic_index_in_dim(every, jnp.maximum(gy - 1, 0), 0, keepdims=False)[1]
        right = lax.dynamic_index_in_dim(every, jnp.minimum(gy + 1, ny - 1), 0, keepdims=False)[0]
        return jnp.where(gy > 0, left, 0.0), jnp.where(gy < ny - 1, right, 0.0)

    data0, strips0, edges0 = pl.pallas_call(
        arrange_kernel,
        out_shape=(shape(rows, 2, NP, LANES), shape(2, NP + 16, LANES), shape(2, 16, LANES)),
        in_specs=[HB] * 5,
        out_specs=(VM, VM, VM),
        scratch_shapes=[
            pltpu.VMEM((4, 16, PITCH, LANES), F32),
            pltpu.VMEM((4, 8, PITCH, LANES), F32),
            pltpu.VMEM((rows, columns), F32),
            pltpu.VMEM((rows, columns), jnp.int32),
            pltpu.VMEM((rows, columns), jnp.int32),
            pltpu.SemaphoreType.DMA((11,)),
        ],
        compiler_params=PARAMS,
        name="arrange",
    )(
        *in_hbm(
            [v.reshape(-1, 2, rows, columns) for v in (misfit, viscosity)] + [friction, ice_mask, grounded]
        )
    )
    left, right = beside(strips0)
    inner = RIM0 - 1

    def face0(which, first, first_inner):
        corner = slice(NP + 8 * which, NP + 8 * which + 8)
        parts = (
            data0[first_inner : first_inner + inner, :, 0:32],
            data0[first : first + RIM0, :, 32:48],
            edges0[which],
            left[corner],
            right[corner],
        )
        return jnp.concatenate([v.reshape(-1, LANES) for v in parts], 0)

    low_face = face0(0, 0, 0)
    high_face = face0(1, rows - RIM0, rows - inner)
    from_low = lax.ppermute(high_face, "gx", upward)
    from_high = lax.ppermute(low_face, "gx", downward)

    total0 = rows + 2 * RIM0
    names = ("data", "diag", "slope", "across", "w", "coef", "scaled")
    rows1 = rows // 2
    group = LANES // STRIP1
    field0 = stored(total0, 3, 32, LANES)
    up0 = (field0, stored(total0, 3, 8 * NC, LANES), field0)
    inner1 = RIM1 - 1
    inner_coarse, *ups0 = pl.pallas_call(
        inner0_kernel,
        out_shape=(shape(rows1, NP, LANES),) + up0,
        in_specs=[VM] * 3,
        out_specs=(VM, HB, HB, HB),
        scratch_shapes=buffers(total0, 3, names) + [pltpu.SemaphoreType.DMA((4,))],
        compiler_params=PARAMS,
        cost_estimate=pl.CostEstimate(flops=40_000_000, bytes_accessed=20_000_000, transcendentals=0),
        name="inner0",
    )(data0, left, right)
    data1, strips1, edges1, w0, coef0, scaled0 = pl.pallas_call(
        outer0_kernel,
        out_shape=(
            shape(rows1, NP, LANES),
            shape(2, rows1 // group, NP, LANES),
            shape(2, 2 * inner1, LANES),
        )
        + up0,
        in_specs=[VM] * 6 + [HB] * 3,
        out_specs=(VM, VM, VM, HB, HB, HB),
        input_output_aliases={6: 3, 7: 4, 8: 5},
        scratch_shapes=buffers(2 * SPAN, 3, names) + [pltpu.SemaphoreType.DMA((6,))],
        compiler_params=PARAMS,
        name="outer0",
    )(data0, left, right, from_low, from_high, inner_coarse, *in_hbm(ups0))

    def face1(which, first, first_inner):
        parts = (data1[first_inner : first_inner + inner1, 0:32], data1[first : first + RIM1, 32:48], edges1[which])
        return jnp.concatenate([v.reshape(-1, LANES) for v in parts], 0)

    from_low = lax.ppermute(face1(1, rows1 - RIM1, rows1 - inner1), "gx", upward)
    from_high = lax.ppermute(face1(0, 0, 0), "gx", downward)
    slots = lax.broadcasted_iota(jnp.int32, (ny, 1, 1, 1), 0)
    sent = jnp.where(slots == gy - 1, strips1[:1], jnp.where(slots == gy + 1, strips1[1:], 0.0).reshape((ny,) + strips1.shape[1:]))
    got = lax.all_to_all(sent, "gy", 0, 0)
    left = jnp.where(gy > 0, lax.dynamic_index_in_dim(got, jnp.maximum(gy - 1, 0), 0, keepdims=False), 0.0).reshape(-1, LANES)
    right = jnp.where(gy < ny - 1, lax.dynamic_index_in_dim(got, jnp.minimum(gy + 1, ny - 1), 0, keepdims=False), 0.0).reshape(-1, LANES)
    sides = jnp.concatenate([left, right], 0)
    sides_low = lax.ppermute(sides, "gx", upward)
    sides_high = lax.ppermute(sides, "gx", downward)

    total1 = rows1 + 2 * RIM1
    rows2 = rows1 // 2
    total2 = rows2 + 2 * RIM2
    field1 = stored(total1, 2, 32, LANES)
    field2 = stored(total2, 1, 32, LANES)
    piece, w1, coef1, scaled1, w2, coef2, scaled2 = pl.pallas_call(
        down12_kernel,
        out_shape=(
            shape(nx, NP, LANES),
            field1,
            stored(total1, 2, 8 * NC, LANES),
            field1,
            field2,
            stored(total2, 1, 8 * NC, LANES),
            field2,
        ),
        in_specs=[VM] * 6,
        out_specs=(VM,) + (HB,) * 6,
        scratch_shapes=buffers(total1, 2, names) + buffers(total2, 1, names) + [pltpu.SemaphoreType.DMA((6,))],
        compiler_params=PARAMS,
        name="down12",
    )(data1, sides, from_low, from_high, sides_low, sides_high)

    pieces = lax.all_gather(lax.all_to_all(piece, "gx", 0, 0), "gy", axis=0)

    rows3 = rows2 // 2
    total3 = nx * rows3 + 2 * RIM3
    ups = ("w", "coef", "scaled", "w", "w")
    result = pl.pallas_call(
        up_kernel,
        out_shape=shape(16, 2, rows, columns),
        in_specs=[SM, VM] + [HB] * 9,
        out_specs=HB,
        scratch_shapes=buffers(total3, 1, ("data", "coef", "scaled", "w", "w", "slope", "across"))
        + buffers(total2, 1, ups)
        + buffers(total1, 2, ups)
        + buffers(total0, 3, ups)
        + buffers(max(total0, total1), 3, ("slope", "across"))
        + [pltpu.VMEM((4, 16, PITCH, LANES), F32), pltpu.SemaphoreType.DMA((9,))],
        compiler_params=pltpu.CompilerParams(vmem_limit_bytes=VMEM_UP),
        name="up",
    )(
        jnp.stack([gx, gy]).astype(jnp.int32),
        pieces,
        *in_hbm([w0, coef0, scaled0, w1, coef1, scaled1, w2, coef2, scaled2]),
    )
    return result.reshape(misfit.shape)


def solution(mesh):
    placed = (
        P(None, None, "gx", "gy"),
        P(None, "gx", "gy"),
        P("gx", "gy"),
        P("gx", "gy"),
        P("gx", "gy"),
    )
    return jax.shard_map(
        per_device, mesh=mesh, in_specs=placed, out_specs=P(None, None, "gx", "gy"), check_vma=False
    )
```
